32 devices in a mesh: face: 4 (over y, x), lon: 8 (over z, core).
Axes of the slice: x: 2, y: 2, z: 4, core: 2. Of those that a mesh axis runs over, the one named last changes fastest.
Arguments:
- source: bfloat16 [1024, 8, 128], P(('face', 'lon')), may hold values from -6 to 6
- intersection_weight: bfloat16 [1024, 4, 128, 128], P(('face', 'lon')), may hold values from -0.5 to 0.5
- dest_tile: int32 [1024, 4], P(('face', 'lon')), may hold values from 0 to 31, all different within a row; in each aligned block of 32 rows (0 to 31, 32 to 63, ...) at most 8 rows name the same one
- dest_row: int32 [1024, 4], P(('face', 'lon')), may hold values from 0 to 63
- prior_state: bfloat16 [8, 128, 2048], P(None, 'face', 'lon'), may hold values from -6 to 6
- lift_weight: bfloat16 [8, 64], replicated, may hold values from -9 to 9
- kernel: bfloat16 [9, 64, 64], replicated, may hold values from -0.23570226 to 0.23570226
- readout_weights: bfloat16 [64, 8], replicated, may hold values from -0.75 to 0.75
Outputs:
- remapped_reference: bfloat16 [8, 128, 2048], P(None, 'face', 'lon')
- network_estimate: bfloat16 [8, 128, 2048], P(None, 'face', 'lon')
- grad_lift: float32 [8, 64], replicated
- grad_kernel: float32 [9, 64, 64], replicated
- grad_head: float32 [64, 8], replicated
The draws below stay inside these ranges and needn't reach their ends.
Inputs may be any that keep to these rules, and one draw needn't show every extreme that they name: `dest_tile`: the 4 intersections of a source block name distinct devices; the source blocks of one device name one device at most 8 times, and exactly 8 times for some device.
All inputs are finite; a program needn't handle non-finite values.
Results may differ from the reference program's by a relative error of at most 0.0013.
The reference program's roundings to bfloat16 on the way count: a program that leaves them out, or rounds other values in their place, can miss the bound.
Values may be sent and summed in bfloat16 or wider, within the bound.
No kernel may reach another device: no remote copies, remote signals or barrier semaphores. Data moves between devices by JAX's collectives and lax.ppermute only.
A program may use at most 128 MiB of HBM per device.

```python
import math
import jax
import jax.numpy as jnp
import numpy as np
from jax import lax

QUANTITY_TOTAL = 8
WIDTH = 64
BLOCK = 128
K = 4
TAPS = 9
S_DEV = 32
ZONE_PARALLELS = 32
W_DEV = 256
TB = 64
CAP = 8
SRC = 1024
NLAT = 128
MERIDIAN_TOTAL = 2048
N_FACE = 4
N_LON = 8
DEVICES = 32


def draw_lift_weight(key, part):
    first_key = jax.random.fold_in(key, 11)
    second_key = jax.random.fold_in(key, 12)
    spread = QUANTITY_TOTAL ** (-0.5)
    private = jnp.clip(jax.random.normal(first_key, (QUANTITY_TOTAL, WIDTH), jnp.float32) * spread, -4.0 * spread, 4.0 * spread)
    shared = jax.random.uniform(second_key, (QUANTITY_TOTAL, 1), jnp.float32, 4.0, 7.0)
    signs = jnp.where(jnp.arange(QUANTITY_TOTAL) % 2 == 0, 1.0, -1.0).astype(jnp.float32)[:, None]
    return (private + shared * signs).astype(jnp.bfloat16)


def draw_kernel(key, part):
    base_key = jax.random.fold_in(key, 21)
    spread = (2.0 * TAPS * WIDTH) ** (-0.5)
    base = jnp.clip(jax.random.normal(base_key, (TAPS, WIDTH, WIDTH), jnp.float32) * spread, -4.0 * spread, 4.0 * spread)
    return (base - jnp.roll(base, 1, axis=1)).astype(jnp.bfloat16)


def with_ends(result, key, low, high):
    shape = result.shape
    spot = [jax.random.randint(jax.random.fold_in(key, axis), (), 0, shape[axis]) for axis in range(len(shape))]
    result = result.at[tuple(spot)].set(low)
    longest = shape.index(max(shape))
    spot[longest] = (spot[longest] + 1) % shape[longest]
    return result.at[tuple(spot)].set(high)


def levels(stream_key, shape, shards, smallest, largest):
    factor_of = 1.0
    for axis_at, blocks in shards:
        steps = jax.random.uniform(jax.random.fold_in(jax.random.fold_in(stream_key, 6), axis_at), (blocks,), jnp.float32, smallest / len(shards), largest / len(shards))
        factor_of = factor_of * jnp.repeat(jnp.exp(steps), shape[axis_at] // blocks).reshape((-1,) + (1,) * (len(shape) - 1 - axis_at))
    return factor_of


def routed_block(rng, own, number, rows, count, top, bound, skew):
    ranking = jax.random.permutation(rng, count)
    packed, usual = portions_of(count, rows * top, bound, skew, True), portions_of(count, rows * top, bound, skew, False)
    places = jnp.arange(count)

    def named(lengths, rotation):
        used = int((lengths > 0).sum())
        fixed = max(1, used // 4)
        shifted = fixed + (places - fixed + rotation * (used - fixed)) % max(1, count - fixed)
        return jnp.zeros((count,), jnp.int32).at[ranking[jnp.where(places < fixed, places, shifted)]].set(jnp.asarray(lengths, jnp.int32))

    lengths = jnp.where(number % 4 == 0, named(packed, number // 4), named(usual, number - number // 4 - 1))
    mixed = jax.random.permutation(jax.random.fold_in(own, 3), count)
    giver, receiver = mixed[0:count // 2 * 2:2], mixed[1:count // 2 * 2:2]
    room = jnp.minimum(lengths[giver] - 1, bound - lengths[receiver]) // 2
    room = jnp.where((giver == ranking[0]) | (receiver == ranking[0]) | (lengths[receiver] == 0), 0, jnp.maximum(room, 0))
    shifted = jax.random.randint(jax.random.fold_in(own, 4), (count // 2,), 0, 1 << 20) % (room + 1)
    lengths = lengths.at[giver].add(-shifted).at[receiver].add(shifted)
    items = jnp.searchsorted(jnp.cumsum(lengths), jnp.arange(rows * top), side="right").astype(jnp.int32)
    listing = items.reshape(top, rows).T
    listing = listing[jax.random.permutation(jax.random.fold_in(own, 1), rows)]
    rotation = jax.random.randint(jax.random.fold_in(own, 2), (rows, 1), 0, top)
    return jnp.take_along_axis(listing, (jnp.arange(top)[None, :] + rotation) % top, axis=1)


def portions_of(amount, total, reach, skew, full):
    weights = [(1 << 20) // math.isqrt(rank ** skew) + 1 for rank in range(1, amount + 1)]
    largest = reach if full else min(reach, max(-(-total // amount), total * weights[0] // sum(weights)))
    least = 1 if total - largest >= amount - 1 else 0
    given, rest = [largest] + [least] * (amount - 1), total - largest - least * (amount - 1)
    while rest > 0:
        candidates = [i for i in range(1, amount) if given[i] < largest] or [i for i in range(1, amount) if given[i] < reach]
        whole, budget = sum([weights[i] for i in candidates]), rest
        for i in candidates:
            more = min(reach - given[i], max(1, budget * weights[i] // whole), rest)
            given[i] = given[i] + more
            rest = rest - more
    return np.array(given)


def normal_values(own_key, dims, scale, limit, split=(), held_as=jnp.bfloat16):
    result = scale * jax.random.normal(own_key, dims, jnp.float32)
    if split:
        result = result * levels(own_key, dims, split, -0.22, 0.18)
    return jnp.clip(result, -limit, limit).astype(held_as)


def setup_inputs(seed: int = 0) -> dict:
    streams_of = jax.random.split(jax.random.key(seed), 9)
    source = normal_values(streams_of[0], (SRC, QUANTITY_TOTAL, BLOCK), 1.0, 6.0, ((0, 32),))
    intersection_weight = normal_values(streams_of[1], (SRC, K, BLOCK, BLOCK), BLOCK ** -0.5, 0.5, ((0, 32),))
    dest_tile_keys = jax.random.split(jax.random.fold_in(streams_of[2], 1), SRC // S_DEV)
    dest_tile_turns = jax.random.permutation(jax.random.fold_in(streams_of[2], 3), SRC // S_DEV)
    dest_tile = jax.vmap(lambda own, number: routed_block(jax.random.fold_in(streams_of[2], 2), own, number, S_DEV, DEVICES, K, CAP, 2))(dest_tile_keys, dest_tile_turns).reshape((SRC, K))
    dest_row = with_ends(jax.random.randint(streams_of[3], (SRC, K), 0, TB), jax.random.fold_in(streams_of[3], 1), 0, TB - 1).astype(jnp.int32)
    prior_state = normal_values(streams_of[4], (QUANTITY_TOTAL, NLAT, MERIDIAN_TOTAL), 1.0, 6.0, ((1, 4), (2, 8)))
    lift_weight = draw_lift_weight(jax.random.fold_in(streams_of[8], 71), 0)
    kernel = draw_kernel(jax.random.fold_in(streams_of[8], 71), 0)
    readout_weights = normal_values(streams_of[7], (WIDTH, QUANTITY_TOTAL), WIDTH ** -0.5, 0.75)
    return {"source": source, "intersection_weight": intersection_weight, "dest_tile": dest_tile, "dest_row": dest_row, "prior_state": prior_state, "lift_weight": lift_weight, "kernel": kernel, "readout_weights": readout_weights}


def wrap_lon(field):
    return jnp.concatenate([field[:, :, -1:], field, field[:, :, :1]], 2)

def conv_taps(kernel, padded, out_rows, out_cols):
    running = jnp.zeros((kernel.shape[2], out_rows * out_cols), jnp.float32)
    for tap_index in range(9):
        row_shift, col_shift = divmod(tap_index, 3)
        window_piece = padded[:, row_shift:row_shift + out_rows, col_shift:col_shift + out_cols].reshape(padded.shape[0], -1)
        running = running + jnp.dot(kernel[tap_index].T, window_piece, preferred_element_type=jnp.float32)
    return running

def back_taps(kernel, padded, out_rows, out_cols):
    running = jnp.zeros((kernel.shape[1], out_rows * out_cols), jnp.float32)
    for tap_index in range(9):
        row_shift, col_shift = divmod(tap_index, 3)
        window_piece = padded[:, 2 - row_shift:2 - row_shift + out_rows, 2 - col_shift:2 - col_shift + out_cols].reshape(padded.shape[0], -1)
        running = running + jnp.dot(kernel[tap_index], window_piece, preferred_element_type=jnp.float32)
    return running

def kernel_taps(padded, slope, out_rows, out_cols):
    grads = []
    for tap_index in range(9):
        row_shift, col_shift = divmod(tap_index, 3)
        window_piece = padded[:, row_shift:row_shift + out_rows, col_shift:col_shift + out_cols].reshape(padded.shape[0], -1)
        grads.append(lax.dot_general(window_piece, slope, (((1,), (1,)), ((), ())), preferred_element_type=jnp.float32))
    return jnp.stack(grads)

def contribute(pair):
    src_block, weight_block = pair
    return jnp.einsum('sfi,skij->skfj', src_block.astype(jnp.float32), weight_block.astype(jnp.float32)).astype(jnp.bfloat16)

def reference(source, intersection_weight, dest_tile, dest_row, prior_state, lift_weight, kernel, readout_weights):
    src_dev = source.reshape(DEVICES, S_DEV, QUANTITY_TOTAL, BLOCK)
    wts_dev = intersection_weight.reshape(DEVICES, S_DEV, K, BLOCK, BLOCK)
    contrib = lax.map(contribute, (src_dev, wts_dev))
    labels = (dest_tile * TB + dest_row).reshape(-1).astype(jnp.int32)
    blocks = jax.ops.segment_sum(contrib.reshape(-1, QUANTITY_TOTAL * BLOCK).astype(jnp.float32), labels, num_segments=DEVICES * TB)
    blocks = blocks.astype(jnp.bfloat16)
    remapped_reference = blocks.reshape(N_FACE, N_LON, ZONE_PARALLELS, W_DEV // BLOCK, QUANTITY_TOTAL, BLOCK)
    remapped_reference = remapped_reference.transpose(4, 0, 2, 1, 3, 5).reshape(QUANTITY_TOTAL, NLAT, MERIDIAN_TOTAL)
    objective_normalizer = 1.0 / math.sqrt(NLAT * MERIDIAN_TOTAL)
    state_pad = jnp.pad(prior_state, ((0, 0), (2, 2), (0, 0)))
    target_pad = jnp.pad(remapped_reference, ((0, 0), (2, 2), (0, 0)))
    valid_pad = jnp.pad(jnp.ones((NLAT,), jnp.float32), 2)

    def band_terms(band_index):
        band_start = (band_index * ZONE_PARALLELS).astype(jnp.int32)
        window = lax.dynamic_slice_in_dim(state_pad, band_start, ZONE_PARALLELS + 4, 1)
        valid_rows = lax.dynamic_slice_in_dim(valid_pad, band_start, ZONE_PARALLELS + 4, 0)
        reference_parallel_entries = lax.dynamic_slice_in_dim(target_pad, band_start + 1, ZONE_PARALLELS + 2, 1)
        lifted_wide = jnp.dot(lift_weight.T, window.reshape(QUANTITY_TOTAL, -1), preferred_element_type=jnp.float32)
        lifted_wide = lifted_wide.reshape(WIDTH, ZONE_PARALLELS + 4, MERIDIAN_TOTAL) * valid_rows[None, :, None]
        lifted = lifted_wide.astype(jnp.bfloat16)
        padded = wrap_lon(lifted)
        act = conv_taps(kernel, padded, ZONE_PARALLELS + 2, MERIDIAN_TOTAL)
        latent_activations = jax.nn.silu(act).astype(jnp.bfloat16)
        starting_condition = window[:, 1:ZONE_PARALLELS + 3].reshape(QUANTITY_TOTAL, -1).astype(jnp.float32)
        predicted_fields = starting_condition + jnp.dot(readout_weights.T, latent_activations, preferred_element_type=jnp.float32)
        predicted_fields = predicted_fields.reshape(QUANTITY_TOTAL, ZONE_PARALLELS + 2, MERIDIAN_TOTAL)
        parallel_cosine_factor = (objective_normalizer * valid_rows[1:ZONE_PARALLELS + 3])[None, :, None]
        prediction_mismatch = ((predicted_fields - reference_parallel_entries.astype(jnp.float32)) * parallel_cosine_factor).astype(jnp.bfloat16)
        latent_gradient = jnp.dot(readout_weights, prediction_mismatch.reshape(QUANTITY_TOTAL, -1), preferred_element_type=jnp.float32)
        sigmoid_act = jax.nn.sigmoid(act)
        slope = (latent_gradient * sigmoid_act * (1.0 + act * (1.0 - sigmoid_act))).astype(jnp.bfloat16)
        slope = slope.reshape(WIDTH, ZONE_PARALLELS + 2, MERIDIAN_TOTAL)
        hidden_band = latent_activations.reshape(WIDTH, ZONE_PARALLELS + 2, MERIDIAN_TOTAL)[:, 1:ZONE_PARALLELS + 1].reshape(WIDTH, -1)
        zone_residual = prediction_mismatch[:, 1:ZONE_PARALLELS + 1].reshape(QUANTITY_TOTAL, -1)
        slope_band = slope[:, 1:ZONE_PARALLELS + 1].reshape(WIDTH, -1)
        readout_term = lax.dot_general(hidden_band, zone_residual, (((1,), (1,)), ((), ())), preferred_element_type=jnp.float32)
        stencil_term = kernel_taps(padded[:, 1:], slope_band, ZONE_PARALLELS, MERIDIAN_TOTAL)
        lifted_grad = back_taps(kernel, wrap_lon(slope), ZONE_PARALLELS, MERIDIAN_TOTAL).astype(jnp.bfloat16)
        state_band = window[:, 2:ZONE_PARALLELS + 2].reshape(QUANTITY_TOTAL, -1)
        embedding_term = lax.dot_general(state_band, lifted_grad, (((1,), (1,)), ((), ())), preferred_element_type=jnp.float32)
        zone_prediction_slice = predicted_fields[:, 1:ZONE_PARALLELS + 1].astype(jnp.bfloat16)
        return (zone_prediction_slice, embedding_term, stencil_term, readout_term)
    bands, lift_terms, kernel_terms, head_terms = lax.map(band_terms, jnp.arange(N_FACE, dtype=jnp.int32))
    network_estimate = bands.transpose(1, 0, 2, 3).reshape(QUANTITY_TOTAL, NLAT, MERIDIAN_TOTAL)
    grad_lift = lax.optimization_barrier(jnp.sum(lift_terms, axis=0))
    grad_kernel = lax.optimization_barrier(jnp.sum(kernel_terms, axis=0))
    grad_head = lax.optimization_barrier(jnp.sum(head_terms, axis=0))
    return (remapped_reference, network_estimate, grad_lift, grad_kernel, grad_head)
```

```python
import functools
import math

import jax
import jax.numpy as jnp
from jax import lax
from jax.experimental import pallas as pl
from jax.experimental.pallas import tpu as pltpu
from jax.sharding import PartitionSpec as P

NT = (((1,), (1,)), ((), ()))
VMEM_LIMIT = 40 * 1024 * 1024


def dot(a, b):
    return jnp.dot(a, b, preferred_element_type=jnp.float32)


def dot_nt(a, b):
    return lax.dot_general(a, b, NT, preferred_element_type=jnp.float32)


def regrid_kernel(capacity, tile_ref, row_ref, src_ref, wts_ref, out_ref, count_ref, head_ref):
    step = pl.program_id(0)
    chunk, fields, width = src_ref.shape
    intersections = wts_ref.shape[1]
    devices = out_ref.shape[0]

    @pl.when(step == 0)
    def _():
        out_ref[...] = jnp.zeros_like(out_ref)
        head_ref[...] = jnp.full_like(head_ref, -1.0)

        def clear(d, carry):
            count_ref[d] = 0
            return carry

        lax.fori_loop(0, devices, clear, 0)

    slot_of_lane = lax.rem(lax.broadcasted_iota(jnp.int32, (1, width), 1) // fields, capacity)
    for s in range(chunk):
        block = src_ref[s]
        for pair in range(0, intersections, 2):
            both = jnp.concatenate([wts_ref[s, k] for k in range(pair, min(pair + 2, intersections))], axis=1)
            contrib = dot(block, both).astype(jnp.bfloat16)
            for k in range(pair, min(pair + 2, intersections)):
                tile = tile_ref[step * chunk + s, k]
                slot = count_ref[tile]
                count_ref[tile] = slot + 1
                out_ref[tile, slot] = contrib[:, (k - pair) * width : (k - pair + 1) * width]
                label = row_ref[step * chunk + s, k].astype(jnp.float32)
                head_ref[pl.ds(tile, 1), :] = jnp.where(
                    slot_of_lane == slot, label, head_ref[pl.ds(tile, 1), :]
                )

    @pl.when(step == pl.num_programs(0) - 1)
    def _():
        for d in range(devices):
            out_ref[d, capacity] = jnp.broadcast_to(
                head_ref[d : d + 1, :], (fields, width)
            ).astype(jnp.bfloat16)


def regrid(source, weights, dest_tile, dest_row, devices, capacity):
    blocks, fields, width = source.shape
    intersections = weights.shape[1]
    chunk = math.gcd(blocks, 8)
    return pl.pallas_call(
        functools.partial(regrid_kernel, capacity),
        grid=(blocks // chunk,),
        out_shape=jax.ShapeDtypeStruct((devices, capacity + 1, fields, width), jnp.bfloat16),
        in_specs=[
            pl.BlockSpec(memory_space=pltpu.SMEM),
            pl.BlockSpec(memory_space=pltpu.SMEM),
            pl.BlockSpec((chunk, fields, width), lambda i: (i, 0, 0)),
            pl.BlockSpec((chunk, intersections, width, width), lambda i: (i, 0, 0, 0)),
        ],
        out_specs=pl.BlockSpec((devices, capacity + 1, fields, width), lambda i: (0, 0, 0, 0)),
        scratch_shapes=[
            pltpu.SMEM((devices,), jnp.int32),
            pltpu.VMEM((devices, width), jnp.float32),
        ],
        compiler_params=pltpu.CompilerParams(vmem_limit_bytes=VMEM_LIMIT),
        cost_estimate=pl.CostEstimate(
            flops=2 * weights.size * fields, bytes_accessed=2 * weights.size, transcendentals=0
        ),
        name="regrid",
    )(dest_tile, dest_row, source, weights)


def forward_kernel(
    channels,
    prior_ref,
    edge_ref,
    side_ref,
    lift_ref,
    conv_ref,
    readout_ref,
    feat_ref,
    stack_ref,
    hidden_ref,
    deriv_ref,
    forecast_ref,
    estimate_ref,
    halo_ref,
):
    rows, fields, width = prior_ref.shape
    pitch = lift_ref.shape[0]
    lift = lift_ref[...]

    def lift_row(values, at):
        feat_ref[pl.ds(pl.multiple_of(at * pitch, 16), pitch), :] = dot(lift, values).astype(jnp.bfloat16)

    lift_row(edge_ref[0], 0)
    lift_row(edge_ref[1], rows + 1)

    def lift_rows(y, carry):
        lift_row(prior_ref[y], y + 1)
        return carry

    lax.fori_loop(0, rows, lift_rows, 0, unroll=4)

    side = dot(lift, side_ref[...])
    shifted = [side] + [pltpu.roll(side, 256 - i, 1) for i in (1, 2)]
    stack = jnp.concatenate(shifted, axis=0).astype(jnp.bfloat16)
    stack_ref[...] = stack
    halo_ref[:, :128] = dot(conv_ref[:channels, :], stack[:, :128])
    halo_ref[:, 128:] = dot(conv_ref[2 * channels :, :], stack[:, 128:])
    lane = lax.broadcasted_iota(jnp.int32, (channels, width), 1)

    def one_row(y):
        window = feat_ref[pl.ds(pl.multiple_of(y * pitch, 16), 3 * pitch), :]
        parts = dot(conv_ref[...], window)
        left = pltpu.roll(parts[:channels], 1, 1)
        right = pltpu.roll(parts[2 * channels :], width - 1, 1)
        from_left = pltpu.roll(halo_ref[:, :128], lax.rem(128 - y, 128), 1)
        from_right = pltpu.roll(halo_ref[:, 128:], 127 - y, 1)
        spread = [jnp.zeros_like(from_left)] * (width // 128 - 1)
        left = jnp.where(lane == 0, jnp.concatenate([from_left] + spread, axis=1), left)
        right = jnp.where(lane == width - 1, jnp.concatenate(spread + [from_right], axis=1), right)
        act = parts[channels : 2 * channels] + left + right
        sig = 1.0 / (1.0 + jnp.exp(-act))
        hidden = (act * sig).astype(jnp.bfloat16)
        at = pl.ds(pl.multiple_of(y * channels, 16), channels)
        hidden_ref[at, :] = hidden
        deriv_ref[at, :] = sig * (1.0 + act * (1.0 - sig))
        forecast = prior_ref[y].astype(jnp.float32) + dot(readout_ref[...], hidden)
        forecast_ref[y] = forecast
        estimate_ref[y] = forecast.astype(jnp.bfloat16)

    def some_rows(step, carry):
        for r in range(4):
            one_row(step * 4 + r)
        return carry

    lax.fori_loop(0, rows // 4, some_rows, 0)


def forward(prior, edges, sides, lift, conv, readout, channels):
    rows, fields, width = prior.shape
    pitch = lift.shape[0]
    return pl.pallas_call(
        functools.partial(forward_kernel, channels),
        out_shape=(
            jax.ShapeDtypeStruct(((rows + 2) * pitch, width), jnp.bfloat16),
            jax.ShapeDtypeStruct((3 * pitch, 256), jnp.bfloat16),
            jax.ShapeDtypeStruct((rows * channels, width), jnp.bfloat16),
            jax.ShapeDtypeStruct((rows * channels, width), jnp.float32),
            jax.ShapeDtypeStruct((rows, fields, width), jnp.float32),
            jax.ShapeDtypeStruct((rows, fields, width), jnp.bfloat16),
        ),
        scratch_shapes=[pltpu.VMEM((channels, 256), jnp.float32)],
        compiler_params=pltpu.CompilerParams(vmem_limit_bytes=VMEM_LIMIT),
        cost_estimate=pl.CostEstimate(
            flops=2 * rows * width * 3 * channels * 3 * pitch,
            bytes_accessed=rows * width * channels * 8,
            transcendentals=rows * width * channels * 2,
        ),
        name="forward",
    )(prior, edges, sides, lift, conv, readout)


def backward_kernel(
    capacity,
    channels,
    norm,
    side_bit,
    arrived_hbm,
    feat_hbm,
    hidden_hbm,
    deriv_hbm,
    forecast_hbm,
    stack_ref,
    readout_ref,
    back_ref,
    contract_ref,
    remapped_ref,
    packed_ref,
    arrived_ref,
    feat_ref,
    hidden_ref,
    deriv_ref,
    forecast_ref,
    picked_ref,
    slope_ref,
    total_ref,
    edge_ref,
    small_ref,
    sems,
):
    pairs = (
        (arrived_hbm, arrived_ref),
        (forecast_hbm, forecast_ref),
        (deriv_hbm, deriv_ref),
        (hidden_hbm, hidden_ref),
        (feat_hbm, feat_ref),
    )
    copies = [pltpu.make_async_copy(a, b, sems.at[i]) for i, (a, b) in enumerate(pairs)]
    for copy in copies:
        copy.start()
    rows, fields, width = remapped_ref.shape
    pitch = feat_ref.shape[0] // (rows + 2)
    devices = arrived_ref.shape[0]
    per_row = width // 128
    blocks = rows * per_row
    group = 128 // (fields * capacity)

    total_ref[...] = jnp.zeros_like(total_ref)
    edge_ref[...] = jnp.zeros_like(edge_ref)
    small_ref[...] = jnp.zeros_like(small_ref)
    slope_ref[:channels, :] = jnp.zeros((channels, width), jnp.bfloat16)
    slope_ref[(rows + 1) * channels :, :] = jnp.zeros((channels, width), jnp.bfloat16)
    lane = lax.broadcasted_iota(jnp.int32, (fields, 128), 1)
    sublane = lax.broadcasted_iota(jnp.int32, (fields, 128), 0)
    wanted = lax.broadcasted_iota(jnp.int32, (blocks, fields, 256), 0) * fields

    copies[0].wait()
    picked = None
    for first in range(0, devices, 2 * group):
        labels, data = [], []
        for half in range(2):
            label = None
            for d in range(group):
                device = first + half * group + d
                mine = arrived_ref[device, capacity * fields : (capacity + 1) * fields, :].astype(jnp.float32)
                label = mine if label is None else jnp.where(lane // (fields * capacity) == d, mine, label)
                data.append(arrived_ref[device, : capacity * fields, :])
            labels.append(label.astype(jnp.int32) * fields + lane % fields - sublane)
        hits = jnp.concatenate(labels, axis=1)[None] == wanted
        hits = jnp.where(hits, 1.0, 0.0).reshape(blocks * fields, 256).astype(jnp.bfloat16)
        part = dot(hits, jnp.concatenate(data, axis=0))
        picked = part if picked is None else picked + part
    picked_ref[...] = picked.astype(jnp.bfloat16).astype(jnp.float32).reshape(blocks, fields, 128)

    for copy in copies[1:]:
        copy.wait()
    col = lax.broadcasted_iota(jnp.int32, (channels, width), 1)
    lane = lax.broadcasted_iota(jnp.int32, (channels, 128), 1)
    batch = 4

    def slopes(step, carry):
        features, trios, hiddens, misfits = [], [], [], []
        ends_left, ends_right = edge_ref[:, :128], edge_ref[:, 128:]
        for r in range(batch):
            y = step * batch + r
            target = jnp.concatenate([picked_ref[y * per_row + b] for b in range(per_row)], axis=1)
            remapped_ref[y] = target.astype(jnp.bfloat16)
            misfit = ((forecast_ref[y] - target) * norm).astype(jnp.bfloat16)
            here = pl.ds(pl.multiple_of(y * channels, 16), channels)
            slope = dot(readout_ref[...], misfit) * deriv_ref[here, :]
            slope_ref[pl.ds(pl.multiple_of((y + 1) * channels, 16), channels), :] = slope.astype(jnp.bfloat16)
            before = jnp.where(col == width - 1, 0.0, pltpu.roll(slope, width - 1, 1))
            after = jnp.where(col == 0, 0.0, pltpu.roll(slope, 1, 1))
            trios.append(jnp.concatenate([before, slope, after], axis=0).astype(jnp.bfloat16))
            features.append(feat_ref[pl.ds(pl.multiple_of(y * pitch, 16), 3 * pitch), :])
            hiddens.append(hidden_ref[here, :])
            misfits.append(misfit)
            ends_left += pltpu.roll(jnp.where(lane == 0, slope[:, :128], 0.0), y, 1)
            ends_right += pltpu.roll(jnp.where(lane == 127, slope[:, -128:], 0.0), y + 1, 1)
        edge_ref[:, :128], edge_ref[:, 128:] = ends_left, ends_right
        total_ref[...] += dot_nt(jnp.concatenate(features, axis=1), jnp.concatenate(trios, axis=1))
        small_ref[0] += dot_nt(jnp.concatenate(misfits, axis=1), jnp.concatenate(hiddens, axis=1))
        return carry

    lax.fori_loop(0, rows // batch, slopes, 0)

    def roundings(step, carry):
        deltas, states = [], []
        for r in range(batch):
            y = step * batch + r
            window = slope_ref[pl.ds(pl.multiple_of(y * channels, 16), 3 * channels), :]
            parts = dot(back_ref[...], window)
            grad = (
                parts[channels : 2 * channels]
                + pltpu.roll(parts[:channels], width - 1, 1)
                + pltpu.roll(parts[2 * channels :], 1, 1)
            )
            inside = (col > 0) & (col < width - 1) & (y > 0) & (y < rows - 1)
            delta = jnp.where(inside, grad.astype(jnp.bfloat16).astype(jnp.float32) - grad, 0.0)
            deltas.append(delta.astype(jnp.bfloat16))
            states.append(
                feat_ref[pl.ds(pl.multiple_of((y + 1) * pitch + channels, 16), pitch - channels), :]
            )
        part = dot_nt(jnp.concatenate(states, axis=1), jnp.concatenate(deltas, axis=1))
        small_ref[1] += part[:fields]
        return carry

    lax.fori_loop(0, rows // batch, roundings, 0)

    ends = edge_ref[...].astype(jnp.bfloat16)
    total_ref[:, :channels] += dot_nt(stack_ref[:, :128], ends[:, :128])
    total_ref[:, 2 * channels :] += dot_nt(stack_ref[:, 128:], ends[:, 128:])
    grad_lift = small_ref[1]
    for i in range(3):
        rest = total_ref[i * pitch + channels : i * pitch + channels + fields, :]
        for _ in range(3):
            piece = rest.astype(jnp.bfloat16)
            rest = rest - piece.astype(jnp.float32)
            grad_lift += dot_nt(piece, contract_ref[i])
    taps = [total_ref[i * pitch : i * pitch + channels, :] for i in range(3)]
    half = channels // 2
    last = [t[:, 2 * channels :] for t in taps]
    packed = [t[:, : 2 * channels] for t in taps]
    packed.append(jnp.concatenate(last[:2], axis=1))
    packed.append(jnp.concatenate([last[2][:half], last[2][half:]], axis=1))
    packed.append(jnp.concatenate([grad_lift, small_ref[0]], axis=1))
    packed.append(jnp.zeros((8, 2 * channels), jnp.float32))
    packed = jnp.concatenate(packed, axis=0)
    cut = packed.shape[0] // 2
    odd = lax.rem(lax.axis_index("lon"), 2)
    packed_ref[odd] = packed[:cut]
    packed_ref[1 - odd] = packed[cut:]


def backward(arrived, feat, stack, hidden, deriv, forecast, readout, back, contract, capacity, norm):
    rows, fields, width = forecast.shape
    channels = readout.shape[0]
    pitch = feat.shape[0] // (rows + 2)
    blocks = rows * (width // 128)
    packed_rows = (3 * channels + channels + channels // 2 + fields + 8) // 2
    any_space = pl.BlockSpec(memory_space=pl.ANY)
    vmem = pl.BlockSpec(memory_space=pltpu.VMEM)
    return pl.pallas_call(
        functools.partial(backward_kernel, capacity, channels, norm, 0),
        out_shape=(
            jax.ShapeDtypeStruct((rows, fields, width), jnp.bfloat16),
            jax.ShapeDtypeStruct((2, packed_rows, 2 * channels), jnp.float32),
        ),
        in_specs=[any_space] * 5 + [vmem] * 4,
        out_specs=(vmem, vmem),
        scratch_shapes=[
            pltpu.VMEM(arrived.shape, jnp.bfloat16),
            pltpu.VMEM(feat.shape, jnp.bfloat16),
            pltpu.VMEM(hidden.shape, jnp.bfloat16),
            pltpu.VMEM(deriv.shape, jnp.float32),
            pltpu.VMEM(forecast.shape, jnp.float32),
            pltpu.VMEM((blocks, fields, 128), jnp.float32),
            pltpu.VMEM(((rows + 2) * channels, width), jnp.bfloat16),
            pltpu.VMEM((3 * pitch, 3 * channels), jnp.float32),
            pltpu.VMEM((channels, 256), jnp.float32),
            pltpu.VMEM((2, fields, channels), jnp.float32),
            pltpu.SemaphoreType.DMA((5,)),
        ],
        compiler_params=pltpu.CompilerParams(vmem_limit_bytes=VMEM_LIMIT),
        cost_estimate=pl.CostEstimate(
            flops=4 * rows * width * 3 * channels * 3 * pitch,
            bytes_accessed=rows * width * channels * 8,
            transcendentals=0,
        ),
        name="backward",
    )(arrived, feat, hidden, deriv, forecast, stack, readout, back, contract)


def unpack_kernel(channels, mine_ref, other_ref, kernel_ref, lift_ref, head_ref):
    odd = lax.rem(lax.axis_index("lon"), 2) == 1
    mine, other = mine_ref[...], other_ref[...]
    packed = jnp.concatenate([jnp.where(odd, other, mine), jnp.where(odd, mine, other)], axis=0)
    half = channels // 2
    for i in range(3):
        block = packed[i * channels : (i + 1) * channels]
        kernel_ref[3 * i] = block[:, :channels]
        kernel_ref[3 * i + 1] = block[:, channels:]
    block = packed[3 * channels : 4 * channels]
    kernel_ref[2] = block[:, :channels]
    kernel_ref[5] = block[:, channels:]
    block = packed[4 * channels : 4 * channels + half]
    kernel_ref[8, :half] = block[:, :channels]
    kernel_ref[8, half:] = block[:, channels:]
    block = packed[4 * channels + half : 4 * channels + half + lift_ref.shape[0]]
    lift_ref[...] = block[:, :channels]
    head_ref[...] = block[:, channels:].T


def unpack(mine, other, channels, fields):
    return pl.pallas_call(
        functools.partial(unpack_kernel, channels),
        out_shape=(
            jax.ShapeDtypeStruct((9, channels, channels), jnp.float32),
            jax.ShapeDtypeStruct((fields, channels), jnp.float32),
            jax.ShapeDtypeStruct((channels, fields), jnp.float32),
        ),
        name="unpack",
    )(mine, other)


def swap(x, axis, bit):
    return lax.ppermute(x, axis, [(i, i ^ bit) for i in range(lax.axis_size(axis))])


def sum_over(x, axis, low, high):
    if high // low == 4:
        a, b, c = (swap(x, axis, k * low) for k in (1, 2, 3))
        return (x + a) + (b + c)
    bit = low
    while bit < high:
        x = x + swap(x, axis, bit)
        bit *= 2
    return x


def pair_swap(even_sends, odd_sends, axis, periodic):
    count = lax.axis_size(axis)
    even = lax.rem(lax.axis_index(axis), 2) == 0
    inner = [(i, i ^ 1) for i in range(count)]
    outer = []
    for i in range(1, count, 2):
        if i + 1 < count or periodic:
            outer += [(i, (i + 1) % count), ((i + 1) % count, i)]
    got_inner = lax.ppermute(jnp.where(even, odd_sends, even_sends), axis, inner)
    got_outer = lax.ppermute(jnp.where(even, even_sends, odd_sends), axis, outer)
    return jnp.where(even, got_outer, got_inner), jnp.where(even, got_inner, got_outer)


def per_device(
    source,
    intersection_weight,
    dest_tile,
    dest_row,
    prior_state,
    lift_weight,
    kernel,
    readout_weights,
):
    face_count = lax.axis_size("face")
    lon_count = lax.axis_size("lon")
    devices = face_count * lon_count
    src_blocks, intersections = dest_tile.shape
    fields, rows, width = prior_state.shape
    channels = kernel.shape[1]
    pitch = channels + 16
    capacity = max(2, 2 * src_blocks * intersections // devices)
    norm = 1.0 / math.sqrt(rows * face_count * width * lon_count)

    outgoing = regrid(source, intersection_weight, dest_tile, dest_row, devices, capacity)
    arrived = lax.all_to_all(outgoing, ("face", "lon"), split_axis=0, concat_axis=0, tiled=True)
    arrived = arrived.reshape(devices, (capacity + 1) * fields, source.shape[2])

    prior = prior_state.transpose(1, 0, 2)
    top, bottom = pair_swap(prior[0], prior[rows - 1], "face", False)
    columns = [
        jnp.pad(
            jnp.concatenate([top[:, at : at + 1], prior_state[:, :, at], bottom[:, at : at + 1]], axis=1),
            ((0, 0), (0, 128 - rows - 2)),
        )
        for at in (0, width - 1)
    ]
    left, right = pair_swap(columns[0], columns[1], "lon", True)

    taps = kernel.reshape(3, 3, channels, channels)
    lift = jnp.concatenate(
        [lift_weight.T, jnp.eye(fields, dtype=jnp.bfloat16), jnp.zeros((16 - fields, fields), jnp.bfloat16)]
    )
    conv = jnp.pad(
        taps.transpose(1, 3, 0, 2), ((0, 0), (0, 0), (0, 0), (0, pitch - channels))
    ).reshape(3 * channels, 3 * pitch)
    back = taps[::-1].transpose(1, 2, 0, 3).reshape(3 * channels, 3 * channels)
    contract = taps.transpose(0, 2, 1, 3).reshape(3, channels, 3 * channels)
    feat, stack, hidden, deriv, forecast, estimate = forward(
        prior,
        jnp.stack([top, bottom]),
        jnp.concatenate([left, right], axis=1),
        lift,
        conv,
        readout_weights.T,
        channels,
    )
    remapped, packed = backward(
        arrived, feat, stack, hidden, deriv, forecast, readout_weights, back, contract, capacity, norm
    )
    part = packed[0] + swap(packed[1], "lon", 1)
    part = sum_over(part, "face", 1, face_count)
    part = sum_over(part, "lon", 2, lon_count)
    grad_kernel, grad_lift, grad_head = unpack(part, swap(part, "lon", 1), channels, fields)
    return (
        remapped.transpose(1, 0, 2),
        estimate.transpose(1, 0, 2),
        grad_lift,
        grad_kernel,
        grad_head,
    )


def solution(mesh):
    return jax.shard_map(
        per_device,
        mesh=mesh,
        in_specs=(
            P(("face", "lon"), None, None),
            P(("face", "lon"), None, None, None),
            P(("face", "lon"), None),
            P(("face", "lon"), None),
            P(None, "face", "lon"),
            P(),
            P(),
            P(),
        ),
        out_specs=(P(None, "face", "lon"), P(None, "face", "lon"), P(), P(), P()),
        check_vma=False,
    )
```

```python
import functools
import math

import jax
import jax.numpy as jnp
from jax import lax
from jax.experimental import pallas as pl
from jax.experimental.pallas import tpu as pltpu
from jax.sharding import PartitionSpec as P

NT = (((1,), (1,)), ((), ()))
VMEM_LIMIT = 24 * 1024 * 1024
REGRID_VMEM = 60 * 1024 * 1024


def dot(a, b):
    return jnp.dot(a, b, preferred_element_type=jnp.float32)


def dot_nt(a, b):
    return lax.dot_general(a, b, NT, preferred_element_type=jnp.float32)


def sigmoid(x):
    return 1.0 / (1.0 + jnp.exp(-x))


def regrid_kernel(capacity, tile_ref, row_ref, src_ref, wts_hbm, out_ref, wts_ref, count_ref, slot_ref, head_ref, sems):
    blocks, fields, width = src_ref.shape
    intersections = wts_ref.shape[1]
    devices = out_ref.shape[0]
    chunks = sems.shape[0]
    chunk = blocks // chunks
    copies = [
        pltpu.make_async_copy(
            wts_hbm.at[pl.ds(i * chunk, chunk)], wts_ref.at[pl.ds(i * chunk, chunk)], sems.at[i]
        )
        for i in range(chunks)
    ]
    for copy in copies:
        copy.start()
    head_ref[...] = jnp.full_like(head_ref, -1.0)
    for d in range(devices):
        count_ref[d] = 0
    slot_of_lane = lax.rem(lax.broadcasted_iota(jnp.int32, (1, width), 1) // fields, capacity)
    for s in range(blocks):
        for k in range(intersections):
            tile = tile_ref[k, s]
            slot = count_ref[tile]
            count_ref[tile] = slot + 1
            slot_ref[k, s] = slot
            label = row_ref[k, s].astype(jnp.float32)
            head_ref[pl.ds(tile, 1), :] = jnp.where(slot_of_lane == slot, label, head_ref[pl.ds(tile, 1), :])
    out_ref[...] = jnp.zeros_like(out_ref)
    for d in range(devices):
        out_ref[d, capacity] = jnp.broadcast_to(head_ref[d : d + 1, :], (fields, width)).astype(jnp.bfloat16)
    for i in range(chunks):
        copies[i].wait()
        for s in range(i * chunk, (i + 1) * chunk):
            block = src_ref[s]
            for pair in range(0, intersections, 2):
                both = range(pair, min(pair + 2, intersections))
                contrib = dot(block, jnp.concatenate([wts_ref[s, k] for k in both], axis=1)).astype(jnp.bfloat16)
                for k in both:
                    out_ref[tile_ref[k, s], slot_ref[k, s]] = contrib[:, (k - pair) * width : (k - pair + 1) * width]


def regrid(source, weights, dest_tile, dest_row, devices, capacity):
    blocks, fields, width = source.shape
    intersections = weights.shape[1]
    chunks = math.gcd(blocks, 4)
    smem = pl.BlockSpec(memory_space=pltpu.SMEM)
    vmem = pl.BlockSpec(memory_space=pltpu.VMEM)
    return pl.pallas_call(
        functools.partial(regrid_kernel, capacity),
        out_shape=jax.ShapeDtypeStruct((devices, capacity + 1, fields, width), jnp.bfloat16),
        in_specs=[smem, smem, vmem, pl.BlockSpec(memory_space=pltpu.HBM)],
        out_specs=vmem,
        scratch_shapes=[
            pltpu.VMEM(weights.shape, jnp.bfloat16),
            pltpu.SMEM((devices,), jnp.int32),
            pltpu.SMEM((intersections, blocks), jnp.int32),
            pltpu.VMEM((devices, width), jnp.float32),
            pltpu.SemaphoreType.DMA((chunks,)),
        ],
        compiler_params=pltpu.CompilerParams(vmem_limit_bytes=REGRID_VMEM),
        cost_estimate=pl.CostEstimate(
            flops=2 * weights.size * fields, bytes_accessed=2 * weights.size, transcendentals=0
        ),
        name="regrid",
    )(dest_tile.T, dest_row.T, source, weights)


def lift_tile(prior_ref, edge_ref, side_ref, lift, feat_ref):
    rows, fields, width = prior_ref.shape
    pitch = lift.shape[0]
    for at in range(rows + 2):
        values = edge_ref[0] if at == 0 else edge_ref[1] if at == rows + 1 else prior_ref[at - 1]
        feat_ref[at * pitch : (at + 1) * pitch, :] = dot(lift, values).astype(jnp.bfloat16)
    side = dot(lift, side_ref[...])
    shifted = [side] + [pltpu.roll(side, 256 - i, 1) for i in (1, 2)]
    return jnp.concatenate(shifted, axis=0).astype(jnp.bfloat16)


def forward_kernel(
    prior_ref,
    edge_ref,
    side_ref,
    lift_weight_ref,
    kernel_ref,
    readout_ref,
    act_ref,
    forecast_ref,
    estimate_ref,
    lift_ref,
    back_ref,
    contract_ref,
    feat_ref,
    halo_ref,
    conv_ref,
    hidden_ref,
):
    rows, fields, width = prior_ref.shape
    channels = kernel_ref.shape[1]
    pitch = lift_ref.shape[0]

    taps = [kernel_ref[t].astype(jnp.float32) for t in range(9)]
    for i in range(3):
        back_ref[i * channels : (i + 1) * channels, :] = jnp.concatenate(
            [taps[6 + i], taps[3 + i], taps[i]], axis=1
        ).astype(jnp.bfloat16)
        contract_ref[i] = jnp.concatenate(taps[3 * i : 3 * i + 3], axis=1).astype(jnp.bfloat16)
    empty = jnp.zeros((pitch - channels, 3 * channels), jnp.float32)
    by_input = [piece for i in range(3) for piece in (jnp.concatenate(taps[3 * i : 3 * i + 3], axis=1), empty)]
    conv_ref[...] = jnp.concatenate(by_input, axis=0).T.astype(jnp.bfloat16)
    same = lax.broadcasted_iota(jnp.int32, (fields, pitch - channels), 0) == lax.broadcasted_iota(
        jnp.int32, (fields, pitch - channels), 1
    )
    lift = jnp.concatenate([lift_weight_ref[...].astype(jnp.float32), jnp.where(same, 1.0, 0.0)], axis=1)
    lift_ref[...] = lift.T.astype(jnp.bfloat16)
    readout = readout_ref[...].astype(jnp.float32).T.astype(jnp.bfloat16)

    stack = lift_tile(prior_ref, edge_ref, side_ref, lift_ref[...], feat_ref)
    halo_ref[:, :128] = dot(conv_ref[:channels, :], stack[:, :128])
    halo_ref[:, 128:] = dot(conv_ref[2 * channels :, :], stack[:, 128:])
    lane = lax.broadcasted_iota(jnp.int32, (channels, width), 1)
    for y in range(rows):
        parts = dot(conv_ref[...], feat_ref[y * pitch : (y + 3) * pitch, :])
        left = pltpu.roll(parts[:channels], 1, 1)
        right = pltpu.roll(parts[2 * channels :], width - 1, 1)
        from_left = pltpu.roll(halo_ref[:, :128], (128 - y) % 128, 1)
        from_right = pltpu.roll(halo_ref[:, 128:], 127 - y, 1)
        spread = [jnp.zeros_like(from_left)] * (width // 128 - 1)
        left = jnp.where(lane == 0, jnp.concatenate([from_left] + spread, axis=1), left)
        right = jnp.where(lane == width - 1, jnp.concatenate(spread + [from_right], axis=1), right)
        act = parts[channels : 2 * channels] + left + right
        act_ref[y * channels : (y + 1) * channels, :] = act
        hidden_ref[y * channels : (y + 1) * channels, :] = (act * sigmoid(act)).astype(jnp.bfloat16)
    for y in range(rows):
        increment = dot(readout, hidden_ref[y * channels : (y + 1) * channels, :])
        forecast = prior_ref[y].astype(jnp.float32) + increment
        forecast_ref[y] = forecast
    estimate_ref[...] = jnp.transpose(forecast_ref[...], (1, 0, 2)).astype(jnp.bfloat16)


def forward(prior, edges, sides, lift_weight, kernel, readout):
    rows, fields, width = prior.shape
    channels = kernel.shape[1]
    pitch = channels + 16
    vmem = pl.BlockSpec(memory_space=pltpu.VMEM)
    return pl.pallas_call(
        forward_kernel,
        out_shape=(
            jax.ShapeDtypeStruct((rows * channels, width), jnp.float32),
            jax.ShapeDtypeStruct((rows, fields, width), jnp.float32),
            jax.ShapeDtypeStruct((fields, rows, width), jnp.bfloat16),
            jax.ShapeDtypeStruct((pitch, fields), jnp.bfloat16),
            jax.ShapeDtypeStruct((3 * channels, 3 * channels), jnp.bfloat16),
            jax.ShapeDtypeStruct((3, channels, 3 * channels), jnp.bfloat16),
        ),
        in_specs=[vmem] * 6,
        out_specs=[vmem] * 6,
        scratch_shapes=[
            pltpu.VMEM(((rows + 2) * pitch, width), jnp.bfloat16),
            pltpu.VMEM((channels, 256), jnp.float32),
            pltpu.VMEM((3 * channels, 3 * pitch), jnp.bfloat16),
            pltpu.VMEM((rows * channels, width), jnp.bfloat16),
        ],
        compiler_params=pltpu.CompilerParams(vmem_limit_bytes=VMEM_LIMIT),
        cost_estimate=pl.CostEstimate(
            flops=2 * rows * width * 3 * channels * 3 * pitch,
            bytes_accessed=rows * width * channels * 8,
            transcendentals=rows * width * channels * 2,
        ),
        name="forward",
    )(prior, edges, sides, lift_weight, kernel, readout)


def backward_kernel(
    capacity,
    channels,
    norm,
    arrived_hbm,
    prior_ref,
    edge_ref,
    side_ref,
    lift_ref,
    act_ref,
    forecast_ref,
    readout_ref,
    back_ref,
    contract_ref,
    remapped_ref,
    packed_ref,
    arrived_ref,
    feat_ref,
    hidden_ref,
    misfit_ref,
    slope_ref,
    before_ref,
    after_ref,
    delta_ref,
    sem,
):
    copy = pltpu.make_async_copy(arrived_hbm, arrived_ref, sem)
    copy.start()
    fields, rows, width = remapped_ref.shape
    pitch = lift_ref.shape[0]
    devices = arrived_ref.shape[0]
    per_row = width // 128
    blocks = rows * per_row
    group = 128 // (fields * capacity)

    stack = lift_tile(prior_ref, edge_ref, side_ref, lift_ref[...], feat_ref)
    slope_ref[:channels, :] = jnp.zeros((channels, width), jnp.bfloat16)
    slope_ref[(rows + 1) * channels :, :] = jnp.zeros((channels, width), jnp.bfloat16)
    lane = lax.broadcasted_iota(jnp.int32, (fields, 128), 1)
    sublane = lax.broadcasted_iota(jnp.int32, (fields, 128), 0)
    wanted = lax.broadcasted_iota(jnp.int32, (blocks, fields, 256), 0) * fields

    copy.wait()
    picked = None
    for first in range(0, devices, 2 * group):
        labels, data = [], []
        for half in range(2):
            label = None
            for d in range(group):
                device = first + half * group + d
                mine = arrived_ref[device, capacity * fields : (capacity + 1) * fields, :].astype(jnp.float32)
                label = mine if label is None else jnp.where(lane // (fields * capacity) == d, mine, label)
                data.append(arrived_ref[device, : capacity * fields, :])
            labels.append(label.astype(jnp.int32) * fields + lane % fields - sublane)
        hits = jnp.concatenate(labels, axis=1)[None] == wanted
        hits = jnp.where(hits, 1.0, 0.0).reshape(blocks * fields, 256).astype(jnp.bfloat16)
        part = dot(hits, jnp.concatenate(data, axis=0))
        picked = part if picked is None else picked + part
    picked = picked.astype(jnp.bfloat16).astype(jnp.float32).reshape(rows, per_row, fields, 128)
    for b in range(per_row):
        remapped_ref[:, :, b * 128 : (b + 1) * 128] = jnp.transpose(picked[:, b], (1, 0, 2)).astype(jnp.bfloat16)
    for y in range(rows):
        target = jnp.concatenate([picked[y, b] for b in range(per_row)], axis=1)
        misfit = (forecast_ref[y] - target) * norm
        misfit_ref[:, y * width : (y + 1) * width] = misfit.astype(jnp.bfloat16)

    col = lax.broadcasted_iota(jnp.int32, (channels, width), 1)
    lane = lax.broadcasted_iota(jnp.int32, (channels, 128), 1)
    ends_left = ends_right = jnp.zeros((channels, 128), jnp.float32)
    for y in range(rows):
        here = slice(y * channels, (y + 1) * channels)
        latent = dot(readout_ref[...], misfit_ref[:, y * width : (y + 1) * width])
        act = act_ref[here, :]
        sig = sigmoid(act)
        hidden_ref[here, :] = (act * sig).astype(jnp.bfloat16)
        slope = latent * sig * (1.0 + act * (1.0 - sig))
        slope_ref[(y + 1) * channels : (y + 2) * channels, :] = slope.astype(jnp.bfloat16)
        before_ref[here, :] = jnp.where(col == width - 1, 0.0, pltpu.roll(slope, width - 1, 1)).astype(jnp.bfloat16)
        after_ref[here, :] = jnp.where(col == 0, 0.0, pltpu.roll(slope, 1, 1)).astype(jnp.bfloat16)
        ends_left += pltpu.roll(jnp.where(lane == 0, slope[:, :128], 0.0), y, 1)
        ends_right += pltpu.roll(jnp.where(lane == 127, slope[:, -128:], 0.0), y + 1, 1)

    batch = 4
    total = None
    for first in range(0, rows, batch):
        span = range(first, first + batch)
        features = jnp.concatenate([feat_ref[y * pitch : (y + 3) * pitch, :] for y in span], axis=1)
        trios = jnp.concatenate(
            [
                jnp.concatenate([ref[(y + d) * channels : (y + d + 1) * channels, :] for y in span], axis=1)
                for ref, d in ((before_ref, 0), (slope_ref, 1), (after_ref, 0))
            ],
            axis=0,
        )
        part = dot_nt(features, trios)
        total = part if total is None else total + part
    from_left = dot_nt(stack[:, :128], ends_left.astype(jnp.bfloat16))
    from_right = dot_nt(stack[:, 128:], ends_right.astype(jnp.bfloat16))
    middle = jnp.zeros((3 * pitch, channels), jnp.float32)
    total += jnp.concatenate([from_left, middle, from_right], axis=1)

    delta_ref[:channels, :] = jnp.zeros((channels, width), jnp.bfloat16)
    delta_ref[(rows - 1) * channels :, :] = jnp.zeros((channels, width), jnp.bfloat16)
    for y in range(1, rows - 1):
        parts = dot(back_ref[...], slope_ref[y * channels : (y + 3) * channels, :])
        grad = (
            parts[channels : 2 * channels]
            + pltpu.roll(parts[:channels], width - 1, 1)
            + pltpu.roll(parts[2 * channels :], 1, 1)
        )
        inside = (col > 0) & (col < width - 1)
        delta = jnp.where(inside, grad.astype(jnp.bfloat16).astype(jnp.float32) - grad, 0.0)
        delta_ref[y * channels : (y + 1) * channels, :] = delta.astype(jnp.bfloat16)

    grad_lift = grad_head = jnp.zeros((fields, channels), jnp.float32)
    for first in range(0, rows, batch):
        span = range(first, first + batch)
        here = [slice(y * channels, (y + 1) * channels) for y in span]
        grad_head += dot_nt(
            misfit_ref[:, first * width : (first + batch) * width],
            jnp.concatenate([hidden_ref[h, :] for h in here], axis=1),
        )
        states = jnp.concatenate(
            [feat_ref[(y + 1) * pitch + channels : (y + 2) * pitch, :] for y in span], axis=1
        )
        grad_lift += dot_nt(states, jnp.concatenate([delta_ref[h, :] for h in here], axis=1))[:fields]
    for i in range(3):
        rest = total[i * pitch + channels : i * pitch + channels + fields, :]
        for _ in range(3):
            piece = rest.astype(jnp.bfloat16)
            rest = rest - piece.astype(jnp.float32)
            grad_lift += dot_nt(piece, contract_ref[i])
    taps = [total[i * pitch : i * pitch + channels, :] for i in range(3)]
    half = channels // 2
    last = [t[:, 2 * channels :] for t in taps]
    packed = [t[:, : 2 * channels] for t in taps]
    packed.append(jnp.concatenate(last[:2], axis=1))
    packed.append(jnp.concatenate([last[2][:half], last[2][half:]], axis=1))
    packed.append(jnp.concatenate([grad_lift, grad_head], axis=1))
    packed.append(jnp.zeros((8, 2 * channels), jnp.float32))
    packed = jnp.concatenate(packed, axis=0)
    cut = packed.shape[0] // 2
    odd = lax.rem(lax.axis_index("lon"), 2)
    packed_ref[odd] = packed[:cut]
    packed_ref[1 - odd] = packed[cut:]


def backward(arrived, prior, edges, sides, lift, act, forecast, readout, back, contract, capacity, norm):
    rows, fields, width = forecast.shape
    channels = readout.shape[0]
    pitch = lift.shape[0]
    packed_rows = (3 * channels + channels + channels // 2 + fields + 8) // 2
    vmem = pl.BlockSpec(memory_space=pltpu.VMEM)
    return pl.pallas_call(
        functools.partial(backward_kernel, capacity, channels, norm),
        out_shape=(
            jax.ShapeDtypeStruct((fields, rows, width), jnp.bfloat16),
            jax.ShapeDtypeStruct((2, packed_rows, 2 * channels), jnp.float32),
        ),
        in_specs=[pl.BlockSpec(memory_space=pl.ANY)] + [vmem] * 9,
        out_specs=(vmem, vmem),
        scratch_shapes=[
            pltpu.VMEM(arrived.shape, jnp.bfloat16),
            pltpu.VMEM(((rows + 2) * pitch, width), jnp.bfloat16),
            pltpu.VMEM((rows * channels, width), jnp.bfloat16),
            pltpu.VMEM((fields, rows * width), jnp.bfloat16),
            pltpu.VMEM(((rows + 2) * channels, width), jnp.bfloat16),
            pltpu.VMEM((rows * channels, width), jnp.bfloat16),
            pltpu.VMEM((rows * channels, width), jnp.bfloat16),
            pltpu.VMEM((rows * channels, width), jnp.bfloat16),
            pltpu.SemaphoreType.DMA,
        ],
        compiler_params=pltpu.CompilerParams(vmem_limit_bytes=VMEM_LIMIT),
        cost_estimate=pl.CostEstimate(
            flops=4 * rows * width * 3 * channels * 3 * pitch,
            bytes_accessed=rows * width * channels * 8,
            transcendentals=0,
        ),
        name="backward",
    )(arrived, prior, edges, sides, lift, act, forecast, readout, back, contract)


def unpack_kernel(channels, mine_ref, other_ref, kernel_ref, lift_ref, head_ref):
    odd = lax.rem(lax.axis_index("lon"), 2) == 1
    mine, other = mine_ref[...], other_ref[...]
    packed = jnp.concatenate([jnp.where(odd, other, mine), jnp.where(odd, mine, other)], axis=0)
    half = channels // 2
    for i in range(3):
        block = packed[i * channels : (i + 1) * channels]
        kernel_ref[3 * i] = block[:, :channels]
        kernel_ref[3 * i + 1] = block[:, channels:]
    block = packed[3 * channels : 4 * channels]
    kernel_ref[2] = block[:, :channels]
    kernel_ref[5] = block[:, channels:]
    block = packed[4 * channels : 4 * channels + half]
    kernel_ref[8, :half] = block[:, :channels]
    kernel_ref[8, half:] = block[:, channels:]
    block = packed[4 * channels + half : 4 * channels + half + lift_ref.shape[0]]
    lift_ref[...] = block[:, :channels]
    head_ref[...] = block[:, channels:]


def unpack(mine, other, channels, fields):
    return pl.pallas_call(
        functools.partial(unpack_kernel, channels),
        out_shape=(
            jax.ShapeDtypeStruct((9, channels, channels), jnp.float32),
            jax.ShapeDtypeStruct((fields, channels), jnp.float32),
            jax.ShapeDtypeStruct((fields, channels), jnp.float32),
        ),
        compiler_params=pltpu.CompilerParams(vmem_limit_bytes=VMEM_LIMIT),
        name="unpack",
    )(mine, other)


def swap(x, axis, bit):
    return lax.ppermute(x, axis, [(i, i ^ bit) for i in range(lax.axis_size(axis))])


def sum_over(x, axis, low, high):
    if high // low == 4:
        a, b, c = (swap(x, axis, k * low) for k in (1, 2, 3))
        return (x + a) + (b + c)
    bit = low
    while bit < high:
        x = x + swap(x, axis, bit)
        bit *= 2
    return x


def pair_swap(even_sends, odd_sends, axis, periodic):
    count = lax.axis_size(axis)
    even = lax.rem(lax.axis_index(axis), 2) == 0
    inner = [(i, i ^ 1) for i in range(count)]
    outer = []
    for i in range(1, count, 2):
        if i + 1 < count or periodic:
            outer += [(i, (i + 1) % count), ((i + 1) % count, i)]
    got_inner = lax.ppermute(jnp.where(even, odd_sends, even_sends), axis, inner)
    got_outer = lax.ppermute(jnp.where(even, even_sends, odd_sends), axis, outer)
    return jnp.where(even, got_outer, got_inner), jnp.where(even, got_inner, got_outer)


def per_device(
    source,
    intersection_weight,
    dest_tile,
    dest_row,
    prior_state,
    lift_weight,
    kernel,
    readout_weights,
):
    face_count = lax.axis_size("face")
    lon_count = lax.axis_size("lon")
    devices = face_count * lon_count
    src_blocks, intersections = dest_tile.shape
    fields, rows, width = prior_state.shape
    channels = kernel.shape[1]
    capacity = max(2, 2 * src_blocks * intersections // devices)
    norm = 1.0 / math.sqrt(rows * face_count * width * lon_count)

    outgoing = regrid(source, intersection_weight, dest_tile, dest_row, devices, capacity)
    outgoing, prior_state, kernel, lift_weight, readout_weights = lax.optimization_barrier(
        (outgoing, prior_state, kernel, lift_weight, readout_weights)
    )
    arrived = lax.all_to_all(outgoing, ("face", "lon"), split_axis=0, concat_axis=0, tiled=True)
    arrived = arrived.reshape(devices, (capacity + 1) * fields, source.shape[2])

    prior = prior_state.transpose(1, 0, 2)
    top, bottom = pair_swap(prior[0], prior[rows - 1], "face", False)
    columns = [
        jnp.pad(
            jnp.concatenate([top[:, at : at + 1], prior_state[:, :, at], bottom[:, at : at + 1]], axis=1),
            ((0, 0), (0, 128 - rows - 2)),
        )
        for at in (0, width - 1)
    ]
    left, right = pair_swap(columns[0], columns[1], "lon", True)

    edges = jnp.stack([top, bottom])
    sides = jnp.concatenate([left, right], axis=1)
    act, forecast, estimate, lift, back, contract = forward(
        prior, edges, sides, lift_weight, kernel, readout_weights
    )
    remapped, packed = backward(
        arrived, prior, edges, sides, lift, act, forecast, readout_weights, back, contract, capacity, norm
    )
    part = packed[0] + swap(packed[1], "lon", 1)
    part = sum_over(part, "face", 1, face_count)
    part = sum_over(part, "lon", 2, lon_count)
    grad_kernel, grad_lift, grad_head = unpack(part, swap(part, "lon", 1), channels, fields)
    return (
        remapped,
        estimate,
        grad_lift,
        grad_kernel,
        grad_head.T,
    )


def solution(mesh):
    return jax.shard_map(
        per_device,
        mesh=mesh,
        in_specs=(
            P(("face", "lon"), None, None),
            P(("face", "lon"), None, None, None),
            P(("face", "lon"), None),
            P(("face", "lon"), None),
            P(None, "face", "lon"),
            P(),
            P(),
            P(),
        ),
        out_specs=(P(None, "face", "lon"), P(None, "face", "lon"), P(), P(), P()),
        check_vma=False,
    )
```

```python
import functools
import math

import jax
import jax.numpy as jnp
from jax import lax
from jax.experimental import pallas as pl
from jax.experimental.pallas import tpu as pltpu
from jax.sharding import PartitionSpec as P

NT = (((1,), (1,)), ((), ()))
VMEM_LIMIT = 24 * 1024 * 1024
REGRID_VMEM = 60 * 1024 * 1024


def dot(a, b):
    return jnp.dot(a, b, preferred_element_type=jnp.float32)


def dot_nt(a, b):
    return lax.dot_general(a, b, NT, preferred_element_type=jnp.float32)


def sigmoid(x):
    return 1.0 / (1.0 + jnp.exp(-x))


def regrid_kernel(capacity, tile_ref, row_ref, src_ref, wts_hbm, out_ref, wts_ref, count_ref, slot_ref, head_ref, sems):
    blocks, fields, width = src_ref.shape
    intersections = wts_ref.shape[1]
    devices = out_ref.shape[0]
    chunks = sems.shape[0]
    chunk = blocks // chunks
    copies = [
        pltpu.make_async_copy(
            wts_hbm.at[pl.ds(i * chunk, chunk)], wts_ref.at[pl.ds(i * chunk, chunk)], sems.at[i]
        )
        for i in range(chunks)
    ]
    for copy in copies:
        copy.start()
    head_ref[...] = jnp.full_like(head_ref, -1.0)
    for d in range(devices):
        count_ref[d] = 0
    slot_of_lane = lax.rem(lax.broadcasted_iota(jnp.int32, (1, width), 1), capacity)
    for s in range(blocks):
        for k in range(intersections):
            tile = tile_ref[k, s]
            slot = count_ref[tile]
            count_ref[tile] = slot + 1
            slot_ref[k, s] = slot
            label = row_ref[k, s].astype(jnp.float32)
            head_ref[pl.ds(tile, 1), :] = jnp.where(slot_of_lane == slot, label, head_ref[pl.ds(tile, 1), :])
    out_ref[...] = jnp.zeros_like(out_ref)
    for d in range(devices):
        out_ref[d, capacity] = jnp.broadcast_to(head_ref[d : d + 1, :], (fields, width)).astype(jnp.bfloat16)
    for i in range(chunks):
        copies[i].wait()
        for s in range(i * chunk, (i + 1) * chunk):
            block = src_ref[s]
            for pair in range(0, intersections, 2):
                both = range(pair, min(pair + 2, intersections))
                contrib = dot(block, jnp.concatenate([wts_ref[s, k] for k in both], axis=1)).astype(jnp.bfloat16)
                for k in both:
                    out_ref[tile_ref[k, s], slot_ref[k, s]] = contrib[:, (k - pair) * width : (k - pair + 1) * width]


def regrid(source, weights, dest_tile, dest_row, devices, capacity):
    blocks, fields, width = source.shape
    intersections = weights.shape[1]
    chunks = math.gcd(blocks, 4)
    smem = pl.BlockSpec(memory_space=pltpu.SMEM)
    vmem = pl.BlockSpec(memory_space=pltpu.VMEM)
    return pl.pallas_call(
        functools.partial(regrid_kernel, capacity),
        out_shape=jax.ShapeDtypeStruct((devices, capacity + 1, fields, width), jnp.bfloat16),
        in_specs=[smem, smem, vmem, pl.BlockSpec(memory_space=pl.ANY)],
        out_specs=vmem,
        scratch_shapes=[
            pltpu.VMEM(weights.shape, jnp.bfloat16),
            pltpu.SMEM((devices,), jnp.int32),
            pltpu.SMEM((intersections, blocks), jnp.int32),
            pltpu.VMEM((devices, width), jnp.float32),
            pltpu.SemaphoreType.DMA((chunks,)),
        ],
        compiler_params=pltpu.CompilerParams(vmem_limit_bytes=REGRID_VMEM),
        cost_estimate=pl.CostEstimate(
            flops=2 * weights.size * fields, bytes_accessed=2 * weights.size, transcendentals=0
        ),
        name="regrid",
    )(dest_tile.T, dest_row.T, source, weights)


def lift_rows(prior_ref, edge_ref, lift, feat_ref):
    rows = prior_ref.shape[0]
    pitch = lift.shape[0]
    for at in range(rows + 2):
        values = edge_ref[0] if at == 0 else edge_ref[1] if at == rows + 1 else prior_ref[at - 1]
        feat_ref[at * pitch : (at + 1) * pitch, :] = dot(lift, values).astype(jnp.bfloat16)


def convolve_kernel(
    prior_ref,
    edge_ref,
    lift_weight_ref,
    kernel_ref,
    act_ref,
    lift_ref,
    conv_ref,
    back_ref,
    contract_ref,
    feat_ref,
):
    rows, fields, width = prior_ref.shape
    channels = kernel_ref.shape[1]
    pitch = lift_ref.shape[0]

    taps = [kernel_ref[t].astype(jnp.float32) for t in range(9)]
    for i in range(3):
        back_ref[i * channels : (i + 1) * channels, :] = jnp.concatenate(
            [taps[6 + i], taps[3 + i], taps[i]], axis=1
        ).astype(jnp.bfloat16)
        contract_ref[i] = jnp.concatenate(taps[3 * i : 3 * i + 3], axis=1).astype(jnp.bfloat16)
    empty = jnp.zeros((pitch - channels, 3 * channels), jnp.float32)
    by_input = [piece for i in range(3) for piece in (jnp.concatenate(taps[3 * i : 3 * i + 3], axis=1), empty)]
    conv_ref[...] = jnp.concatenate(by_input, axis=0).T.astype(jnp.bfloat16)
    same = lax.broadcasted_iota(jnp.int32, (fields, pitch - channels), 0) == lax.broadcasted_iota(
        jnp.int32, (fields, pitch - channels), 1
    )
    lift = jnp.concatenate([lift_weight_ref[...].astype(jnp.float32), jnp.where(same, 1.0, 0.0)], axis=1)
    lift_ref[...] = lift.T.astype(jnp.bfloat16)

    lift_rows(prior_ref, edge_ref, lift_ref[...], feat_ref)
    lane = lax.broadcasted_iota(jnp.int32, (channels, width), 1)
    for y in range(rows):
        parts = dot(conv_ref[...], feat_ref[y * pitch : (y + 3) * pitch, :])
        left = jnp.where(lane == 0, 0.0, pltpu.roll(parts[:channels], 1, 1))
        right = jnp.where(lane == width - 1, 0.0, pltpu.roll(parts[2 * channels :], width - 1, 1))
        act_ref[y * channels : (y + 1) * channels, :] = parts[channels : 2 * channels] + left + right


def convolve(prior, edges, lift_weight, kernel):
    rows, fields, width = prior.shape
    channels = kernel.shape[1]
    pitch = channels + 16
    vmem = pl.BlockSpec(memory_space=pltpu.VMEM)
    return pl.pallas_call(
        convolve_kernel,
        out_shape=(
            jax.ShapeDtypeStruct((rows * channels, width), jnp.float32),
            jax.ShapeDtypeStruct((pitch, fields), jnp.bfloat16),
            jax.ShapeDtypeStruct((3 * channels, 3 * pitch), jnp.bfloat16),
            jax.ShapeDtypeStruct((3 * channels, 3 * channels), jnp.bfloat16),
            jax.ShapeDtypeStruct((3, channels, 3 * channels), jnp.bfloat16),
        ),
        in_specs=[vmem] * 4,
        out_specs=[vmem] * 5,
        scratch_shapes=[pltpu.VMEM(((rows + 2) * pitch, width), jnp.bfloat16)],
        compiler_params=pltpu.CompilerParams(vmem_limit_bytes=VMEM_LIMIT),
        cost_estimate=pl.CostEstimate(
            flops=2 * rows * width * 3 * channels * 3 * pitch,
            bytes_accessed=rows * width * channels * 8,
            transcendentals=0,
        ),
        name="convolve",
    )(prior, edges, lift_weight, kernel)


def finish_kernel(
    part_ref,
    prior_ref,
    side_ref,
    lift_ref,
    conv_ref,
    readout_ref,
    act_ref,
    stack_ref,
    forecast_ref,
    estimate_ref,
    halo_ref,
    hidden_ref,
    by_row_ref,
):
    rows, fields, width = prior_ref.shape
    channels = readout_ref.shape[0]
    side = dot(lift_ref[...], side_ref[...])
    shifted = [side] + [pltpu.roll(side, 256 - i, 1) for i in (1, 2)]
    stack = jnp.concatenate(shifted, axis=0).astype(jnp.bfloat16)
    stack_ref[...] = stack
    halo_ref[:, :128] = dot(conv_ref[:channels, :], stack[:, :128])
    halo_ref[:, 128:] = dot(conv_ref[2 * channels :, :], stack[:, 128:])
    readout = readout_ref[...].astype(jnp.float32).T.astype(jnp.bfloat16)
    lane = lax.broadcasted_iota(jnp.int32, (channels, 128), 1)
    spread = [jnp.zeros((channels, 128), jnp.float32)] * (width // 128 - 1)
    for y in range(rows):
        here = slice(y * channels, (y + 1) * channels)
        from_left = jnp.where(lane == 0, pltpu.roll(halo_ref[:, :128], (128 - y) % 128, 1), 0.0)
        from_right = jnp.where(lane == 127, pltpu.roll(halo_ref[:, 128:], 127 - y, 1), 0.0)
        act = (
            part_ref[here, :]
            + jnp.concatenate([from_left] + spread, axis=1)
            + jnp.concatenate(spread + [from_right], axis=1)
        )
        act_ref[here, :] = act
        hidden_ref[here, :] = (act * sigmoid(act)).astype(jnp.bfloat16)
    for y in range(rows):
        increment = dot(readout, hidden_ref[y * channels : (y + 1) * channels, :])
        by_row_ref[y] = prior_ref[y].astype(jnp.float32) + increment
    forecast = jnp.transpose(by_row_ref[...], (1, 0, 2))
    forecast_ref[...] = forecast
    estimate_ref[...] = forecast.astype(jnp.bfloat16)


def finish(part, prior, sides, lift, conv, readout):
    rows, fields, width = prior.shape
    channels = readout.shape[0]
    vmem = pl.BlockSpec(memory_space=pltpu.VMEM)
    return pl.pallas_call(
        finish_kernel,
        out_shape=(
            jax.ShapeDtypeStruct(part.shape, jnp.float32),
            jax.ShapeDtypeStruct((conv.shape[1], 256), jnp.bfloat16),
            jax.ShapeDtypeStruct((fields, rows, width), jnp.float32),
            jax.ShapeDtypeStruct((fields, rows, width), jnp.bfloat16),
        ),
        in_specs=[vmem] * 6,
        out_specs=[vmem] * 4,
        scratch_shapes=[
            pltpu.VMEM((channels, 256), jnp.float32),
            pltpu.VMEM((rows * channels, width), jnp.bfloat16),
            pltpu.VMEM((rows, fields, width), jnp.float32),
        ],
        input_output_aliases={0: 0},
        compiler_params=pltpu.CompilerParams(vmem_limit_bytes=VMEM_LIMIT),
        cost_estimate=pl.CostEstimate(
            flops=2 * rows * width * channels * fields,
            bytes_accessed=rows * width * channels * 8,
            transcendentals=rows * width * channels * 2,
        ),
        name="finish",
    )(part, prior, sides, lift, conv, readout)


def backward_kernel(
    capacity,
    channels,
    norm,
    arrived_ref,
    prior_ref,
    edge_ref,
    stack_ref,
    lift_ref,
    act_ref,
    forecast_ref,
    readout_ref,
    remapped_ref,
    packed_ref,
    slope_ref,
    moment_ref,
    feat_ref,
    hidden_ref,
    block_ref,
    misfit_ref,
    state_ref,
    before_ref,
    after_ref,
):
    fields, rows, width = remapped_ref.shape
    pitch = lift_ref.shape[0]
    devices = arrived_ref.shape[0]
    per_row = width // 128
    slots = devices * capacity

    lift_rows(prior_ref, edge_ref, lift_ref[...], feat_ref)
    slope_ref[:channels, :] = jnp.zeros((channels, width), jnp.bfloat16)
    slope_ref[(rows + 1) * channels :, :] = jnp.zeros((channels, width), jnp.bfloat16)
    depth = fields * rows
    lane = lax.broadcasted_iota(jnp.int32, (fields, depth), 1)
    spread = jnp.where(lane // rows == lax.broadcasted_iota(jnp.int32, (fields, depth), 0), 1.0, 0.0)
    spread = dot(readout_ref[...], spread.astype(jnp.bfloat16))
    lane = lax.broadcasted_iota(jnp.int32, (channels, depth), 1) % rows
    for y in range(rows):
        block_ref[y * channels : (y + 1) * channels, :] = jnp.where(lane == y, spread, 0.0).astype(jnp.bfloat16)

    labels = []
    for first in range(0, devices, 128 // capacity):
        lane = lax.broadcasted_iota(jnp.int32, (fields, 128), 1) // capacity
        label = None
        for d in range(min(devices, 128 // capacity)):
            mine = arrived_ref[first + d, capacity * fields : (capacity + 1) * fields, :].astype(jnp.float32)
            label = mine if label is None else jnp.where(lane == d, mine, label)
        labels.append(label)
    labels = jnp.concatenate(labels, axis=1).astype(jnp.int32)
    tile_blocks = rows * per_row
    labels = jnp.concatenate([labels] * (tile_blocks // fields), axis=0)
    at = lax.broadcasted_iota(jnp.int32, (tile_blocks, slots), 0)
    hits = jnp.where(labels == (at % rows) * per_row + at // rows, 1.0, 0.0).astype(jnp.bfloat16)
    data = arrived_ref[:, : capacity * fields, :].astype(jnp.float32).reshape(slots, fields, 128)
    data = jnp.transpose(data, (1, 0, 2)).astype(jnp.bfloat16)
    for f in range(0, fields, 2):
        picked = dot(hits, jnp.concatenate([data[f], data[f + 1]], axis=1))
        for g in range(2):
            target = picked[:, g * 128 : (g + 1) * 128].astype(jnp.bfloat16)
            target = jnp.concatenate([target[b * rows : (b + 1) * rows] for b in range(per_row)], axis=1)
            remapped_ref[f + g] = target
            misfit_ref[f + g] = (forecast_ref[f + g] - target.astype(jnp.float32)) * norm
    by_row = jnp.transpose(misfit_ref[...], (1, 0, 2))
    empty = jnp.zeros((fields, width), jnp.float32)
    for y in range(rows):
        state_ref[:, y * width : (y + 1) * width] = jnp.concatenate([by_row[y], empty], axis=0).astype(jnp.bfloat16)

    col = lax.broadcasted_iota(jnp.int32, (channels, width), 1)
    lane = lax.broadcasted_iota(jnp.int32, (channels, 128), 1)
    ends_left = ends_right = jnp.zeros((channels, 128), jnp.float32)
    batch = 8
    misfits = misfit_ref[...].reshape(depth, width).astype(jnp.bfloat16)
    for first in range(0, rows, batch):
        latents = dot(block_ref[first * channels : (first + batch) * channels, :], misfits)
        for y in range(first, first + batch):
            here = slice(y * channels, (y + 1) * channels)
            act = act_ref[here, :]
            sig = sigmoid(act)
            hidden_ref[here, :] = (act * sig).astype(jnp.bfloat16)
            latent = latents[(y - first) * channels : (y - first + 1) * channels]
            slope = latent * sig * (1.0 + act * (1.0 - sig))
            slope_ref[(y + 1) * channels : (y + 2) * channels, :] = slope.astype(jnp.bfloat16)
            before = jnp.where(col == width - 1, 0.0, pltpu.roll(slope, width - 1, 1))
            before_ref[here, :] = before.astype(jnp.bfloat16)
            after_ref[here, :] = jnp.where(col == 0, 0.0, pltpu.roll(slope, 1, 1)).astype(jnp.bfloat16)
            ends_left += pltpu.roll(jnp.where(lane == 0, slope[:, :128], 0.0), y, 1)
            ends_right += pltpu.roll(jnp.where(lane == 127, slope[:, -128:], 0.0), y + 1, 1)

    total = None
    for first in range(0, rows, batch):
        span = range(first, first + batch)
        features = jnp.concatenate([feat_ref[y * pitch : (y + 3) * pitch, :] for y in span], axis=1)
        features = jnp.concatenate([features, state_ref[:, first * width : (first + batch) * width]], axis=0)
        others = jnp.concatenate(
            [
                jnp.concatenate([ref[(y + d) * channels : (y + d + 1) * channels, :] for y in span], axis=1)
                for ref, d in ((before_ref, 0), (slope_ref, 1), (after_ref, 0), (hidden_ref, 0))
            ],
            axis=0,
        )
        part = dot_nt(features, others)
        total = part if total is None else total + part
    grad_head = total[3 * pitch : 3 * pitch + fields, 3 * channels :]
    stack = stack_ref[...]
    from_left = dot_nt(stack[:, :128], ends_left.astype(jnp.bfloat16))
    from_right = dot_nt(stack[:, 128:], ends_right.astype(jnp.bfloat16))
    middle = jnp.zeros((3 * pitch, channels), jnp.float32)
    total = total[: 3 * pitch, : 3 * channels] + jnp.concatenate([from_left, middle, from_right], axis=1)
    for i in range(3):
        moment_ref[i] = total[i * pitch + channels : i * pitch + channels + fields, :]
    taps = [total[i * pitch : i * pitch + channels, :] for i in range(3)]
    half = channels // 2
    last = [t[:, 2 * channels :] for t in taps]
    packed = [t[:, : 2 * channels] for t in taps]
    packed.append(jnp.concatenate(last[:2], axis=1))
    packed.append(jnp.concatenate([last[2][:half], last[2][half:]], axis=1))
    packed.append(jnp.concatenate([grad_head, jnp.zeros_like(grad_head)], axis=1))
    packed.append(jnp.zeros((8, 2 * channels), jnp.float32))
    packed = jnp.concatenate(packed, axis=0)
    cut = packed.shape[0] // 2
    odd = lax.rem(lax.axis_index("lon"), 2)
    packed_ref[odd] = packed[:cut]
    packed_ref[1 - odd] = packed[cut:]


def backward(arrived, prior, edges, stack, lift, act, forecast, readout, capacity, norm):
    fields, rows, width = forecast.shape
    channels = readout.shape[0]
    pitch = lift.shape[0]
    packed_rows = (3 * channels + channels + channels // 2 + fields + 8) // 2
    vmem = pl.BlockSpec(memory_space=pltpu.VMEM)
    return pl.pallas_call(
        functools.partial(backward_kernel, capacity, channels, norm),
        out_shape=(
            jax.ShapeDtypeStruct((fields, rows, width), jnp.bfloat16),
            jax.ShapeDtypeStruct((2, packed_rows, 2 * channels), jnp.float32),
            jax.ShapeDtypeStruct(((rows + 2) * channels, width), jnp.bfloat16),
            jax.ShapeDtypeStruct((3, fields, 3 * channels), jnp.float32),
        ),
        in_specs=[vmem] * 8,
        out_specs=[vmem] * 4,
        scratch_shapes=[
            pltpu.VMEM(((rows + 2) * pitch, width), jnp.bfloat16),
            pltpu.VMEM((rows * channels, width), jnp.bfloat16),
            pltpu.VMEM((rows * channels, rows * fields), jnp.bfloat16),
            pltpu.VMEM((fields, rows, width), jnp.float32),
            pltpu.VMEM((2 * fields, rows * width), jnp.bfloat16),
            pltpu.VMEM((rows * channels, width), jnp.bfloat16),
            pltpu.VMEM((rows * channels, width), jnp.bfloat16),
        ],
        compiler_params=pltpu.CompilerParams(vmem_limit_bytes=VMEM_LIMIT),
        cost_estimate=pl.CostEstimate(
            flops=2 * rows * width * 3 * channels * 3 * pitch,
            bytes_accessed=rows * width * channels * 8,
            transcendentals=0,
        ),
        name="backward",
    )(arrived, prior, edges, stack, lift, act, forecast, readout)


def lift_gradient_kernel(slope_ref, prior_ref, back_ref, contract_ref, moment_ref, out_ref, delta_ref):
    rows, fields, width = prior_ref.shape
    channels = contract_ref.shape[1]
    col = lax.broadcasted_iota(jnp.int32, (channels, width), 1)
    delta_ref[:channels, :] = jnp.zeros((channels, width), jnp.bfloat16)
    delta_ref[(rows - 1) * channels :, :] = jnp.zeros((channels, width), jnp.bfloat16)
    for y in range(1, rows - 1):
        parts = dot(back_ref[...], slope_ref[y * channels : (y + 3) * channels, :])
        grad = (
            parts[channels : 2 * channels]
            + pltpu.roll(parts[:channels], width - 1, 1)
            + pltpu.roll(parts[2 * channels :], 1, 1)
        )
        inside = (col > 0) & (col < width - 1)
        delta = jnp.where(inside, grad.astype(jnp.bfloat16).astype(jnp.float32) - grad, 0.0)
        delta_ref[y * channels : (y + 1) * channels, :] = delta.astype(jnp.bfloat16)
    grad_lift = jnp.zeros((fields, channels), jnp.float32)
    batch = 4
    for first in range(0, rows, batch):
        span = range(first, first + batch)
        states = jnp.concatenate([prior_ref[y] for y in span], axis=1)
        deltas = jnp.concatenate([delta_ref[y * channels : (y + 1) * channels, :] for y in span], axis=1)
        grad_lift += dot_nt(states, deltas)
    for i in range(3):
        rest = moment_ref[i]
        for _ in range(3):
            piece = rest.astype(jnp.bfloat16)
            rest = rest - piece.astype(jnp.float32)
            grad_lift += dot_nt(piece, contract_ref[i])
    out_ref[...] = jnp.concatenate([grad_lift, jnp.zeros_like(grad_lift)], axis=1)


def lift_gradient(slope, prior, back, contract, moment):
    rows, fields, width = prior.shape
    channels = contract.shape[1]
    vmem = pl.BlockSpec(memory_space=pltpu.VMEM)
    return pl.pallas_call(
        lift_gradient_kernel,
        out_shape=jax.ShapeDtypeStruct((fields, 2 * channels), jnp.float32),
        in_specs=[vmem] * 5,
        out_specs=vmem,
        scratch_shapes=[pltpu.VMEM((rows * channels, width), jnp.bfloat16)],
        compiler_params=pltpu.CompilerParams(vmem_limit_bytes=VMEM_LIMIT),
        cost_estimate=pl.CostEstimate(
            flops=2 * rows * width * 9 * channels * channels, bytes_accessed=slope.size * 2, transcendentals=0
        ),
        name="lift_gradient",
    )(slope, prior, back, contract, moment)


def unpack_kernel(channels, mine_ref, other_ref, kernel_ref, lift_ref, head_ref):
    odd = lax.rem(lax.axis_index("lon"), 2) == 1
    fields = lift_ref.shape[0]
    lift_ref[...] = (mine_ref[-fields:, :] + other_ref[-fields:, :])[:, :channels]
    mine, other = mine_ref[:-fields, :], other_ref[:-fields, :]
    packed = jnp.concatenate([jnp.where(odd, other, mine), jnp.where(odd, mine, other)], axis=0)
    half = channels // 2
    for i in range(3):
        block = packed[i * channels : (i + 1) * channels]
        kernel_ref[3 * i] = block[:, :channels]
        kernel_ref[3 * i + 1] = block[:, channels:]
    block = packed[3 * channels : 4 * channels]
    kernel_ref[2] = block[:, :channels]
    kernel_ref[5] = block[:, channels:]
    block = packed[4 * channels : 4 * channels + half]
    kernel_ref[8, :half] = block[:, :channels]
    kernel_ref[8, half:] = block[:, channels:]
    head_ref[...] = packed[4 * channels + half : 4 * channels + half + fields, :channels]


def unpack(mine, other, channels, fields):
    return pl.pallas_call(
        functools.partial(unpack_kernel, channels),
        out_shape=(
            jax.ShapeDtypeStruct((9, channels, channels), jnp.float32),
            jax.ShapeDtypeStruct((fields, channels), jnp.float32),
            jax.ShapeDtypeStruct((fields, channels), jnp.float32),
        ),
        compiler_params=pltpu.CompilerParams(vmem_limit_bytes=VMEM_LIMIT),
        name="unpack",
    )(mine, other)


def swap(x, axis, bit):
    return lax.ppermute(x, axis, [(i, i ^ bit) for i in range(lax.axis_size(axis))])


def sum_over(x, axis, low, high):
    if high // low == 4:
        a, b, c = (swap(x, axis, k * low) for k in (1, 2, 3))
        return (x + a) + (b + c)
    bit = low
    while bit < high:
        x = x + swap(x, axis, bit)
        bit *= 2
    return x


def pair_swap(even_sends, odd_sends, axis, periodic):
    count = lax.axis_size(axis)
    even = lax.rem(lax.axis_index(axis), 2) == 0
    inner = [(i, i ^ 1) for i in range(count)]
    outer = []
    for i in range(1, count, 2):
        if i + 1 < count or periodic:
            outer += [(i, (i + 1) % count), ((i + 1) % count, i)]
    got_inner = lax.ppermute(jnp.where(even, odd_sends, even_sends), axis, inner)
    got_outer = lax.ppermute(jnp.where(even, even_sends, odd_sends), axis, outer)
    return jnp.where(even, got_outer, got_inner), jnp.where(even, got_inner, got_outer)


def per_device(
    source,
    intersection_weight,
    dest_tile,
    dest_row,
    prior_state,
    lift_weight,
    kernel,
    readout_weights,
):
    face_count = lax.axis_size("face")
    lon_count = lax.axis_size("lon")
    devices = face_count * lon_count
    src_blocks, intersections = dest_tile.shape
    fields, rows, width = prior_state.shape
    channels = kernel.shape[1]
    capacity = max(2, 2 * src_blocks * intersections // devices)
    norm = 1.0 / math.sqrt(rows * face_count * width * lon_count)

    outgoing = regrid(source, intersection_weight, dest_tile, dest_row, devices, capacity)
    outgoing, prior_state, kernel, lift_weight, readout_weights = lax.optimization_barrier(
        (outgoing, prior_state, kernel, lift_weight, readout_weights)
    )
    arrived = lax.all_to_all(outgoing, ("face", "lon"), split_axis=0, concat_axis=0, tiled=True)
    arrived = arrived.reshape(devices, (capacity + 1) * fields, source.shape[2])

    prior = prior_state.transpose(1, 0, 2)
    top, bottom = pair_swap(prior[0], prior[rows - 1], "face", False)
    columns = [
        jnp.pad(
            jnp.concatenate([top[:, at : at + 1], prior_state[:, :, at], bottom[:, at : at + 1]], axis=1),
            ((0, 0), (0, 128 - rows - 2)),
        )
        for at in (0, width - 1)
    ]
    left, right = pair_swap(columns[0], columns[1], "lon", True)

    edges = jnp.stack([top, bottom])
    sides = jnp.concatenate([left, right], axis=1)
    part, lift, conv, back, contract = convolve(prior, edges, lift_weight, kernel)
    act, stack, forecast, estimate = finish(part, prior, sides, lift, conv, readout_weights)
    remapped, packed, slope, moment = backward(
        arrived, prior, edges, stack, lift, act, forecast, readout_weights, capacity, norm
    )
    part = packed[0] + swap(packed[1], "lon", 1)
    part = jnp.concatenate([part, lift_gradient(slope, prior, back, contract, moment)])
    part = sum_over(part, "face", 1, face_count)
    part = sum_over(part, "lon", 2, lon_count)
    grad_kernel, grad_lift, grad_head = unpack(part, swap(part, "lon", 1), channels, fields)
    return (
        remapped,
        estimate,
        grad_lift,
        grad_kernel,
        grad_head.T,
    )


def solution(mesh):
    return jax.shard_map(
        per_device,
        mesh=mesh,
        in_specs=(
            P(("face", "lon"), None, None),
            P(("face", "lon"), None, None, None),
            P(("face", "lon"), None),
            P(("face", "lon"), None),
            P(None, "face", "lon"),
            P(),
            P(),
            P(),
        ),
        out_specs=(P(None, "face", "lon"), P(None, "face", "lon"), P(), P(), P()),
        check_vma=False,
    )
```

```python
import functools
import math

import jax
import jax.numpy as jnp
from jax import lax
from jax.experimental import pallas as pl
from jax.experimental.pallas import tpu as pltpu
from jax.sharding import PartitionSpec as P

NT = (((1,), (1,)), ((), ()))
VMEM_LIMIT = 24 * 1024 * 1024
REGRID_VMEM = 60 * 1024 * 1024


def dot(a, b):
    return jnp.dot(a, b, preferred_element_type=jnp.float32)


def dot_nt(a, b):
    return lax.dot_general(a, b, NT, preferred_element_type=jnp.float32)


def sigmoid(x):
    return 1.0 / (1.0 + jnp.exp(-x))


def regrid_kernel(
    capacity,
    tile_hbm,
    row_hbm,
    src_hbm,
    wts_hbm,
    out_ref,
    tile_ref,
    row_ref,
    src_ref,
    wts_ref,
    count_ref,
    slot_ref,
    head_ref,
    sems,
):
    blocks, fields, width = src_ref.shape
    intersections = wts_ref.shape[1]
    devices = out_ref.shape[0]
    chunks = sems.shape[0] - 3
    chunk = blocks // chunks
    copies = [
        pltpu.make_async_copy(
            wts_hbm.at[pl.ds(i * chunk, chunk)], wts_ref.at[pl.ds(i * chunk, chunk)], sems.at[i]
        )
        for i in range(chunks)
    ]
    pairs = ((tile_hbm, tile_ref), (row_hbm, row_ref), (src_hbm, src_ref))
    first = [pltpu.make_async_copy(a, b, sems.at[chunks + i]) for i, (a, b) in enumerate(pairs)]
    for copy in first + copies:
        copy.start()
    head_ref[...] = jnp.full_like(head_ref, -1.0)
    for d in range(devices):
        count_ref[d] = 0
    for copy in first:
        copy.wait()
    slot_of_lane = lax.rem(lax.broadcasted_iota(jnp.int32, (1, width), 1), capacity)
    for s in range(blocks):
        for k in range(intersections):
            tile = tile_ref[k, s]
            slot = count_ref[tile]
            count_ref[tile] = slot + 1
            slot_ref[k, s] = slot
            label = row_ref[k, s].astype(jnp.float32)
            head_ref[pl.ds(tile, 1), :] = jnp.where(slot_of_lane == slot, label, head_ref[pl.ds(tile, 1), :])
    out_ref[...] = jnp.zeros_like(out_ref)
    for d in range(devices):
        out_ref[d, capacity] = jnp.broadcast_to(head_ref[d : d + 1, :], (fields, width)).astype(jnp.bfloat16)
    for i in range(chunks):
        copies[i].wait()
        for s in range(i * chunk, (i + 1) * chunk):
            block = src_ref[s]
            for pair in range(0, intersections, 2):
                both = range(pair, min(pair + 2, intersections))
                contrib = dot(block, jnp.concatenate([wts_ref[s, k] for k in both], axis=1)).astype(jnp.bfloat16)
                for k in both:
                    out_ref[tile_ref[k, s], slot_ref[k, s]] = contrib[:, (k - pair) * width : (k - pair + 1) * width]


def regrid(source, weights, dest_tile, dest_row, devices, capacity):
    blocks, fields, width = source.shape
    intersections = weights.shape[1]
    chunks = math.gcd(blocks, 4)
    vmem = pl.BlockSpec(memory_space=pltpu.VMEM)
    return pl.pallas_call(
        functools.partial(regrid_kernel, capacity),
        out_shape=jax.ShapeDtypeStruct((devices, capacity + 1, fields, width), jnp.bfloat16),
        in_specs=[pl.BlockSpec(memory_space=pl.ANY)] * 4,
        out_specs=vmem,
        scratch_shapes=[
            pltpu.SMEM((intersections, blocks), jnp.int32),
            pltpu.SMEM((intersections, blocks), jnp.int32),
            pltpu.VMEM(source.shape, jnp.bfloat16),
            pltpu.VMEM(weights.shape, jnp.bfloat16),
            pltpu.SMEM((devices,), jnp.int32),
            pltpu.SMEM((intersections, blocks), jnp.int32),
            pltpu.VMEM((devices, width), jnp.float32),
            pltpu.SemaphoreType.DMA((chunks + 3,)),
        ],
        compiler_params=pltpu.CompilerParams(vmem_limit_bytes=REGRID_VMEM),
        cost_estimate=pl.CostEstimate(
            flops=2 * weights.size * fields, bytes_accessed=2 * weights.size, transcendentals=0
        ),
        name="regrid",
    )(dest_tile.T, dest_row.T, source, weights)


def lift_rows(prior_ref, edge_ref, lift, feat_ref):
    rows = prior_ref.shape[0]
    pitch = lift.shape[0]
    for at in range(rows + 2):
        values = edge_ref[0] if at == 0 else edge_ref[1] if at == rows + 1 else prior_ref[at - 1]
        feat_ref[at * pitch : (at + 1) * pitch, :] = dot(lift, values).astype(jnp.bfloat16)


def convolve_kernel(
    prior_ref,
    edge_ref,
    lift_weight_ref,
    kernel_ref,
    act_ref,
    lift_ref,
    conv_ref,
    back_ref,
    contract_ref,
    feat_ref,
):
    rows, fields, width = prior_ref.shape
    channels = kernel_ref.shape[1]
    pitch = lift_ref.shape[0]

    taps = [kernel_ref[t].astype(jnp.float32) for t in range(9)]
    for i in range(3):
        back_ref[i * channels : (i + 1) * channels, :] = jnp.concatenate(
            [taps[6 + i], taps[3 + i], taps[i]], axis=1
        ).astype(jnp.bfloat16)
        contract_ref[i] = jnp.concatenate(taps[3 * i : 3 * i + 3], axis=1).astype(jnp.bfloat16)
    empty = jnp.zeros((pitch - channels, 3 * channels), jnp.float32)
    by_input = [piece for i in range(3) for piece in (jnp.concatenate(taps[3 * i : 3 * i + 3], axis=1), empty)]
    conv_ref[...] = jnp.concatenate(by_input, axis=0).T.astype(jnp.bfloat16)
    same = lax.broadcasted_iota(jnp.int32, (fields, pitch - channels), 0) == lax.broadcasted_iota(
        jnp.int32, (fields, pitch - channels), 1
    )
    lift = jnp.concatenate([lift_weight_ref[...].astype(jnp.float32), jnp.where(same, 1.0, 0.0)], axis=1)
    lift_ref[...] = lift.T.astype(jnp.bfloat16)

    lift_rows(prior_ref, edge_ref, lift_ref[...], feat_ref)
    lane = lax.broadcasted_iota(jnp.int32, (channels, width), 1)
    for y in range(rows):
        parts = dot(conv_ref[...], feat_ref[y * pitch : (y + 3) * pitch, :])
        left = jnp.where(lane == 0, 0.0, pltpu.roll(parts[:channels], 1, 1))
        right = jnp.where(lane == width - 1, 0.0, pltpu.roll(parts[2 * channels :], width - 1, 1))
        act_ref[y * channels : (y + 1) * channels, :] = parts[channels : 2 * channels] + left + right


def convolve(prior, edges, lift_weight, kernel):
    rows, fields, width = prior.shape
    channels = kernel.shape[1]
    pitch = channels + 16
    vmem = pl.BlockSpec(memory_space=pltpu.VMEM)
    return pl.pallas_call(
        convolve_kernel,
        out_shape=(
            jax.ShapeDtypeStruct((rows * channels, width), jnp.float32),
            jax.ShapeDtypeStruct((pitch, fields), jnp.bfloat16),
            jax.ShapeDtypeStruct((3 * channels, 3 * pitch), jnp.bfloat16),
            jax.ShapeDtypeStruct((3 * channels, 3 * channels), jnp.bfloat16),
            jax.ShapeDtypeStruct((3, channels, 3 * channels), jnp.bfloat16),
        ),
        in_specs=[vmem] * 4,
        out_specs=[vmem] * 5,
        scratch_shapes=[pltpu.VMEM(((rows + 2) * pitch, width), jnp.bfloat16)],
        compiler_params=pltpu.CompilerParams(vmem_limit_bytes=VMEM_LIMIT),
        cost_estimate=pl.CostEstimate(
            flops=2 * rows * width * 3 * channels * 3 * pitch,
            bytes_accessed=rows * width * channels * 8,
            transcendentals=0,
        ),
        name="convolve",
    )(prior, edges, lift_weight, kernel)


def finish_kernel(
    part_ref,
    prior_ref,
    side_ref,
    lift_ref,
    conv_ref,
    readout_ref,
    act_ref,
    stack_ref,
    forecast_ref,
    halo_ref,
    hidden_ref,
    by_row_ref,
):
    rows, fields, width = prior_ref.shape
    channels = readout_ref.shape[0]
    side = dot(lift_ref[...], side_ref[...])
    shifted = [side] + [pltpu.roll(side, 256 - i, 1) for i in (1, 2)]
    stack = jnp.concatenate(shifted, axis=0).astype(jnp.bfloat16)
    stack_ref[...] = stack
    halo_ref[:, :128] = dot(conv_ref[:channels, :], stack[:, :128])
    halo_ref[:, 128:] = dot(conv_ref[2 * channels :, :], stack[:, 128:])
    readout = readout_ref[...].astype(jnp.float32).T.astype(jnp.bfloat16)
    lane = lax.broadcasted_iota(jnp.int32, (channels, 128), 1)
    spread = [jnp.zeros((channels, 128), jnp.float32)] * (width // 128 - 1)
    for y in range(rows):
        here = slice(y * channels, (y + 1) * channels)
        from_left = jnp.where(lane == 0, pltpu.roll(halo_ref[:, :128], (128 - y) % 128, 1), 0.0)
        from_right = jnp.where(lane == 127, pltpu.roll(halo_ref[:, 128:], 127 - y, 1), 0.0)
        act = (
            part_ref[here, :]
            + jnp.concatenate([from_left] + spread, axis=1)
            + jnp.concatenate(spread + [from_right], axis=1)
        )
        act_ref[here, :] = act
        hidden_ref[here, :] = (act * sigmoid(act)).astype(jnp.bfloat16)
    for y in range(rows):
        increment = dot(readout, hidden_ref[y * channels : (y + 1) * channels, :])
        by_row_ref[y] = prior_ref[y].astype(jnp.float32) + increment
    forecast_ref[...] = jnp.transpose(by_row_ref[...], (1, 0, 2))


def finish(part, prior, sides, lift, conv, readout):
    rows, fields, width = prior.shape
    channels = readout.shape[0]
    vmem = pl.BlockSpec(memory_space=pltpu.VMEM)
    return pl.pallas_call(
        finish_kernel,
        out_shape=(
            jax.ShapeDtypeStruct(part.shape, jnp.float32),
            jax.ShapeDtypeStruct((conv.shape[1], 256), jnp.bfloat16),
            jax.ShapeDtypeStruct((fields, rows, width), jnp.float32),
        ),
        in_specs=[vmem] * 6,
        out_specs=[vmem] * 3,
        scratch_shapes=[
            pltpu.VMEM((channels, 256), jnp.float32),
            pltpu.VMEM((rows * channels, width), jnp.bfloat16),
            pltpu.VMEM((rows, fields, width), jnp.float32),
        ],
        input_output_aliases={0: 0},
        compiler_params=pltpu.CompilerParams(vmem_limit_bytes=VMEM_LIMIT),
        cost_estimate=pl.CostEstimate(
            flops=2 * rows * width * channels * fields,
            bytes_accessed=rows * width * channels * 8,
            transcendentals=rows * width * channels * 2,
        ),
        name="finish",
    )(part, prior, sides, lift, conv, readout)


def backward_kernel(
    capacity,
    channels,
    norm,
    arrived_ref,
    prior_ref,
    edge_ref,
    stack_ref,
    lift_ref,
    act_ref,
    forecast_ref,
    readout_ref,
    remapped_ref,
    packed_ref,
    slope_ref,
    moment_ref,
    feat_ref,
    hidden_ref,
    block_ref,
    misfit_ref,
    state_ref,
    before_ref,
    after_ref,
):
    fields, rows, width = remapped_ref.shape
    pitch = lift_ref.shape[0]
    devices = arrived_ref.shape[0]
    per_row = width // 128
    slots = devices * capacity

    lift_rows(prior_ref, edge_ref, lift_ref[...], feat_ref)
    slope_ref[:channels, :] = jnp.zeros((channels, width), jnp.bfloat16)
    slope_ref[(rows + 1) * channels :, :] = jnp.zeros((channels, width), jnp.bfloat16)
    depth = fields * rows
    lane = lax.broadcasted_iota(jnp.int32, (fields, depth), 1)
    spread = jnp.where(lane // rows == lax.broadcasted_iota(jnp.int32, (fields, depth), 0), 1.0, 0.0)
    spread = dot(readout_ref[...], spread.astype(jnp.bfloat16))
    lane = lax.broadcasted_iota(jnp.int32, (channels, depth), 1) % rows
    for y in range(rows):
        block_ref[y * channels : (y + 1) * channels, :] = jnp.where(lane == y, spread, 0.0).astype(jnp.bfloat16)

    labels = []
    for first in range(0, devices, 128 // capacity):
        lane = lax.broadcasted_iota(jnp.int32, (fields, 128), 1) // capacity
        label = None
        for d in range(min(devices, 128 // capacity)):
            mine = arrived_ref[first + d, capacity * fields : (capacity + 1) * fields, :].astype(jnp.float32)
            label = mine if label is None else jnp.where(lane == d, mine, label)
        labels.append(label)
    labels = jnp.concatenate(labels, axis=1).astype(jnp.int32)
    tile_blocks = rows * per_row
    labels = jnp.concatenate([labels] * (tile_blocks // fields), axis=0)
    at = lax.broadcasted_iota(jnp.int32, (tile_blocks, slots), 0)
    hits = jnp.where(labels == (at % rows) * per_row + at // rows, 1.0, 0.0).astype(jnp.bfloat16)
    data = arrived_ref[:, : capacity * fields, :].astype(jnp.float32).reshape(slots, fields, 128)
    data = jnp.transpose(data, (1, 0, 2)).astype(jnp.bfloat16)
    for f in range(0, fields, 2):
        picked = dot(hits, jnp.concatenate([data[f], data[f + 1]], axis=1))
        for g in range(2):
            target = picked[:, g * 128 : (g + 1) * 128].astype(jnp.bfloat16)
            target = jnp.concatenate([target[b * rows : (b + 1) * rows] for b in range(per_row)], axis=1)
            target = target.astype(jnp.float32)
            remapped_ref[f + g] = target
            misfit_ref[f + g] = (forecast_ref[f + g] - target) * norm
    by_row = jnp.transpose(misfit_ref[...], (1, 0, 2))
    empty = jnp.zeros((fields, width), jnp.float32)
    for y in range(rows):
        state_ref[:, y * width : (y + 1) * width] = jnp.concatenate([by_row[y], empty], axis=0).astype(jnp.bfloat16)

    col = lax.broadcasted_iota(jnp.int32, (channels, width), 1)
    lane = lax.broadcasted_iota(jnp.int32, (channels, 128), 1)
    ends_left = ends_right = jnp.zeros((channels, 128), jnp.float32)
    batch = 8
    misfits = misfit_ref[...].reshape(depth, width).astype(jnp.bfloat16)
    for first in range(0, rows, batch):
        latents = dot(block_ref[first * channels : (first + batch) * channels, :], misfits)
        for y in range(first, first + batch):
            here = slice(y * channels, (y + 1) * channels)
            act = act_ref[here, :]
            sig = sigmoid(act)
            hidden_ref[here, :] = (act * sig).astype(jnp.bfloat16)
            latent = latents[(y - first) * channels : (y - first + 1) * channels]
            slope = latent * sig * (1.0 + act * (1.0 - sig))
            slope_ref[(y + 1) * channels : (y + 2) * channels, :] = slope.astype(jnp.bfloat16)
            before = jnp.where(col == width - 1, 0.0, pltpu.roll(slope, width - 1, 1))
            before_ref[here, :] = before.astype(jnp.bfloat16)
            after_ref[here, :] = jnp.where(col == 0, 0.0, pltpu.roll(slope, 1, 1)).astype(jnp.bfloat16)
            ends_left += pltpu.roll(jnp.where(lane == 0, slope[:, :128], 0.0), y, 1)
            ends_right += pltpu.roll(jnp.where(lane == 127, slope[:, -128:], 0.0), y + 1, 1)

    total = None
    for first in range(0, rows, batch):
        span = range(first, first + batch)
        features = jnp.concatenate([feat_ref[y * pitch : (y + 3) * pitch, :] for y in span], axis=1)
        features = jnp.concatenate([features, state_ref[:, first * width : (first + batch) * width]], axis=0)
        others = jnp.concatenate(
            [
                jnp.concatenate([ref[(y + d) * channels : (y + d + 1) * channels, :] for y in span], axis=1)
                for ref, d in ((before_ref, 0), (slope_ref, 1), (after_ref, 0), (hidden_ref, 0))
            ],
            axis=0,
        )
        part = dot_nt(features, others)
        total = part if total is None else total + part
    grad_head = total[3 * pitch : 3 * pitch + fields, 3 * channels :]
    stack = stack_ref[...]
    from_left = dot_nt(stack[:, :128], ends_left.astype(jnp.bfloat16))
    from_right = dot_nt(stack[:, 128:], ends_right.astype(jnp.bfloat16))
    middle = jnp.zeros((3 * pitch, channels), jnp.float32)
    total = total[: 3 * pitch, : 3 * channels] + jnp.concatenate([from_left, middle, from_right], axis=1)
    for i in range(3):
        moment_ref[i] = total[i * pitch + channels : i * pitch + channels + fields, :]
    taps = [total[i * pitch : i * pitch + channels, :] for i in range(3)]
    half = channels // 2
    last = [t[:, 2 * channels :] for t in taps]
    packed = [t[:, : 2 * channels] for t in taps]
    packed.append(jnp.concatenate(last[:2], axis=1))
    packed.append(jnp.concatenate([last[2][:half], last[2][half:]], axis=1))
    packed.append(jnp.concatenate([grad_head, jnp.zeros_like(grad_head)], axis=1))
    packed.append(jnp.zeros((8, 2 * channels), jnp.float32))
    packed = jnp.concatenate(packed, axis=0)
    cut = packed.shape[0] // 2
    odd = lax.rem(lax.axis_index("lon"), 2)
    packed_ref[odd] = packed[:cut]
    packed_ref[1 - odd] = packed[cut:]


def backward(arrived, prior, edges, stack, lift, act, forecast, readout, capacity, norm):
    fields, rows, width = forecast.shape
    channels = readout.shape[0]
    pitch = lift.shape[0]
    packed_rows = (3 * channels + channels + channels // 2 + fields + 8) // 2
    vmem = pl.BlockSpec(memory_space=pltpu.VMEM)
    return pl.pallas_call(
        functools.partial(backward_kernel, capacity, channels, norm),
        out_shape=(
            jax.ShapeDtypeStruct((fields, rows, width), jnp.float32),
            jax.ShapeDtypeStruct((2, packed_rows, 2 * channels), jnp.float32),
            jax.ShapeDtypeStruct(((rows + 2) * channels, width), jnp.bfloat16),
            jax.ShapeDtypeStruct((3, fields, 3 * channels), jnp.float32),
        ),
        in_specs=[vmem] * 8,
        out_specs=[vmem] * 4,
        scratch_shapes=[
            pltpu.VMEM(((rows + 2) * pitch, width), jnp.bfloat16),
            pltpu.VMEM((rows * channels, width), jnp.bfloat16),
            pltpu.VMEM((rows * channels, rows * fields), jnp.bfloat16),
            pltpu.VMEM((fields, rows, width), jnp.float32),
            pltpu.VMEM((2 * fields, rows * width), jnp.bfloat16),
            pltpu.VMEM((rows * channels, width), jnp.bfloat16),
            pltpu.VMEM((rows * channels, width), jnp.bfloat16),
        ],
        compiler_params=pltpu.CompilerParams(vmem_limit_bytes=VMEM_LIMIT),
        cost_estimate=pl.CostEstimate(
            flops=2 * rows * width * 3 * channels * 3 * pitch,
            bytes_accessed=rows * width * channels * 8,
            transcendentals=0,
        ),
        name="backward",
    )(arrived, prior, edges, stack, lift, act, forecast, readout)


def lift_gradient_kernel(slope_ref, prior_ref, back_ref, contract_ref, moment_ref, out_ref, delta_ref):
    rows, fields, width = prior_ref.shape
    channels = contract_ref.shape[1]
    col = lax.broadcasted_iota(jnp.int32, (fields, width), 1)
    inside = (col > 0) & (col < width - 1)
    delta_ref[:channels, :] = jnp.zeros((channels, width), jnp.bfloat16)
    delta_ref[(rows - 1) * channels :, :] = jnp.zeros((channels, width), jnp.bfloat16)
    for y in range(1, rows - 1):
        parts = dot(back_ref[...], slope_ref[y * channels : (y + 3) * channels, :])
        grad = (
            parts[channels : 2 * channels]
            + pltpu.roll(parts[:channels], width - 1, 1)
            + pltpu.roll(parts[2 * channels :], 1, 1)
        )
        delta = grad.astype(jnp.bfloat16).astype(jnp.float32) - grad
        delta_ref[y * channels : (y + 1) * channels, :] = delta.astype(jnp.bfloat16)
    grad_lift = jnp.zeros((fields, channels), jnp.float32)
    batch = 4
    for first in range(0, rows, batch):
        span = range(first, first + batch)
        states = [jnp.where(inside, prior_ref[y].astype(jnp.float32), 0.0).astype(jnp.bfloat16) for y in span]
        states = jnp.concatenate(states, axis=1)
        deltas = jnp.concatenate([delta_ref[y * channels : (y + 1) * channels, :] for y in span], axis=1)
        grad_lift += dot_nt(states, deltas)
    for i in range(3):
        rest = moment_ref[i]
        for _ in range(3):
            piece = rest.astype(jnp.bfloat16)
            rest = rest - piece.astype(jnp.float32)
            grad_lift += dot_nt(piece, contract_ref[i])
    out_ref[...] = jnp.concatenate([grad_lift, jnp.zeros_like(grad_lift)], axis=1)


def lift_gradient(slope, prior, back, contract, moment):
    rows, fields, width = prior.shape
    channels = contract.shape[1]
    vmem = pl.BlockSpec(memory_space=pltpu.VMEM)
    return pl.pallas_call(
        lift_gradient_kernel,
        out_shape=jax.ShapeDtypeStruct((fields, 2 * channels), jnp.float32),
        in_specs=[vmem] * 5,
        out_specs=vmem,
        scratch_shapes=[pltpu.VMEM((rows * channels, width), jnp.bfloat16)],
        compiler_params=pltpu.CompilerParams(vmem_limit_bytes=VMEM_LIMIT),
        cost_estimate=pl.CostEstimate(
            flops=2 * rows * width * 9 * channels * channels, bytes_accessed=slope.size * 2, transcendentals=0
        ),
        name="lift_gradient",
    )(slope, prior, back, contract, moment)


def unpack_kernel(channels, mine_ref, other_ref, kernel_ref, lift_ref, head_ref):
    odd = lax.rem(lax.axis_index("lon"), 2) == 1
    fields = lift_ref.shape[0]
    lift_ref[...] = (mine_ref[-fields:, :] + other_ref[-fields:, :])[:, :channels]
    mine, other = mine_ref[:-fields, :], other_ref[:-fields, :]
    packed = jnp.concatenate([jnp.where(odd, other, mine), jnp.where(odd, mine, other)], axis=0)
    half = channels // 2
    for i in range(3):
        block = packed[i * channels : (i + 1) * channels]
        kernel_ref[3 * i] = block[:, :channels]
        kernel_ref[3 * i + 1] = block[:, channels:]
    block = packed[3 * channels : 4 * channels]
    kernel_ref[2] = block[:, :channels]
    kernel_ref[5] = block[:, channels:]
    block = packed[4 * channels : 4 * channels + half]
    kernel_ref[8, :half] = block[:, :channels]
    kernel_ref[8, half:] = block[:, channels:]
    head_ref[...] = packed[4 * channels + half : 4 * channels + half + fields, :channels]


def unpack(mine, other, channels, fields):
    return pl.pallas_call(
        functools.partial(unpack_kernel, channels),
        out_shape=(
            jax.ShapeDtypeStruct((9, channels, channels), jnp.float32),
            jax.ShapeDtypeStruct((fields, channels), jnp.float32),
            jax.ShapeDtypeStruct((fields, channels), jnp.float32),
        ),
        compiler_params=pltpu.CompilerParams(vmem_limit_bytes=VMEM_LIMIT),
        name="unpack",
    )(mine, other)


def swap(x, axis, bit):
    return lax.ppermute(x, axis, [(i, i ^ bit) for i in range(lax.axis_size(axis))])


def sum_over(x, axis, low, high):
    if high // low == 4:
        a, b, c = (swap(x, axis, k * low) for k in (1, 2, 3))
        return (x + a) + (b + c)
    bit = low
    while bit < high:
        x = x + swap(x, axis, bit)
        bit *= 2
    return x


def pair_swap(even_sends, odd_sends, axis, periodic):
    count = lax.axis_size(axis)
    even = lax.rem(lax.axis_index(axis), 2) == 0
    inner = [(i, i ^ 1) for i in range(count)]
    outer = []
    for i in range(1, count, 2):
        if i + 1 < count or periodic:
            outer += [(i, (i + 1) % count), ((i + 1) % count, i)]
    got_inner = lax.ppermute(jnp.where(even, odd_sends, even_sends), axis, inner)
    got_outer = lax.ppermute(jnp.where(even, even_sends, odd_sends), axis, outer)
    return jnp.where(even, got_outer, got_inner), jnp.where(even, got_inner, got_outer)


def per_device(
    source,
    intersection_weight,
    dest_tile,
    dest_row,
    prior_state,
    lift_weight,
    kernel,
    readout_weights,
):
    face_count = lax.axis_size("face")
    lon_count = lax.axis_size("lon")
    devices = face_count * lon_count
    src_blocks, intersections = dest_tile.shape
    fields, rows, width = prior_state.shape
    channels = kernel.shape[1]
    capacity = max(2, 2 * src_blocks * intersections // devices)
    norm = 1.0 / math.sqrt(rows * face_count * width * lon_count)

    outgoing = regrid(source, intersection_weight, dest_tile, dest_row, devices, capacity)
    outgoing, prior_state, kernel, lift_weight, readout_weights = lax.optimization_barrier(
        (outgoing, prior_state, kernel, lift_weight, readout_weights)
    )
    arrived = lax.all_to_all(outgoing, ("face", "lon"), split_axis=0, concat_axis=0, tiled=True)
    arrived = arrived.reshape(devices, (capacity + 1) * fields, source.shape[2])

    prior = prior_state.transpose(1, 0, 2)
    top, bottom = pair_swap(prior[0], prior[rows - 1], "face", False)
    columns = [
        jnp.pad(
            jnp.concatenate([top[:, at : at + 1], prior_state[:, :, at], bottom[:, at : at + 1]], axis=1),
            ((0, 0), (0, 128 - rows - 2)),
        )
        for at in (0, width - 1)
    ]
    left, right = pair_swap(columns[0], columns[1], "lon", True)

    edges = jnp.stack([top, bottom])
    sides = jnp.concatenate([left, right], axis=1)
    part, lift, conv, back, contract = convolve(prior, edges, lift_weight, kernel)
    act, stack, forecast = finish(part, prior, sides, lift, conv, readout_weights)
    remapped, packed, slope, moment = backward(
        arrived, prior, edges, stack, lift, act, forecast, readout_weights, capacity, norm
    )
    part = packed[0] + swap(packed[1], "lon", 1)
    part = jnp.concatenate([part, lift_gradient(slope, prior, back, contract, moment)])
    part = sum_over(part, "face", 1, face_count)
    part = sum_over(part, "lon", 2, lon_count)
    grad_kernel, grad_lift, grad_head = unpack(part, swap(part, "lon", 1), channels, fields)
    return (
        remapped.astype(jnp.bfloat16),
        forecast.astype(jnp.bfloat16),
        grad_lift,
        grad_kernel,
        grad_head.T,
    )


def solution(mesh):
    return jax.shard_map(
        per_device,
        mesh=mesh,
        in_specs=(
            P(("face", "lon"), None, None),
            P(("face", "lon"), None, None, None),
            P(("face", "lon"), None),
            P(("face", "lon"), None),
            P(None, "face", "lon"),
            P(),
            P(),
            P(),
        ),
        out_specs=(P(None, "face", "lon"), P(None, "face", "lon"), P(), P(), P()),
        check_vma=False,
    )
```

```python
import functools
import math

import jax
import jax.numpy as jnp
from jax import lax
from jax.experimental import pallas as pl
from jax.experimental.pallas import tpu as pltpu
from jax.sharding import PartitionSpec as P

NT = (((1,), (1,)), ((), ()))
VMEM_LIMIT = 24 * 1024 * 1024
REGRID_VMEM = 60 * 1024 * 1024


def dot(a, b):
    return jnp.dot(a, b, preferred_element_type=jnp.float32)


def dot_nt(a, b):
    return lax.dot_general(a, b, NT, preferred_element_type=jnp.float32)


def sigmoid(x):
    return 1.0 / (1.0 + jnp.exp(-x))


def regrid_kernel(
    capacity,
    tile_hbm,
    row_hbm,
    src_hbm,
    wts_hbm,
    out_ref,
    tile_ref,
    row_ref,
    src_ref,
    wts_ref,
    count_ref,
    slot_ref,
    head_ref,
    sems,
):
    blocks, fields, width = src_ref.shape
    intersections = wts_ref.shape[1]
    devices = out_ref.shape[0]
    chunks = sems.shape[0] - 3
    chunk = blocks // chunks
    copies = [
        pltpu.make_async_copy(
            wts_hbm.at[pl.ds(i * chunk, chunk)], wts_ref.at[pl.ds(i * chunk, chunk)], sems.at[i]
        )
        for i in range(chunks)
    ]
    pairs = ((tile_hbm, tile_ref), (row_hbm, row_ref), (src_hbm, src_ref))
    first = [pltpu.make_async_copy(a, b, sems.at[chunks + i]) for i, (a, b) in enumerate(pairs)]
    for copy in first + copies:
        copy.start()
    head_ref[...] = jnp.full_like(head_ref, -1.0)
    for d in range(devices):
        count_ref[d] = 0
    for copy in first:
        copy.wait()
    slot_of_lane = lax.rem(lax.broadcasted_iota(jnp.int32, (1, width), 1), capacity)
    for s in range(blocks):
        for k in range(intersections):
            tile = tile_ref[k, s]
            slot = count_ref[tile]
            count_ref[tile] = slot + 1
            slot_ref[k, s] = slot
            label = row_ref[k, s].astype(jnp.float32)
            head_ref[pl.ds(tile, 1), :] = jnp.where(slot_of_lane == slot, label, head_ref[pl.ds(tile, 1), :])
    out_ref[...] = jnp.zeros_like(out_ref)
    for d in range(devices):
        out_ref[d, capacity] = jnp.broadcast_to(head_ref[d : d + 1, :], (fields, width)).astype(jnp.bfloat16)
    for i in range(chunks):
        copies[i].wait()
        for s in range(i * chunk, (i + 1) * chunk):
            block = src_ref[s]
            for pair in range(0, intersections, 2):
                both = range(pair, min(pair + 2, intersections))
                contrib = dot(block, jnp.concatenate([wts_ref[s, k] for k in both], axis=1)).astype(jnp.bfloat16)
                for k in both:
                    out_ref[tile_ref[k, s], slot_ref[k, s]] = contrib[:, (k - pair) * width : (k - pair + 1) * width]


def regrid(source, weights, dest_tile, dest_row, devices, capacity):
    blocks, fields, width = source.shape
    intersections = weights.shape[1]
    chunks = math.gcd(blocks, 4)
    vmem = pl.BlockSpec(memory_space=pltpu.VMEM)
    return pl.pallas_call(
        functools.partial(regrid_kernel, capacity),
        out_shape=jax.ShapeDtypeStruct((devices, capacity + 1, fields, width), jnp.bfloat16),
        in_specs=[pl.BlockSpec(memory_space=pl.ANY)] * 4,
        out_specs=vmem,
        scratch_shapes=[
            pltpu.SMEM((intersections, blocks), jnp.int32),
            pltpu.SMEM((intersections, blocks), jnp.int32),
            pltpu.VMEM(source.shape, jnp.bfloat16),
            pltpu.VMEM(weights.shape, jnp.bfloat16),
            pltpu.SMEM((devices,), jnp.int32),
            pltpu.SMEM((intersections, blocks), jnp.int32),
            pltpu.VMEM((devices, width), jnp.float32),
            pltpu.SemaphoreType.DMA((chunks + 3,)),
        ],
        compiler_params=pltpu.CompilerParams(vmem_limit_bytes=REGRID_VMEM),
        cost_estimate=pl.CostEstimate(
            flops=2 * weights.size * fields, bytes_accessed=2 * weights.size, transcendentals=0
        ),
        name="regrid",
    )(dest_tile.T, dest_row.T, source, weights)


def lift_rows(prior_ref, edge_ref, lift, feat_ref):
    rows = prior_ref.shape[0]
    pitch = lift.shape[0]
    for at in range(rows + 2):
        values = edge_ref[0] if at == 0 else edge_ref[1] if at == rows + 1 else prior_ref[at - 1]
        feat_ref[at * pitch : (at + 1) * pitch, :] = dot(lift, values).astype(jnp.bfloat16)


def convolve_kernel(
    prior_ref,
    edge_ref,
    lift_weight_ref,
    kernel_ref,
    act_ref,
    lift_ref,
    conv_ref,
    back_ref,
    contract_ref,
    feat_ref,
):
    rows, fields, width = prior_ref.shape
    channels = kernel_ref.shape[1]
    pitch = lift_ref.shape[0]

    taps = [kernel_ref[t].astype(jnp.float32) for t in range(9)]
    for i in range(3):
        back_ref[i * channels : (i + 1) * channels, :] = jnp.concatenate(
            [taps[6 + i], taps[3 + i], taps[i]], axis=1
        ).astype(jnp.bfloat16)
        contract_ref[i] = jnp.concatenate(taps[3 * i : 3 * i + 3], axis=1).astype(jnp.bfloat16)
    empty = jnp.zeros((pitch - channels, 3 * channels), jnp.float32)
    by_input = [piece for i in range(3) for piece in (jnp.concatenate(taps[3 * i : 3 * i + 3], axis=1), empty)]
    conv_ref[...] = jnp.concatenate(by_input, axis=0).T.astype(jnp.bfloat16)
    same = lax.broadcasted_iota(jnp.int32, (fields, pitch - channels), 0) == lax.broadcasted_iota(
        jnp.int32, (fields, pitch - channels), 1
    )
    lift = jnp.concatenate([lift_weight_ref[...].astype(jnp.float32), jnp.where(same, 1.0, 0.0)], axis=1)
    lift_ref[...] = lift.T.astype(jnp.bfloat16)

    lift_rows(prior_ref, edge_ref, lift_ref[...], feat_ref)
    lane = lax.broadcasted_iota(jnp.int32, (channels, width), 1)
    for y in range(rows):
        parts = dot(conv_ref[...], feat_ref[y * pitch : (y + 3) * pitch, :])
        left = jnp.where(lane == 0, 0.0, pltpu.roll(parts[:channels], 1, 1))
        right = jnp.where(lane == width - 1, 0.0, pltpu.roll(parts[2 * channels :], width - 1, 1))
        act_ref[y * channels : (y + 1) * channels, :] = parts[channels : 2 * channels] + left + right


def convolve(prior, edges, lift_weight, kernel):
    rows, fields, width = prior.shape
    channels = kernel.shape[1]
    pitch = channels + 16
    vmem = pl.BlockSpec(memory_space=pltpu.VMEM)
    return pl.pallas_call(
        convolve_kernel,
        out_shape=(
            jax.ShapeDtypeStruct((rows * channels, width), jnp.float32),
            jax.ShapeDtypeStruct((pitch, fields), jnp.bfloat16),
            jax.ShapeDtypeStruct((3 * channels, 3 * pitch), jnp.bfloat16),
            jax.ShapeDtypeStruct((3 * channels, 3 * channels), jnp.bfloat16),
            jax.ShapeDtypeStruct((3, channels, 3 * channels), jnp.bfloat16),
        ),
        in_specs=[vmem] * 4,
        out_specs=[vmem] * 5,
        scratch_shapes=[pltpu.VMEM(((rows + 2) * pitch, width), jnp.bfloat16)],
        compiler_params=pltpu.CompilerParams(vmem_limit_bytes=VMEM_LIMIT),
        cost_estimate=pl.CostEstimate(
            flops=2 * rows * width * 3 * channels * 3 * pitch,
            bytes_accessed=rows * width * channels * 8,
            transcendentals=0,
        ),
        name="convolve",
    )(prior, edges, lift_weight, kernel)


def finish_kernel(
    part_ref,
    prior_ref,
    side_ref,
    lift_ref,
    conv_ref,
    readout_ref,
    act_ref,
    stack_ref,
    forecast_ref,
    halo_ref,
    hidden_ref,
    by_row_ref,
):
    rows, fields, width = prior_ref.shape
    channels = readout_ref.shape[0]
    side = dot(lift_ref[...], side_ref[...])
    shifted = [side] + [pltpu.roll(side, 256 - i, 1) for i in (1, 2)]
    stack = jnp.concatenate(shifted, axis=0).astype(jnp.bfloat16)
    stack_ref[...] = stack
    halo_ref[:, :128] = dot(conv_ref[:channels, :], stack[:, :128])
    halo_ref[:, 128:] = dot(conv_ref[2 * channels :, :], stack[:, 128:])
    readout = readout_ref[...].astype(jnp.float32).T.astype(jnp.bfloat16)
    lane = lax.broadcasted_iota(jnp.int32, (channels, 128), 1)
    spread = [jnp.zeros((channels, 128), jnp.float32)] * (width // 128 - 1)
    for y in range(rows):
        here = slice(y * channels, (y + 1) * channels)
        from_left = jnp.where(lane == 0, pltpu.roll(halo_ref[:, :128], (128 - y) % 128, 1), 0.0)
        from_right = jnp.where(lane == 127, pltpu.roll(halo_ref[:, 128:], 127 - y, 1), 0.0)
        act = (
            part_ref[here, :]
            + jnp.concatenate([from_left] + spread, axis=1)
            + jnp.concatenate(spread + [from_right], axis=1)
        )
        act_ref[here, :] = act
        hidden_ref[here, :] = (act * sigmoid(act)).astype(jnp.bfloat16)
    for y in range(rows):
        increment = dot(readout, hidden_ref[y * channels : (y + 1) * channels, :])
        by_row_ref[y] = prior_ref[y].astype(jnp.float32) + increment
    forecast_ref[...] = jnp.transpose(by_row_ref[...], (1, 0, 2))


def finish(part, prior, sides, lift, conv, readout):
    rows, fields, width = prior.shape
    channels = readout.shape[0]
    vmem = pl.BlockSpec(memory_space=pltpu.VMEM)
    return pl.pallas_call(
        finish_kernel,
        out_shape=(
            jax.ShapeDtypeStruct(part.shape, jnp.float32),
            jax.ShapeDtypeStruct((conv.shape[1], 256), jnp.bfloat16),
            jax.ShapeDtypeStruct((fields, rows, width), jnp.float32),
        ),
        in_specs=[vmem] * 6,
        out_specs=[vmem] * 3,
        scratch_shapes=[
            pltpu.VMEM((channels, 256), jnp.float32),
            pltpu.VMEM((rows * channels, width), jnp.bfloat16),
            pltpu.VMEM((rows, fields, width), jnp.float32),
        ],
        input_output_aliases={0: 0},
        compiler_params=pltpu.CompilerParams(vmem_limit_bytes=VMEM_LIMIT),
        cost_estimate=pl.CostEstimate(
            flops=2 * rows * width * channels * fields,
            bytes_accessed=rows * width * channels * 8,
            transcendentals=rows * width * channels * 2,
        ),
        name="finish",
    )(part, prior, sides, lift, conv, readout)


def backward_kernel(
    capacity,
    channels,
    norm,
    arrived_ref,
    prior_ref,
    edge_ref,
    stack_ref,
    lift_ref,
    act_ref,
    forecast_ref,
    readout_ref,
    remapped_ref,
    packed_ref,
    slope_ref,
    moment_ref,
    feat_ref,
    hidden_ref,
    block_ref,
    misfit_ref,
    state_ref,
    before_ref,
    after_ref,
):
    fields, rows, width = remapped_ref.shape
    pitch = lift_ref.shape[0]
    devices = arrived_ref.shape[0]
    per_row = width // 128
    slots = devices * capacity

    lift_rows(prior_ref, edge_ref, lift_ref[...], feat_ref)
    slope_ref[:channels, :] = jnp.zeros((channels, width), jnp.bfloat16)
    slope_ref[(rows + 1) * channels :, :] = jnp.zeros((channels, width), jnp.bfloat16)
    depth = fields * rows
    lane = lax.broadcasted_iota(jnp.int32, (fields, depth), 1)
    spread = jnp.where(lane // rows == lax.broadcasted_iota(jnp.int32, (fields, depth), 0), 1.0, 0.0)
    spread = dot(readout_ref[...], spread.astype(jnp.bfloat16))
    lane = lax.broadcasted_iota(jnp.int32, (channels, depth), 1) % rows
    for y in range(rows):
        block_ref[y * channels : (y + 1) * channels, :] = jnp.where(lane == y, spread, 0.0).astype(jnp.bfloat16)

    labels = []
    for first in range(0, devices, 128 // capacity):
        lane = lax.broadcasted_iota(jnp.int32, (fields, 128), 1) // capacity
        label = None
        for d in range(min(devices, 128 // capacity)):
            mine = arrived_ref[first + d, capacity * fields : (capacity + 1) * fields, :].astype(jnp.float32)
            label = mine if label is None else jnp.where(lane == d, mine, label)
        labels.append(label)
    labels = jnp.concatenate(labels, axis=1).astype(jnp.int32)
    tile_blocks = rows * per_row
    labels = jnp.concatenate([labels] * (tile_blocks // fields), axis=0)
    at = lax.broadcasted_iota(jnp.int32, (tile_blocks, slots), 0)
    hits = jnp.where(labels == (at % rows) * per_row + at // rows, 1.0, 0.0).astype(jnp.bfloat16)
    data = arrived_ref[:, : capacity * fields, :].astype(jnp.float32).reshape(slots, fields, 128)
    data = jnp.transpose(data, (1, 0, 2)).astype(jnp.bfloat16)
    for f in range(0, fields, 2):
        picked = dot(hits, jnp.concatenate([data[f], data[f + 1]], axis=1))
        for g in range(2):
            target = picked[:, g * 128 : (g + 1) * 128].astype(jnp.bfloat16)
            target = jnp.concatenate([target[b * rows : (b + 1) * rows] for b in range(per_row)], axis=1)
            target = target.astype(jnp.float32)
            remapped_ref[f + g] = target
            misfit_ref[f + g] = (forecast_ref[f + g] - target) * norm
    by_row = jnp.transpose(misfit_ref[...], (1, 0, 2))
    empty = jnp.zeros((fields, width), jnp.float32)
    for y in range(rows):
        state_ref[:, y * width : (y + 1) * width] = jnp.concatenate([by_row[y], empty], axis=0).astype(jnp.bfloat16)

    col = lax.broadcasted_iota(jnp.int32, (channels, width), 1)
    lane = lax.broadcasted_iota(jnp.int32, (channels, 128), 1)
    ends_left = ends_right = jnp.zeros((channels, 128), jnp.float32)
    batch = 8
    misfits = misfit_ref[...].reshape(depth, width).astype(jnp.bfloat16)
    for first in range(0, rows, batch):
        latents = dot(block_ref[first * channels : (first + batch) * channels, :], misfits)
        for y in range(first, first + batch):
            here = slice(y * channels, (y + 1) * channels)
            act = act_ref[here, :]
            sig = sigmoid(act)
            hidden_ref[here, :] = (act * sig).astype(jnp.bfloat16)
            latent = latents[(y - first) * channels : (y - first + 1) * channels]
            slope = latent * sig * (1.0 + act * (1.0 - sig))
            slope_ref[(y + 1) * channels : (y + 2) * channels, :] = slope.astype(jnp.bfloat16)
            before = jnp.where(col == width - 1, 0.0, pltpu.roll(slope, width - 1, 1))
            before_ref[here, :] = before.astype(jnp.bfloat16)
            after_ref[here, :] = jnp.where(col == 0, 0.0, pltpu.roll(slope, 1, 1)).astype(jnp.bfloat16)
            ends_left += pltpu.roll(jnp.where(lane == 0, slope[:, :128], 0.0), y, 1)
            ends_right += pltpu.roll(jnp.where(lane == 127, slope[:, -128:], 0.0), y + 1, 1)

    total = None
    for first in range(0, rows, batch):
        span = range(first, first + batch)
        features = jnp.concatenate([feat_ref[y * pitch : (y + 3) * pitch, :] for y in span], axis=1)
        features = jnp.concatenate([features, state_ref[:, first * width : (first + batch) * width]], axis=0)
        others = jnp.concatenate(
            [
                jnp.concatenate([ref[(y + d) * channels : (y + d + 1) * channels, :] for y in span], axis=1)
                for ref, d in ((before_ref, 0), (slope_ref, 1), (after_ref, 0), (hidden_ref, 0))
            ],
            axis=0,
        )
        part = dot_nt(features, others)
        total = part if total is None else total + part
    grad_head = total[3 * pitch : 3 * pitch + fields, 3 * channels :]
    stack = stack_ref[...]
    from_left = dot_nt(stack[:, :128], ends_left.astype(jnp.bfloat16))
    from_right = dot_nt(stack[:, 128:], ends_right.astype(jnp.bfloat16))
    middle = jnp.zeros((3 * pitch, channels), jnp.float32)
    total = total[: 3 * pitch, : 3 * channels] + jnp.concatenate([from_left, middle, from_right], axis=1)
    for i in range(3):
        moment_ref[i] = total[i * pitch + channels : i * pitch + channels + fields, :]
    taps = [total[i * pitch : i * pitch + channels, :] for i in range(3)]
    half = channels // 2
    last = [t[:, 2 * channels :] for t in taps]
    packed = [t[:, : 2 * channels] for t in taps]
    packed.append(jnp.concatenate(last[:2], axis=1))
    packed.append(jnp.concatenate([last[2][:half], last[2][half:]], axis=1))
    packed = jnp.concatenate(packed, axis=0)
    cut = packed.shape[0] // 2
    head = jnp.concatenate([grad_head, jnp.zeros_like(grad_head)], axis=1)
    odd = lax.rem(lax.axis_index("lon"), 2)
    packed_ref[odd] = jnp.concatenate([packed[:cut], head], axis=0)
    packed_ref[1 - odd] = jnp.concatenate([packed[cut:], jnp.zeros_like(head)], axis=0)


def backward(arrived, prior, edges, stack, lift, act, forecast, readout, capacity, norm):
    fields, rows, width = forecast.shape
    channels = readout.shape[0]
    pitch = lift.shape[0]
    packed_rows = (3 * channels + channels + channels // 2) // 2 + fields
    vmem = pl.BlockSpec(memory_space=pltpu.VMEM)
    return pl.pallas_call(
        functools.partial(backward_kernel, capacity, channels, norm),
        out_shape=(
            jax.ShapeDtypeStruct((fields, rows, width), jnp.float32),
            jax.ShapeDtypeStruct((2, packed_rows, 2 * channels), jnp.float32),
            jax.ShapeDtypeStruct(((rows + 2) * channels, width), jnp.bfloat16),
            jax.ShapeDtypeStruct((3, fields, 3 * channels), jnp.float32),
        ),
        in_specs=[vmem] * 8,
        out_specs=[vmem] * 4,
        scratch_shapes=[
            pltpu.VMEM(((rows + 2) * pitch, width), jnp.bfloat16),
            pltpu.VMEM((rows * channels, width), jnp.bfloat16),
            pltpu.VMEM((rows * channels, rows * fields), jnp.bfloat16),
            pltpu.VMEM((fields, rows, width), jnp.float32),
            pltpu.VMEM((2 * fields, rows * width), jnp.bfloat16),
            pltpu.VMEM((rows * channels, width), jnp.bfloat16),
            pltpu.VMEM((rows * channels, width), jnp.bfloat16),
        ],
        compiler_params=pltpu.CompilerParams(vmem_limit_bytes=VMEM_LIMIT),
        cost_estimate=pl.CostEstimate(
            flops=2 * rows * width * 3 * channels * 3 * pitch,
            bytes_accessed=rows * width * channels * 8,
            transcendentals=0,
        ),
        name="backward",
    )(arrived, prior, edges, stack, lift, act, forecast, readout)


def lift_gradient_kernel(slope_ref, prior_ref, back_ref, contract_ref, moment_ref, out_ref, delta_ref):
    rows, fields, width = prior_ref.shape
    channels = contract_ref.shape[1]
    col = lax.broadcasted_iota(jnp.int32, (fields, width), 1)
    inside = (col > 0) & (col < width - 1)
    delta_ref[:channels, :] = jnp.zeros((channels, width), jnp.bfloat16)
    delta_ref[(rows - 1) * channels :, :] = jnp.zeros((channels, width), jnp.bfloat16)
    for y in range(1, rows - 1):
        parts = dot(back_ref[...], slope_ref[y * channels : (y + 3) * channels, :])
        grad = (
            parts[channels : 2 * channels]
            + pltpu.roll(parts[:channels], width - 1, 1)
            + pltpu.roll(parts[2 * channels :], 1, 1)
        )
        delta = grad.astype(jnp.bfloat16).astype(jnp.float32) - grad
        delta_ref[y * channels : (y + 1) * channels, :] = delta.astype(jnp.bfloat16)
    crossed = jnp.zeros((channels, fields), jnp.float32)
    batch = 4
    for first in range(0, rows, batch):
        span = range(first, first + batch)
        states = [jnp.where(inside, prior_ref[y].astype(jnp.float32), 0.0).astype(jnp.bfloat16) for y in span]
        states = jnp.concatenate(states, axis=1)
        deltas = jnp.concatenate([delta_ref[y * channels : (y + 1) * channels, :] for y in span], axis=1)
        crossed += dot_nt(deltas, states)
    grad_lift = crossed.T
    for i in range(3):
        rest, pieces = moment_ref[i], []
        for _ in range(3):
            pieces.append(rest.astype(jnp.bfloat16).astype(jnp.float32))
            rest = rest - pieces[-1]
        part = dot_nt(jnp.concatenate(pieces, axis=0).astype(jnp.bfloat16), contract_ref[i])
        grad_lift += part[:fields] + part[fields : 2 * fields] + part[2 * fields :]
    out_ref[...] = jnp.zeros_like(out_ref)
    out_ref[-fields:, channels:] = grad_lift


def lift_gradient(slope, prior, back, contract, moment, packed_rows):
    rows, fields, width = prior.shape
    channels = contract.shape[1]
    vmem = pl.BlockSpec(memory_space=pltpu.VMEM)
    return pl.pallas_call(
        lift_gradient_kernel,
        out_shape=jax.ShapeDtypeStruct((packed_rows, 2 * channels), jnp.float32),
        in_specs=[vmem] * 5,
        out_specs=vmem,
        scratch_shapes=[pltpu.VMEM((rows * channels, width), jnp.bfloat16)],
        compiler_params=pltpu.CompilerParams(vmem_limit_bytes=VMEM_LIMIT),
        cost_estimate=pl.CostEstimate(
            flops=2 * rows * width * 9 * channels * channels, bytes_accessed=slope.size * 2, transcendentals=0
        ),
        name="lift_gradient",
    )(slope, prior, back, contract, moment)


def unpack_kernel(channels, mine_ref, other_ref, kernel_ref, lift_ref, head_ref):
    odd = lax.rem(lax.axis_index("lon"), 2) == 1
    fields = lift_ref.shape[0]
    mine, other = mine_ref[-fields:, :], other_ref[-fields:, :]
    lift_ref[...] = (mine + other)[:, channels:]
    head_ref[...] = jnp.where(odd, other, mine)[:, :channels]
    mine, other = mine_ref[:-fields, :], other_ref[:-fields, :]
    packed = jnp.concatenate([jnp.where(odd, other, mine), jnp.where(odd, mine, other)], axis=0)
    half = channels // 2
    for i in range(3):
        block = packed[i * channels : (i + 1) * channels]
        kernel_ref[3 * i] = block[:, :channels]
        kernel_ref[3 * i + 1] = block[:, channels:]
    block = packed[3 * channels : 4 * channels]
    kernel_ref[2] = block[:, :channels]
    kernel_ref[5] = block[:, channels:]
    block = packed[4 * channels : 4 * channels + half]
    kernel_ref[8, :half] = block[:, :channels]
    kernel_ref[8, half:] = block[:, channels:]


def unpack(mine, other, channels, fields):
    return pl.pallas_call(
        functools.partial(unpack_kernel, channels),
        out_shape=(
            jax.ShapeDtypeStruct((9, channels, channels), jnp.float32),
            jax.ShapeDtypeStruct((fields, channels), jnp.float32),
            jax.ShapeDtypeStruct((fields, channels), jnp.float32),
        ),
        compiler_params=pltpu.CompilerParams(vmem_limit_bytes=VMEM_LIMIT),
        name="unpack",
    )(mine, other)


def swap(x, axis, bit):
    return lax.ppermute(x, axis, [(i, i ^ bit) for i in range(lax.axis_size(axis))])


def sum_over(x, axis, low, high):
    if high // low == 4:
        a, b, c = (swap(x, axis, k * low) for k in (1, 2, 3))
        return (x + a) + (b + c)
    bit = low
    while bit < high:
        x = x + swap(x, axis, bit)
        bit *= 2
    return x


def pair_swap(even_sends, odd_sends, axis, periodic):
    count = lax.axis_size(axis)
    even = lax.rem(lax.axis_index(axis), 2) == 0
    inner = [(i, i ^ 1) for i in range(count)]
    outer = []
    for i in range(1, count, 2):
        if i + 1 < count or periodic:
            outer += [(i, (i + 1) % count), ((i + 1) % count, i)]
    got_inner = lax.ppermute(jnp.where(even, odd_sends, even_sends), axis, inner)
    got_outer = lax.ppermute(jnp.where(even, even_sends, odd_sends), axis, outer)
    return jnp.where(even, got_outer, got_inner), jnp.where(even, got_inner, got_outer)


def per_device(
    source,
    intersection_weight,
    dest_tile,
    dest_row,
    prior_state,
    lift_weight,
    kernel,
    readout_weights,
):
    face_count = lax.axis_size("face")
    lon_count = lax.axis_size("lon")
    devices = face_count * lon_count
    src_blocks, intersections = dest_tile.shape
    fields, rows, width = prior_state.shape
    channels = kernel.shape[1]
    capacity = max(2, 2 * src_blocks * intersections // devices)
    norm = 1.0 / math.sqrt(rows * face_count * width * lon_count)

    outgoing = regrid(source, intersection_weight, dest_tile, dest_row, devices, capacity)
    outgoing, prior_state, kernel, lift_weight, readout_weights = lax.optimization_barrier(
        (outgoing, prior_state, kernel, lift_weight, readout_weights)
    )
    arrived = lax.all_to_all(outgoing, ("face", "lon"), split_axis=0, concat_axis=0, tiled=True)
    arrived = arrived.reshape(devices, (capacity + 1) * fields, source.shape[2])

    prior = prior_state.transpose(1, 0, 2)
    top, bottom = pair_swap(prior[0], prior[rows - 1], "face", False)
    columns = [
        jnp.pad(
            jnp.concatenate([top[:, at : at + 1], prior_state[:, :, at], bottom[:, at : at + 1]], axis=1),
            ((0, 0), (0, 128 - rows - 2)),
        )
        for at in (0, width - 1)
    ]
    left, right = pair_swap(columns[0], columns[1], "lon", True)

    edges = jnp.stack([top, bottom])
    sides = jnp.concatenate([left, right], axis=1)
    part, lift, conv, back, contract = convolve(prior, edges, lift_weight, kernel)
    act, stack, forecast = finish(part, prior, sides, lift, conv, readout_weights)
    remapped, packed, slope, moment = backward(
        arrived, prior, edges, stack, lift, act, forecast, readout_weights, capacity, norm
    )
    lift_part = lift_gradient(slope, prior, back, contract, moment, packed.shape[1])
    part = packed[0] + swap(packed[1], "lon", 1) + lift_part
    part = sum_over(part, "face", 1, face_count)
    part = sum_over(part, "lon", 2, lon_count)
    grad_kernel, grad_lift, grad_head = unpack(part, swap(part, "lon", 1), channels, fields)
    return (
        remapped.astype(jnp.bfloat16),
        forecast.astype(jnp.bfloat16),
        grad_lift,
        grad_kernel,
        grad_head.T,
    )


def solution(mesh):
    return jax.shard_map(
        per_device,
        mesh=mesh,
        in_specs=(
            P(("face", "lon"), None, None),
            P(("face", "lon"), None, None, None),
            P(("face", "lon"), None),
            P(("face", "lon"), None),
            P(None, "face", "lon"),
            P(),
            P(),
            P(),
        ),
        out_specs=(P(None, "face", "lon"), P(None, "face", "lon"), P(), P(), P()),
        check_vma=False,
    )
```

```python
import functools
import math

import jax
import jax.numpy as jnp
from jax import lax
from jax.experimental import pallas as pl
from jax.experimental.pallas import tpu as pltpu
from jax.sharding import PartitionSpec as P

NT = (((1,), (1,)), ((), ()))
VMEM_LIMIT = 24 * 1024 * 1024
REGRID_VMEM = 60 * 1024 * 1024


def dot(a, b):
    return jnp.dot(a, b, preferred_element_type=jnp.float32)


def dot_nt(a, b):
    return lax.dot_general(a, b, NT, preferred_element_type=jnp.float32)


def sigmoid(x):
    return 1.0 / (1.0 + jnp.exp(-x))


def regrid_kernel(
    capacity,
    tile_hbm,
    row_hbm,
    src_hbm,
    wts_hbm,
    out_ref,
    tile_ref,
    row_ref,
    src_ref,
    wts_ref,
    count_ref,
    slot_ref,
    head_ref,
    sems,
):
    blocks, fields, width = src_ref.shape
    intersections = wts_ref.shape[1]
    devices = out_ref.shape[0]
    chunks = sems.shape[0] - 3
    chunk = blocks // chunks
    copies = [
        pltpu.make_async_copy(
            wts_hbm.at[pl.ds(i * chunk, chunk)], wts_ref.at[pl.ds(i * chunk, chunk)], sems.at[i]
        )
        for i in range(chunks)
    ]
    pairs = ((tile_hbm, tile_ref), (row_hbm, row_ref), (src_hbm, src_ref))
    first = [pltpu.make_async_copy(a, b, sems.at[chunks + i]) for i, (a, b) in enumerate(pairs)]
    for copy in first + copies:
        copy.start()
    head_ref[...] = jnp.full_like(head_ref, -1.0)
    for d in range(devices):
        count_ref[d] = 0
    for copy in first:
        copy.wait()
    slot_of_lane = lax.rem(lax.broadcasted_iota(jnp.int32, (1, width), 1), capacity)
    for s in range(blocks):
        for k in range(intersections):
            tile = tile_ref[k, s]
            slot = count_ref[tile]
            count_ref[tile] = slot + 1
            slot_ref[k, s] = slot
            label = row_ref[k, s].astype(jnp.float32)
            head_ref[pl.ds(tile, 1), :] = jnp.where(slot_of_lane == slot, label, head_ref[pl.ds(tile, 1), :])
    out_ref[...] = jnp.zeros_like(out_ref)
    for d in range(devices):
        out_ref[d, capacity] = jnp.broadcast_to(head_ref[d : d + 1, :], (fields, width)).astype(jnp.bfloat16)
    for i in range(chunks):
        copies[i].wait()
        for s in range(i * chunk, (i + 1) * chunk):
            block = src_ref[s]
            for pair in range(0, intersections, 2):
                both = range(pair, min(pair + 2, intersections))
                contrib = dot(block, jnp.concatenate([wts_ref[s, k] for k in both], axis=1)).astype(jnp.bfloat16)
                for k in both:
                    out_ref[tile_ref[k, s], slot_ref[k, s]] = contrib[:, (k - pair) * width : (k - pair + 1) * width]


def regrid(source, weights, dest_tile, dest_row, devices, capacity):
    blocks, fields, width = source.shape
    intersections = weights.shape[1]
    chunks = math.gcd(blocks, 4)
    vmem = pl.BlockSpec(memory_space=pltpu.VMEM)
    return pl.pallas_call(
        functools.partial(regrid_kernel, capacity),
        out_shape=jax.ShapeDtypeStruct((devices, capacity + 1, fields, width), jnp.bfloat16),
        in_specs=[pl.BlockSpec(memory_space=pl.ANY)] * 4,
        out_specs=vmem,
        scratch_shapes=[
            pltpu.SMEM((intersections, blocks), jnp.int32),
            pltpu.SMEM((intersections, blocks), jnp.int32),
            pltpu.VMEM(source.shape, jnp.bfloat16),
            pltpu.VMEM(weights.shape, jnp.bfloat16),
            pltpu.SMEM((devices,), jnp.int32),
            pltpu.SMEM((intersections, blocks), jnp.int32),
            pltpu.VMEM((devices, width), jnp.float32),
            pltpu.SemaphoreType.DMA((chunks + 3,)),
        ],
        compiler_params=pltpu.CompilerParams(vmem_limit_bytes=REGRID_VMEM),
        cost_estimate=pl.CostEstimate(
            flops=2 * weights.size * fields, bytes_accessed=2 * weights.size, transcendentals=0
        ),
        name="regrid",
    )(dest_tile.T, dest_row.T, source, weights)


def lift_rows(prior_ref, edge_ref, lift, feat_ref):
    rows = prior_ref.shape[0]
    pitch = lift.shape[0]
    for at in range(rows + 2):
        values = edge_ref[0] if at == 0 else edge_ref[1] if at == rows + 1 else prior_ref[at - 1]
        feat_ref[at * pitch : (at + 1) * pitch, :] = dot(lift, values).astype(jnp.bfloat16)


def convolve_kernel(
    prior_ref,
    edge_ref,
    lift_weight_ref,
    kernel_ref,
    act_ref,
    lift_ref,
    conv_ref,
    back_ref,
    contract_ref,
    feat_ref,
):
    rows, fields, width = prior_ref.shape
    channels = kernel_ref.shape[1]
    pitch = lift_ref.shape[0]

    taps = [kernel_ref[t].astype(jnp.float32) for t in range(9)]
    for i in range(3):
        back_ref[i * channels : (i + 1) * channels, :] = jnp.concatenate(
            [taps[6 + i], taps[3 + i], taps[i]], axis=1
        ).astype(jnp.bfloat16)
        contract_ref[i] = jnp.concatenate(taps[3 * i : 3 * i + 3], axis=1).astype(jnp.bfloat16)
    empty = jnp.zeros((pitch - channels, 3 * channels), jnp.float32)
    by_input = [piece for i in range(3) for piece in (jnp.concatenate(taps[3 * i : 3 * i + 3], axis=1), empty)]
    conv_ref[...] = jnp.concatenate(by_input, axis=0).T.astype(jnp.bfloat16)
    same = lax.broadcasted_iota(jnp.int32, (fields, pitch - channels), 0) == lax.broadcasted_iota(
        jnp.int32, (fields, pitch - channels), 1
    )
    lift = jnp.concatenate([lift_weight_ref[...].astype(jnp.float32), jnp.where(same, 1.0, 0.0)], axis=1)
    lift_ref[...] = lift.T.astype(jnp.bfloat16)

    lift_rows(prior_ref, edge_ref, lift_ref[...], feat_ref)
    lane = lax.broadcasted_iota(jnp.int32, (channels, width), 1)
    for y in range(rows):
        parts = dot(conv_ref[...], feat_ref[y * pitch : (y + 3) * pitch, :])
        left = jnp.where(lane == 0, 0.0, pltpu.roll(parts[:channels], 1, 1))
        right = jnp.where(lane == width - 1, 0.0, pltpu.roll(parts[2 * channels :], width - 1, 1))
        act_ref[y * channels : (y + 1) * channels, :] = parts[channels : 2 * channels] + left + right


def convolve(prior, edges, lift_weight, kernel):
    rows, fields, width = prior.shape
    channels = kernel.shape[1]
    pitch = channels + 16
    vmem = pl.BlockSpec(memory_space=pltpu.VMEM)
    return pl.pallas_call(
        convolve_kernel,
        out_shape=(
            jax.ShapeDtypeStruct((rows * channels, width), jnp.float32),
            jax.ShapeDtypeStruct((pitch, fields), jnp.bfloat16),
            jax.ShapeDtypeStruct((3 * channels, 3 * pitch), jnp.bfloat16),
            jax.ShapeDtypeStruct((3 * channels, 3 * channels), jnp.bfloat16),
            jax.ShapeDtypeStruct((3, channels, 3 * channels), jnp.bfloat16),
        ),
        in_specs=[vmem] * 4,
        out_specs=[vmem] * 5,
        scratch_shapes=[pltpu.VMEM(((rows + 2) * pitch, width), jnp.bfloat16)],
        compiler_params=pltpu.CompilerParams(vmem_limit_bytes=VMEM_LIMIT),
        cost_estimate=pl.CostEstimate(
            flops=2 * rows * width * 3 * channels * 3 * pitch,
            bytes_accessed=rows * width * channels * 8,
            transcendentals=0,
        ),
        name="convolve",
    )(prior, edges, lift_weight, kernel)


def finish_kernel(
    part_ref,
    prior_ref,
    side_ref,
    lift_ref,
    conv_ref,
    readout_ref,
    act_ref,
    stack_ref,
    forecast_ref,
    halo_ref,
    hidden_ref,
    by_row_ref,
):
    rows, fields, width = prior_ref.shape
    channels = readout_ref.shape[0]
    side = dot(lift_ref[...], side_ref[...])
    shifted = [side] + [pltpu.roll(side, 256 - i, 1) for i in (1, 2)]
    stack = jnp.concatenate(shifted, axis=0).astype(jnp.bfloat16)
    stack_ref[...] = stack
    halo_ref[:, :128] = dot(conv_ref[:channels, :], stack[:, :128])
    halo_ref[:, 128:] = dot(conv_ref[2 * channels :, :], stack[:, 128:])
    readout = readout_ref[...].astype(jnp.float32).T.astype(jnp.bfloat16)
    lane = lax.broadcasted_iota(jnp.int32, (channels, 128), 1)
    spread = [jnp.zeros((channels, 128), jnp.float32)] * (width // 128 - 1)
    for y in range(rows):
        here = slice(y * channels, (y + 1) * channels)
        from_left = jnp.where(lane == 0, pltpu.roll(halo_ref[:, :128], (128 - y) % 128, 1), 0.0)
        from_right = jnp.where(lane == 127, pltpu.roll(halo_ref[:, 128:], 127 - y, 1), 0.0)
        act = (
            part_ref[here, :]
            + jnp.concatenate([from_left] + spread, axis=1)
            + jnp.concatenate(spread + [from_right], axis=1)
        )
        act_ref[here, :] = act
        hidden_ref[here, :] = (act * sigmoid(act)).astype(jnp.bfloat16)
    for y in range(rows):
        increment = dot(readout, hidden_ref[y * channels : (y + 1) * channels, :])
        by_row_ref[y] = prior_ref[y].astype(jnp.float32) + increment
    forecast_ref[...] = jnp.transpose(by_row_ref[...], (1, 0, 2))


def finish(part, prior, sides, lift, conv, readout):
    rows, fields, width = prior.shape
    channels = readout.shape[0]
    vmem = pl.BlockSpec(memory_space=pltpu.VMEM)
    return pl.pallas_call(
        finish_kernel,
        out_shape=(
            jax.ShapeDtypeStruct(part.shape, jnp.float32),
            jax.ShapeDtypeStruct((conv.shape[1], 256), jnp.bfloat16),
            jax.ShapeDtypeStruct((fields, rows, width), jnp.float32),
        ),
        in_specs=[vmem] * 6,
        out_specs=[vmem] * 3,
        scratch_shapes=[
            pltpu.VMEM((channels, 256), jnp.float32),
            pltpu.VMEM((rows * channels, width), jnp.bfloat16),
            pltpu.VMEM((rows, fields, width), jnp.float32),
        ],
        input_output_aliases={0: 0},
        compiler_params=pltpu.CompilerParams(vmem_limit_bytes=VMEM_LIMIT),
        cost_estimate=pl.CostEstimate(
            flops=2 * rows * width * channels * fields,
            bytes_accessed=rows * width * channels * 8,
            transcendentals=rows * width * channels * 2,
        ),
        name="finish",
    )(part, prior, sides, lift, conv, readout)


def backward_kernel(
    capacity,
    channels,
    norm,
    arrived_ref,
    prior_ref,
    edge_ref,
    stack_ref,
    lift_ref,
    act_ref,
    forecast_ref,
    readout_ref,
    remapped_ref,
    packed_ref,
    slope_ref,
    moment_ref,
    feat_ref,
    hidden_ref,
    block_ref,
    misfit_ref,
    state_ref,
    before_ref,
    after_ref,
):
    fields, rows, width = remapped_ref.shape
    pitch = lift_ref.shape[0]
    devices = arrived_ref.shape[0]
    per_row = width // 128
    slots = devices * capacity

    lift_rows(prior_ref, edge_ref, lift_ref[...], feat_ref)
    slope_ref[:channels, :] = jnp.zeros((channels, width), jnp.bfloat16)
    slope_ref[(rows + 1) * channels :, :] = jnp.zeros((channels, width), jnp.bfloat16)
    depth = fields * rows
    lane = lax.broadcasted_iota(jnp.int32, (fields, depth), 1)
    spread = jnp.where(lane // rows == lax.broadcasted_iota(jnp.int32, (fields, depth), 0), 1.0, 0.0)
    spread = dot(readout_ref[...], spread.astype(jnp.bfloat16))
    lane = lax.broadcasted_iota(jnp.int32, (channels, depth), 1) % rows
    for y in range(rows):
        block_ref[y * channels : (y + 1) * channels, :] = jnp.where(lane == y, spread, 0.0).astype(jnp.bfloat16)

    labels = []
    for first in range(0, devices, 128 // capacity):
        lane = lax.broadcasted_iota(jnp.int32, (fields, 128), 1) // capacity
        label = None
        for d in range(min(devices, 128 // capacity)):
            mine = arrived_ref[first + d, capacity * fields : (capacity + 1) * fields, :].astype(jnp.float32)
            label = mine if label is None else jnp.where(lane == d, mine, label)
        labels.append(label)
    labels = jnp.concatenate(labels, axis=1).astype(jnp.int32)
    tile_blocks = rows * per_row
    labels = jnp.concatenate([labels] * (tile_blocks // fields), axis=0)
    at = lax.broadcasted_iota(jnp.int32, (tile_blocks, slots), 0)
    hits = jnp.where(labels == (at % rows) * per_row + at // rows, 1.0, 0.0).astype(jnp.bfloat16)
    data = arrived_ref[:, : capacity * fields, :].astype(jnp.float32).reshape(slots, fields, 128)
    data = jnp.transpose(data, (1, 0, 2)).astype(jnp.bfloat16)
    for f in range(0, fields, 2):
        picked = dot(hits, jnp.concatenate([data[f], data[f + 1]], axis=1))
        for g in range(2):
            target = picked[:, g * 128 : (g + 1) * 128].astype(jnp.bfloat16)
            target = jnp.concatenate([target[b * rows : (b + 1) * rows] for b in range(per_row)], axis=1)
            target = target.astype(jnp.float32)
            remapped_ref[f + g] = target
            misfit_ref[f + g] = (forecast_ref[f + g] - target) * norm
    by_row = jnp.transpose(misfit_ref[...], (1, 0, 2))
    empty = jnp.zeros((fields, width), jnp.float32)
    for y in range(rows):
        state_ref[:, y * width : (y + 1) * width] = jnp.concatenate([by_row[y], empty], axis=0).astype(jnp.bfloat16)

    col = lax.broadcasted_iota(jnp.int32, (channels, width), 1)
    lane = lax.broadcasted_iota(jnp.int32, (channels, 128), 1)
    ends_left = ends_right = jnp.zeros((channels, 128), jnp.float32)
    batch = 8
    misfits = misfit_ref[...].reshape(depth, width).astype(jnp.bfloat16)
    for first in range(0, rows, batch):
        latents = dot(block_ref[first * channels : (first + batch) * channels, :], misfits)
        for y in range(first, first + batch):
            here = slice(y * channels, (y + 1) * channels)
            act = act_ref[here, :]
            sig = sigmoid(act)
            hidden_ref[here, :] = (act * sig).astype(jnp.bfloat16)
            latent = latents[(y - first) * channels : (y - first + 1) * channels]
            slope = latent * sig * (1.0 + act * (1.0 - sig))
            slope_ref[(y + 1) * channels : (y + 2) * channels, :] = slope.astype(jnp.bfloat16)
            before = jnp.where(col == width - 1, 0.0, pltpu.roll(slope, width - 1, 1))
            before_ref[here, :] = before.astype(jnp.bfloat16)
            after_ref[here, :] = jnp.where(col == 0, 0.0, pltpu.roll(slope, 1, 1)).astype(jnp.bfloat16)
            ends_left += pltpu.roll(jnp.where(lane == 0, slope[:, :128], 0.0), y, 1)
            ends_right += pltpu.roll(jnp.where(lane == 127, slope[:, -128:], 0.0), y + 1, 1)

    total = None
    for first in range(0, rows, batch):
        span = range(first, first + batch)
        features = jnp.concatenate([feat_ref[y * pitch : (y + 3) * pitch, :] for y in span], axis=1)
        features = jnp.concatenate([features, state_ref[:, first * width : (first + batch) * width]], axis=0)
        others = jnp.concatenate(
            [
                jnp.concatenate([ref[(y + d) * channels : (y + d + 1) * channels, :] for y in span], axis=1)
                for ref, d in ((before_ref, 0), (slope_ref, 1), (after_ref, 0), (hidden_ref, 0))
            ],
            axis=0,
        )
        part = dot_nt(features, others)
        total = part if total is None else total + part
    grad_head = total[3 * pitch : 3 * pitch + fields, 3 * channels :]
    stack = stack_ref[...]
    from_left = dot_nt(stack[:, :128], ends_left.astype(jnp.bfloat16))
    from_right = dot_nt(stack[:, 128:], ends_right.astype(jnp.bfloat16))
    middle = jnp.zeros((3 * pitch, channels), jnp.float32)
    total = total[: 3 * pitch, : 3 * channels] + jnp.concatenate([from_left, middle, from_right], axis=1)
    for i in range(3):
        moment_ref[i] = total[i * pitch + channels : i * pitch + channels + fields, :]
    taps = [total[i * pitch : i * pitch + channels, :] for i in range(3)]
    half = channels // 2
    last = [t[:, 2 * channels :] for t in taps]
    packed = [t[:, : 2 * channels] for t in taps]
    packed.append(jnp.concatenate(last[:2], axis=1))
    packed.append(jnp.concatenate([last[2][:half], last[2][half:]], axis=1))
    packed = jnp.concatenate(packed, axis=0)
    cut = packed.shape[0] // 2
    head = jnp.concatenate([grad_head, jnp.zeros_like(grad_head)], axis=1)
    odd = lax.rem(lax.axis_index("lon"), 2)
    packed_ref[odd] = jnp.concatenate([packed[:cut], head], axis=0)
    packed_ref[1 - odd] = jnp.concatenate([packed[cut:], jnp.zeros_like(head)], axis=0)


def backward(arrived, prior, edges, stack, lift, act, forecast, readout, capacity, norm):
    fields, rows, width = forecast.shape
    channels = readout.shape[0]
    pitch = lift.shape[0]
    packed_rows = (3 * channels + channels + channels // 2) // 2 + fields
    vmem = pl.BlockSpec(memory_space=pltpu.VMEM)
    return pl.pallas_call(
        functools.partial(backward_kernel, capacity, channels, norm),
        out_shape=(
            jax.ShapeDtypeStruct((fields, rows, width), jnp.float32),
            jax.ShapeDtypeStruct((2, packed_rows, 2 * channels), jnp.float32),
            jax.ShapeDtypeStruct(((rows + 2) * channels, width), jnp.bfloat16),
            jax.ShapeDtypeStruct((3, fields, 3 * channels), jnp.float32),
        ),
        in_specs=[vmem] * 8,
        out_specs=[vmem] * 4,
        scratch_shapes=[
            pltpu.VMEM(((rows + 2) * pitch, width), jnp.bfloat16),
            pltpu.VMEM((rows * channels, width), jnp.bfloat16),
            pltpu.VMEM((rows * channels, rows * fields), jnp.bfloat16),
            pltpu.VMEM((fields, rows, width), jnp.float32),
            pltpu.VMEM((2 * fields, rows * width), jnp.bfloat16),
            pltpu.VMEM((rows * channels, width), jnp.bfloat16),
            pltpu.VMEM((rows * channels, width), jnp.bfloat16),
        ],
        compiler_params=pltpu.CompilerParams(vmem_limit_bytes=VMEM_LIMIT),
        cost_estimate=pl.CostEstimate(
            flops=2 * rows * width * 3 * channels * 3 * pitch,
            bytes_accessed=rows * width * channels * 8,
            transcendentals=0,
        ),
        name="backward",
    )(arrived, prior, edges, stack, lift, act, forecast, readout)


def lift_gradient_kernel(slope_ref, prior_ref, back_ref, contract_ref, moment_ref, out_ref, delta_ref):
    rows, fields, width = prior_ref.shape
    channels = contract_ref.shape[1]
    col = lax.broadcasted_iota(jnp.int32, (fields, width), 1)
    inside = (col > 0) & (col < width - 1)
    delta_ref[:channels, :] = jnp.zeros((channels, width), jnp.bfloat16)
    delta_ref[(rows - 1) * channels :, :] = jnp.zeros((channels, width), jnp.bfloat16)
    for y in range(1, rows - 1):
        parts = dot(back_ref[...], slope_ref[y * channels : (y + 3) * channels, :])
        grad = (
            parts[channels : 2 * channels]
            + pltpu.roll(parts[:channels], width - 1, 1)
            + pltpu.roll(parts[2 * channels :], 1, 1)
        )
        delta = grad.astype(jnp.bfloat16).astype(jnp.float32) - grad
        delta_ref[y * channels : (y + 1) * channels, :] = delta.astype(jnp.bfloat16)
    crossed = jnp.zeros((channels, fields), jnp.float32)
    batch = 4
    for first in range(0, rows, batch):
        span = range(first, first + batch)
        states = [jnp.where(inside, prior_ref[y].astype(jnp.float32), 0.0).astype(jnp.bfloat16) for y in span]
        states = jnp.concatenate(states, axis=1)
        deltas = jnp.concatenate([delta_ref[y * channels : (y + 1) * channels, :] for y in span], axis=1)
        crossed += dot_nt(deltas, states)
    grad_lift = crossed.T
    for i in range(3):
        rest, pieces = moment_ref[i], []
        for _ in range(3):
            pieces.append(rest.astype(jnp.bfloat16).astype(jnp.float32))
            rest = rest - pieces[-1]
        part = dot_nt(jnp.concatenate(pieces, axis=0).astype(jnp.bfloat16), contract_ref[i])
        grad_lift += part[:fields] + part[fields : 2 * fields] + part[2 * fields :]
    out_ref[...] = jnp.zeros_like(out_ref)
    out_ref[-fields:, channels:] = grad_lift


def lift_gradient(slope, prior, back, contract, moment, packed_rows):
    rows, fields, width = prior.shape
    channels = contract.shape[1]
    vmem = pl.BlockSpec(memory_space=pltpu.VMEM)
    return pl.pallas_call(
        lift_gradient_kernel,
        out_shape=jax.ShapeDtypeStruct((packed_rows, 2 * channels), jnp.float32),
        in_specs=[vmem] * 5,
        out_specs=vmem,
        scratch_shapes=[pltpu.VMEM((rows * channels, width), jnp.bfloat16)],
        compiler_params=pltpu.CompilerParams(vmem_limit_bytes=VMEM_LIMIT),
        cost_estimate=pl.CostEstimate(
            flops=2 * rows * width * 9 * channels * channels, bytes_accessed=slope.size * 2, transcendentals=0
        ),
        name="lift_gradient",
    )(slope, prior, back, contract, moment)


def unpack_kernel(channels, mine_ref, other_ref, kernel_ref, lift_ref, head_ref):
    odd = lax.rem(lax.axis_index("lon"), 2) == 1
    fields = lift_ref.shape[0]
    mine, other = mine_ref[-fields:, :], other_ref[-fields:, :]
    lift_ref[...] = (mine + other)[:, channels:]
    head_ref[...] = jnp.where(odd, other, mine)[:, :channels]
    mine, other = mine_ref[:-fields, :], other_ref[:-fields, :]
    packed = jnp.concatenate([jnp.where(odd, other, mine), jnp.where(odd, mine, other)], axis=0)
    half = channels // 2
    for i in range(3):
        block = packed[i * channels : (i + 1) * channels]
        kernel_ref[3 * i] = block[:, :channels]
        kernel_ref[3 * i + 1] = block[:, channels:]
    block = packed[3 * channels : 4 * channels]
    kernel_ref[2] = block[:, :channels]
    kernel_ref[5] = block[:, channels:]
    block = packed[4 * channels : 4 * channels + half]
    kernel_ref[8, :half] = block[:, :channels]
    kernel_ref[8, half:] = block[:, channels:]


def unpack(mine, other, channels, fields):
    return pl.pallas_call(
        functools.partial(unpack_kernel, channels),
        out_shape=(
            jax.ShapeDtypeStruct((9, channels, channels), jnp.float32),
            jax.ShapeDtypeStruct((fields, channels), jnp.float32),
            jax.ShapeDtypeStruct((fields, channels), jnp.float32),
        ),
        compiler_params=pltpu.CompilerParams(vmem_limit_bytes=VMEM_LIMIT),
        name="unpack",
    )(mine, other)


def swap(x, axis, bit):
    return lax.ppermute(x, axis, [(i, i ^ bit) for i in range(lax.axis_size(axis))])


def sum_over(x, axis, low, high):
    if high // low == 4:
        a, b, c = (swap(x, axis, k * low) for k in (1, 2, 3))
        return (x + a) + (b + c)
    bit = low
    while bit < high:
        x = x + swap(x, axis, bit)
        bit *= 2
    return x


def pair_swap(even_sends, odd_sends, axis, periodic):
    count = lax.axis_size(axis)
    even = lax.rem(lax.axis_index(axis), 2) == 0
    inner = [(i, i ^ 1) for i in range(count)]
    outer = []
    for i in range(1, count, 2):
        if i + 1 < count or periodic:
            outer += [(i, (i + 1) % count), ((i + 1) % count, i)]
    got_inner = lax.ppermute(jnp.where(even, odd_sends, even_sends), axis, inner)
    got_outer = lax.ppermute(jnp.where(even, even_sends, odd_sends), axis, outer)
    return jnp.where(even, got_outer, got_inner), jnp.where(even, got_inner, got_outer)


def per_device(
    source,
    intersection_weight,
    dest_tile,
    dest_row,
    prior_state,
    lift_weight,
    kernel,
    readout_weights,
):
    face_count = lax.axis_size("face")
    lon_count = lax.axis_size("lon")
    devices = face_count * lon_count
    src_blocks, intersections = dest_tile.shape
    fields, rows, width = prior_state.shape
    channels = kernel.shape[1]
    capacity = max(2, 2 * src_blocks * intersections // devices)
    norm = 1.0 / math.sqrt(rows * face_count * width * lon_count)

    outgoing = regrid(source, intersection_weight, dest_tile, dest_row, devices, capacity)
    outgoing, prior_state, kernel, lift_weight, readout_weights = lax.optimization_barrier(
        (outgoing, prior_state, kernel, lift_weight, readout_weights)
    )
    arrived = lax.all_to_all(outgoing, ("face", "lon"), split_axis=0, concat_axis=0, tiled=True)
    arrived = arrived.reshape(devices, (capacity + 1) * fields, source.shape[2])

    prior = prior_state.transpose(1, 0, 2)
    top, bottom = pair_swap(prior[0], prior[rows - 1], "face", False)
    columns = [
        jnp.pad(
            jnp.concatenate([top[:, at : at + 1], prior_state[:, :, at], bottom[:, at : at + 1]], axis=1),
            ((0, 0), (0, 128 - rows - 2)),
        )
        for at in (0, width - 1)
    ]
    left, right = pair_swap(columns[0], columns[1], "lon", True)

    edges = jnp.stack([top, bottom])
    sides = jnp.concatenate([left, right], axis=1)
    part, lift, conv, back, contract = convolve(prior, edges, lift_weight, kernel)
    act, stack, forecast = finish(part, prior, sides, lift, conv, readout_weights)
    remapped, packed, slope, moment = backward(
        arrived, prior, edges, stack, lift, act, forecast, readout_weights, capacity, norm
    )
    lift_part = lift_gradient(slope, prior, back, contract, moment, packed.shape[1])
    part = packed[0] + swap(packed[1], "lon", 1) + lift_part
    part = sum_over(part, "face", 1, face_count)
    part, remapped, estimate = lax.optimization_barrier(
        (part, remapped.astype(jnp.bfloat16), forecast.astype(jnp.bfloat16))
    )
    part = sum_over(part, "lon", 2, lon_count)
    grad_kernel, grad_lift, grad_head = unpack(part, swap(part, "lon", 1), channels, fields)
    return (
        remapped,
        estimate,
        grad_lift,
        grad_kernel,
        grad_head.T,
    )


def solution(mesh):
    return jax.shard_map(
        per_device,
        mesh=mesh,
        in_specs=(
            P(("face", "lon"), None, None),
            P(("face", "lon"), None, None, None),
            P(("face", "lon"), None),
            P(("face", "lon"), None),
            P(None, "face", "lon"),
            P(),
            P(),
            P(),
        ),
        out_specs=(P(None, "face", "lon"), P(None, "face", "lon"), P(), P(), P()),
        check_vma=False,
    )
```

```python
import functools
import math

import jax
import jax.numpy as jnp
from jax import lax
from jax.experimental import pallas as pl
from jax.experimental.pallas import tpu as pltpu
from jax.sharding import PartitionSpec as P

NT = (((1,), (1,)), ((), ()))
VMEM_LIMIT = 24 * 1024 * 1024
REGRID_VMEM = 60 * 1024 * 1024


def dot(a, b):
    return jnp.dot(a, b, preferred_element_type=jnp.float32)


def dot_nt(a, b):
    return lax.dot_general(a, b, NT, preferred_element_type=jnp.float32)


def sigmoid(x):
    return 1.0 / (1.0 + jnp.exp(-x))


def regrid_kernel(
    capacity,
    tile_hbm,
    row_hbm,
    src_hbm,
    wts_hbm,
    out_ref,
    tile_ref,
    row_ref,
    src_ref,
    wts_ref,
    count_ref,
    slot_ref,
    head_ref,
    sems,
):
    blocks, fields, width = src_ref.shape
    intersections = wts_ref.shape[1]
    devices = out_ref.shape[0]
    chunks = sems.shape[0] - 3
    chunk = blocks // chunks
    copies = [
        pltpu.make_async_copy(
            wts_hbm.at[pl.ds(i * chunk, chunk)], wts_ref.at[pl.ds(i * chunk, chunk)], sems.at[i]
        )
        for i in range(chunks)
    ]
    pairs = ((tile_hbm, tile_ref), (row_hbm, row_ref), (src_hbm, src_ref))
    first = [pltpu.make_async_copy(a, b, sems.at[chunks + i]) for i, (a, b) in enumerate(pairs)]
    for copy in first + copies:
        copy.start()
    head_ref[...] = jnp.full_like(head_ref, -1.0)
    for d in range(devices):
        count_ref[d] = 0
    for copy in first:
        copy.wait()
    slot_of_lane = lax.rem(lax.broadcasted_iota(jnp.int32, (1, width), 1), capacity)
    for s in range(blocks):
        for k in range(intersections):
            tile = tile_ref[k, s]
            slot = count_ref[tile]
            count_ref[tile] = slot + 1
            slot_ref[k, s] = slot
            label = row_ref[k, s].astype(jnp.float32)
            head_ref[pl.ds(tile, 1), :] = jnp.where(slot_of_lane == slot, label, head_ref[pl.ds(tile, 1), :])
    out_ref[...] = jnp.zeros_like(out_ref)
    for d in range(devices):
        out_ref[d, capacity] = jnp.broadcast_to(head_ref[d : d + 1, :], (fields, width)).astype(jnp.bfloat16)
    for i in range(chunks):
        copies[i].wait()
        for s in range(i * chunk, (i + 1) * chunk):
            block = src_ref[s]
            for pair in range(0, intersections, 2):
                both = range(pair, min(pair + 2, intersections))
                contrib = dot(block, jnp.concatenate([wts_ref[s, k] for k in both], axis=1)).astype(jnp.bfloat16)
                for k in both:
                    out_ref[tile_ref[k, s], slot_ref[k, s]] = contrib[:, (k - pair) * width : (k - pair + 1) * width]


def regrid(source, weights, dest_tile, dest_row, devices, capacity):
    blocks, fields, width = source.shape
    intersections = weights.shape[1]
    chunks = math.gcd(blocks, 4)
    vmem = pl.BlockSpec(memory_space=pltpu.VMEM)
    return pl.pallas_call(
        functools.partial(regrid_kernel, capacity),
        out_shape=jax.ShapeDtypeStruct((devices, capacity + 1, fields, width), jnp.bfloat16),
        in_specs=[pl.BlockSpec(memory_space=pl.ANY)] * 4,
        out_specs=vmem,
        scratch_shapes=[
            pltpu.SMEM((intersections, blocks), jnp.int32),
            pltpu.SMEM((intersections, blocks), jnp.int32),
            pltpu.VMEM(source.shape, jnp.bfloat16),
            pltpu.VMEM(weights.shape, jnp.bfloat16),
            pltpu.SMEM((devices,), jnp.int32),
            pltpu.SMEM((intersections, blocks), jnp.int32),
            pltpu.VMEM((devices, width), jnp.float32),
            pltpu.SemaphoreType.DMA((chunks + 3,)),
        ],
        compiler_params=pltpu.CompilerParams(vmem_limit_bytes=REGRID_VMEM),
        cost_estimate=pl.CostEstimate(
            flops=2 * weights.size * fields, bytes_accessed=2 * weights.size, transcendentals=0
        ),
        name="regrid",
    )(dest_tile.T, dest_row.T, source, weights)


def lift_rows(prior_ref, edge_ref, lift, feat_ref):
    rows = prior_ref.shape[0]
    pitch = lift.shape[0]
    for at in range(rows + 2):
        values = edge_ref[0] if at == 0 else edge_ref[1] if at == rows + 1 else prior_ref[at - 1]
        feat_ref[at * pitch : (at + 1) * pitch, :] = dot(lift, values).astype(jnp.bfloat16)


def convolve_kernel(
    prior_ref,
    edge_ref,
    lift_weight_ref,
    kernel_ref,
    readout_ref,
    act_ref,
    forecast_ref,
    ends_ref,
    lift_ref,
    conv_ref,
    back_ref,
    contract_ref,
    turned_ref,
    feat_ref,
    hidden_ref,
    by_row_ref,
):
    rows, fields, width = prior_ref.shape
    channels = kernel_ref.shape[1]
    pitch = lift_ref.shape[0]

    taps = [kernel_ref[t].astype(jnp.float32) for t in range(9)]
    for i in range(3):
        back_ref[i * channels : (i + 1) * channels, :] = jnp.concatenate(
            [taps[6 + i], taps[3 + i], taps[i]], axis=1
        ).astype(jnp.bfloat16)
        contract_ref[i] = jnp.concatenate(taps[3 * i : 3 * i + 3], axis=1).astype(jnp.bfloat16)
    empty = jnp.zeros((pitch - channels, 3 * channels), jnp.float32)
    by_input = [piece for i in range(3) for piece in (jnp.concatenate(taps[3 * i : 3 * i + 3], axis=1), empty)]
    conv_ref[...] = jnp.concatenate(by_input, axis=0).T.astype(jnp.bfloat16)
    same = lax.broadcasted_iota(jnp.int32, (fields, pitch - channels), 0) == lax.broadcasted_iota(
        jnp.int32, (fields, pitch - channels), 1
    )
    lift = jnp.concatenate([lift_weight_ref[...].astype(jnp.float32), jnp.where(same, 1.0, 0.0)], axis=1)
    lift_ref[...] = lift.T.astype(jnp.bfloat16)
    turned_ref[...] = readout_ref[...].astype(jnp.float32).T.astype(jnp.bfloat16)

    lift_rows(prior_ref, edge_ref, lift_ref[...], feat_ref)
    col = lax.broadcasted_iota(jnp.int32, (channels, width), 1)
    lane = lax.broadcasted_iota(jnp.int32, (channels, 128), 1)
    ends_left = ends_right = jnp.zeros((channels, 128), jnp.float32)
    for y in range(rows):
        parts = dot(conv_ref[...], feat_ref[y * pitch : (y + 3) * pitch, :])
        left = jnp.where(col == 0, 0.0, pltpu.roll(parts[:channels], 1, 1))
        right = jnp.where(col == width - 1, 0.0, pltpu.roll(parts[2 * channels :], width - 1, 1))
        act = parts[channels : 2 * channels] + left + right
        act_ref[y * channels : (y + 1) * channels, :] = act
        hidden_ref[y * channels : (y + 1) * channels, :] = (act * sigmoid(act)).astype(jnp.bfloat16)
        ends_left += pltpu.roll(jnp.where(lane == 0, act[:, :128], 0.0), y, 1)
        ends_right += pltpu.roll(jnp.where(lane == 127, act[:, -128:], 0.0), y + 1, 1)
    ends_ref[:, :128] = ends_left
    ends_ref[:, 128:] = ends_right
    for y in range(rows):
        increment = dot(turned_ref[...], hidden_ref[y * channels : (y + 1) * channels, :])
        by_row_ref[y] = prior_ref[y].astype(jnp.float32) + increment
    forecast_ref[...] = jnp.transpose(by_row_ref[...], (1, 0, 2))


def convolve(prior, edges, lift_weight, kernel, readout):
    rows, fields, width = prior.shape
    channels = kernel.shape[1]
    pitch = channels + 16
    vmem = pl.BlockSpec(memory_space=pltpu.VMEM)
    return pl.pallas_call(
        convolve_kernel,
        out_shape=(
            jax.ShapeDtypeStruct((rows * channels, width), jnp.float32),
            jax.ShapeDtypeStruct((fields, rows, width), jnp.float32),
            jax.ShapeDtypeStruct((channels, 256), jnp.float32),
            jax.ShapeDtypeStruct((pitch, fields), jnp.bfloat16),
            jax.ShapeDtypeStruct((3 * channels, 3 * pitch), jnp.bfloat16),
            jax.ShapeDtypeStruct((3 * channels, 3 * channels), jnp.bfloat16),
            jax.ShapeDtypeStruct((3, channels, 3 * channels), jnp.bfloat16),
            jax.ShapeDtypeStruct((fields, channels), jnp.bfloat16),
        ),
        in_specs=[vmem] * 5,
        out_specs=[vmem] * 8,
        scratch_shapes=[
            pltpu.VMEM(((rows + 2) * pitch, width), jnp.bfloat16),
            pltpu.VMEM((rows * channels, width), jnp.bfloat16),
            pltpu.VMEM((rows, fields, width), jnp.float32),
        ],
        compiler_params=pltpu.CompilerParams(vmem_limit_bytes=VMEM_LIMIT),
        cost_estimate=pl.CostEstimate(
            flops=2 * rows * width * 3 * channels * 3 * pitch,
            bytes_accessed=rows * width * channels * 8,
            transcendentals=rows * width * channels * 2,
        ),
        name="convolve",
    )(prior, edges, lift_weight, kernel, readout)


def finish_kernel(
    old_act_ref,
    old_forecast_ref,
    ends_ref,
    own_ref,
    side_ref,
    lift_ref,
    conv_ref,
    turned_ref,
    act_ref,
    forecast_ref,
    stack_ref,
):
    fields, rows, width = forecast_ref.shape
    channels = ends_ref.shape[0]
    side = dot(lift_ref[...], side_ref[...])
    shifted = [side] + [pltpu.roll(side, 256 - i, 1) for i in (1, 2)]
    stack = jnp.concatenate(shifted, axis=0).astype(jnp.bfloat16)
    stack_ref[...] = stack
    left = ends_ref[:, :128] + dot(conv_ref[:channels, :], stack[:, :128])
    right = ends_ref[:, 128:] + dot(conv_ref[2 * channels :, :], stack[:, 128:])
    hidden = jnp.concatenate([(act * sigmoid(act)).astype(jnp.bfloat16) for act in (left, right)], axis=1)
    forecast = pltpu.roll(own_ref[...].astype(jnp.float32), 255, 1) + dot(turned_ref[...], hidden)

    lane = lax.broadcasted_iota(jnp.int32, (channels, 128), 1)
    for y in range(rows):
        here = slice(y * channels, (y + 1) * channels)
        from_left = pltpu.roll(left, (128 - y) % 128, 1)
        from_right = pltpu.roll(right, 127 - y, 1)
        if width == 128:
            act = jnp.where(lane == 0, from_left, jnp.where(lane == 127, from_right, old_act_ref[here, :]))
            act_ref[here, :] = act
        else:
            act_ref[here, :128] = jnp.where(lane == 0, from_left, old_act_ref[here, :128])
            act_ref[here, -128:] = jnp.where(lane == 127, from_right, old_act_ref[here, -128:])
            if width > 256:
                act_ref[here, 128:-128] = old_act_ref[here, 128:-128]
    col = lax.broadcasted_iota(jnp.int32, (rows, width), 1)
    by_row = forecast.T
    for f in range(fields):
        from_left = jnp.broadcast_to(by_row[:rows, f : f + 1], (rows, width))
        from_right = jnp.broadcast_to(by_row[128 : 128 + rows, f : f + 1], (rows, width))
        forecast_ref[f] = jnp.where(
            col == 0, from_left, jnp.where(col == width - 1, from_right, old_forecast_ref[f])
        )


def finish(act, forecast, ends, own, sides, lift, conv, turned):
    vmem = pl.BlockSpec(memory_space=pltpu.VMEM)
    return pl.pallas_call(
        finish_kernel,
        out_shape=(
            jax.ShapeDtypeStruct(act.shape, jnp.float32),
            jax.ShapeDtypeStruct(forecast.shape, jnp.float32),
            jax.ShapeDtypeStruct((conv.shape[1], 256), jnp.bfloat16),
        ),
        in_specs=[vmem] * 8,
        out_specs=[vmem] * 3,
        input_output_aliases={0: 0, 1: 1},
        compiler_params=pltpu.CompilerParams(vmem_limit_bytes=VMEM_LIMIT),
        cost_estimate=pl.CostEstimate(flops=2 * act.size, bytes_accessed=8 * act.size, transcendentals=0),
        name="finish",
    )(act, forecast, ends, own, sides, lift, conv, turned)


def backward_kernel(
    capacity,
    channels,
    norm,
    arrived_ref,
    prior_ref,
    edge_ref,
    stack_ref,
    lift_ref,
    act_ref,
    forecast_ref,
    readout_ref,
    remapped_ref,
    packed_ref,
    slope_ref,
    moment_ref,
    feat_ref,
    hidden_ref,
    block_ref,
    misfit_ref,
    state_ref,
    before_ref,
    after_ref,
):
    fields, rows, width = remapped_ref.shape
    pitch = lift_ref.shape[0]
    devices = arrived_ref.shape[0]
    per_row = width // 128
    slots = devices * capacity

    lift_rows(prior_ref, edge_ref, lift_ref[...], feat_ref)
    slope_ref[:channels, :] = jnp.zeros((channels, width), jnp.bfloat16)
    slope_ref[(rows + 1) * channels :, :] = jnp.zeros((channels, width), jnp.bfloat16)
    depth = fields * rows
    lane = lax.broadcasted_iota(jnp.int32, (fields, depth), 1)
    spread = jnp.where(lane // rows == lax.broadcasted_iota(jnp.int32, (fields, depth), 0), 1.0, 0.0)
    spread = dot(readout_ref[...], spread.astype(jnp.bfloat16))
    lane = lax.broadcasted_iota(jnp.int32, (channels, depth), 1) % rows
    for y in range(rows):
        block_ref[y * channels : (y + 1) * channels, :] = jnp.where(lane == y, spread, 0.0).astype(jnp.bfloat16)

    labels = []
    for first in range(0, devices, 128 // capacity):
        lane = lax.broadcasted_iota(jnp.int32, (fields, 128), 1) // capacity
        label = None
        for d in range(min(devices, 128 // capacity)):
            mine = arrived_ref[first + d, capacity * fields : (capacity + 1) * fields, :].astype(jnp.float32)
            label = mine if label is None else jnp.where(lane == d, mine, label)
        labels.append(label)
    labels = jnp.concatenate(labels, axis=1).astype(jnp.int32)
    tile_blocks = rows * per_row
    labels = jnp.concatenate([labels] * (tile_blocks // fields), axis=0)
    at = lax.broadcasted_iota(jnp.int32, (tile_blocks, slots), 0)
    hits = jnp.where(labels == (at % rows) * per_row + at // rows, 1.0, 0.0).astype(jnp.bfloat16)
    data = arrived_ref[:, : capacity * fields, :].astype(jnp.float32).reshape(slots, fields, 128)
    data = jnp.transpose(data, (1, 0, 2)).astype(jnp.bfloat16)
    for f in range(0, fields, 2):
        picked = dot(hits, jnp.concatenate([data[f], data[f + 1]], axis=1))
        for g in range(2):
            target = picked[:, g * 128 : (g + 1) * 128].astype(jnp.bfloat16)
            target = jnp.concatenate([target[b * rows : (b + 1) * rows] for b in range(per_row)], axis=1)
            target = target.astype(jnp.float32)
            remapped_ref[f + g] = target
            misfit_ref[f + g] = (forecast_ref[f + g] - target) * norm
    by_row = jnp.transpose(misfit_ref[...], (1, 0, 2))
    empty = jnp.zeros((fields, width), jnp.float32)
    for y in range(rows):
        state_ref[:, y * width : (y + 1) * width] = jnp.concatenate([by_row[y], empty], axis=0).astype(jnp.bfloat16)

    col = lax.broadcasted_iota(jnp.int32, (channels, width), 1)
    lane = lax.broadcasted_iota(jnp.int32, (channels, 128), 1)
    ends_left = ends_right = jnp.zeros((channels, 128), jnp.float32)
    batch = 8
    misfits = misfit_ref[...].reshape(depth, width).astype(jnp.bfloat16)
    for first in range(0, rows, batch):
        latents = dot(block_ref[first * channels : (first + batch) * channels, :], misfits)
        for y in range(first, first + batch):
            here = slice(y * channels, (y + 1) * channels)
            act = act_ref[here, :]
            sig = sigmoid(act)
            hidden_ref[here, :] = (act * sig).astype(jnp.bfloat16)
            latent = latents[(y - first) * channels : (y - first + 1) * channels]
            slope = latent * sig * (1.0 + act * (1.0 - sig))
            slope_ref[(y + 1) * channels : (y + 2) * channels, :] = slope.astype(jnp.bfloat16)
            before = jnp.where(col == width - 1, 0.0, pltpu.roll(slope, width - 1, 1))
            before_ref[here, :] = before.astype(jnp.bfloat16)
            after_ref[here, :] = jnp.where(col == 0, 0.0, pltpu.roll(slope, 1, 1)).astype(jnp.bfloat16)
            ends_left += pltpu.roll(jnp.where(lane == 0, slope[:, :128], 0.0), y, 1)
            ends_right += pltpu.roll(jnp.where(lane == 127, slope[:, -128:], 0.0), y + 1, 1)

    total = None
    for first in range(0, rows, batch):
        span = range(first, first + batch)
        features = jnp.concatenate([feat_ref[y * pitch : (y + 3) * pitch, :] for y in span], axis=1)
        features = jnp.concatenate([features, state_ref[:, first * width : (first + batch) * width]], axis=0)
        others = jnp.concatenate(
            [
                jnp.concatenate([ref[(y + d) * channels : (y + d + 1) * channels, :] for y in span], axis=1)
                for ref, d in ((before_ref, 0), (slope_ref, 1), (after_ref, 0), (hidden_ref, 0))
            ],
            axis=0,
        )
        part = dot_nt(features, others)
        total = part if total is None else total + part
    grad_head = total[3 * pitch : 3 * pitch + fields, 3 * channels :]
    stack = stack_ref[...]
    from_left = dot_nt(stack[:, :128], ends_left.astype(jnp.bfloat16))
    from_right = dot_nt(stack[:, 128:], ends_right.astype(jnp.bfloat16))
    middle = jnp.zeros((3 * pitch, channels), jnp.float32)
    total = total[: 3 * pitch, : 3 * channels] + jnp.concatenate([from_left, middle, from_right], axis=1)
    for i in range(3):
        moment_ref[i] = total[i * pitch + channels : i * pitch + channels + fields, :]
    taps = [total[i * pitch : i * pitch + channels, :] for i in range(3)]
    half = channels // 2
    last = [t[:, 2 * channels :] for t in taps]
    packed = [t[:, : 2 * channels] for t in taps]
    packed.append(jnp.concatenate(last[:2], axis=1))
    packed.append(jnp.concatenate([last[2][:half], last[2][half:]], axis=1))
    packed = jnp.concatenate(packed, axis=0)
    cut = packed.shape[0] // 2
    head = jnp.concatenate([grad_head, jnp.zeros_like(grad_head)], axis=1)
    odd = lax.rem(lax.axis_index("lon"), 2)
    packed_ref[odd] = jnp.concatenate([packed[:cut], head], axis=0)
    packed_ref[1 - odd] = jnp.concatenate([packed[cut:], jnp.zeros_like(head)], axis=0)


def backward(arrived, prior, edges, stack, lift, act, forecast, readout, capacity, norm):
    fields, rows, width = forecast.shape
    channels = readout.shape[0]
    pitch = lift.shape[0]
    packed_rows = (3 * channels + channels + channels // 2) // 2 + fields
    vmem = pl.BlockSpec(memory_space=pltpu.VMEM)
    return pl.pallas_call(
        functools.partial(backward_kernel, capacity, channels, norm),
        out_shape=(
            jax.ShapeDtypeStruct((fields, rows, width), jnp.float32),
            jax.ShapeDtypeStruct((2, packed_rows, 2 * channels), jnp.float32),
            jax.ShapeDtypeStruct(((rows + 2) * channels, width), jnp.bfloat16),
            jax.ShapeDtypeStruct((3, fields, 3 * channels), jnp.float32),
        ),
        in_specs=[vmem] * 8,
        out_specs=[vmem] * 4,
        scratch_shapes=[
            pltpu.VMEM(((rows + 2) * pitch, width), jnp.bfloat16),
            pltpu.VMEM((rows * channels, width), jnp.bfloat16),
            pltpu.VMEM((rows * channels, rows * fields), jnp.bfloat16),
            pltpu.VMEM((fields, rows, width), jnp.float32),
            pltpu.VMEM((2 * fields, rows * width), jnp.bfloat16),
            pltpu.VMEM((rows * channels, width), jnp.bfloat16),
            pltpu.VMEM((rows * channels, width), jnp.bfloat16),
        ],
        compiler_params=pltpu.CompilerParams(vmem_limit_bytes=VMEM_LIMIT),
        cost_estimate=pl.CostEstimate(
            flops=2 * rows * width * 3 * channels * 3 * pitch,
            bytes_accessed=rows * width * channels * 8,
            transcendentals=0,
        ),
        name="backward",
    )(arrived, prior, edges, stack, lift, act, forecast, readout)


def lift_gradient_kernel(slope_ref, prior_ref, back_ref, contract_ref, moment_ref, out_ref, delta_ref):
    rows, fields, width = prior_ref.shape
    channels = contract_ref.shape[1]
    col = lax.broadcasted_iota(jnp.int32, (fields, width), 1)
    inside = (col > 0) & (col < width - 1)
    delta_ref[:channels, :] = jnp.zeros((channels, width), jnp.bfloat16)
    delta_ref[(rows - 1) * channels :, :] = jnp.zeros((channels, width), jnp.bfloat16)
    for y in range(1, rows - 1):
        parts = dot(back_ref[...], slope_ref[y * channels : (y + 3) * channels, :])
        grad = (
            parts[channels : 2 * channels]
            + pltpu.roll(parts[:channels], width - 1, 1)
            + pltpu.roll(parts[2 * channels :], 1, 1)
        )
        delta = grad.astype(jnp.bfloat16).astype(jnp.float32) - grad
        delta_ref[y * channels : (y + 1) * channels, :] = delta.astype(jnp.bfloat16)
    crossed = jnp.zeros((channels, fields), jnp.float32)
    batch = 4
    for first in range(0, rows, batch):
        span = range(first, first + batch)
        states = [jnp.where(inside, prior_ref[y].astype(jnp.float32), 0.0).astype(jnp.bfloat16) for y in span]
        states = jnp.concatenate(states, axis=1)
        deltas = jnp.concatenate([delta_ref[y * channels : (y + 1) * channels, :] for y in span], axis=1)
        crossed += dot_nt(deltas, states)
    grad_lift = crossed.T
    for i in range(3):
        rest, pieces = moment_ref[i], []
        for _ in range(3):
            pieces.append(rest.astype(jnp.bfloat16).astype(jnp.float32))
            rest = rest - pieces[-1]
        part = dot_nt(jnp.concatenate(pieces, axis=0).astype(jnp.bfloat16), contract_ref[i])
        grad_lift += part[:fields] + part[fields : 2 * fields] + part[2 * fields :]
    out_ref[...] = jnp.zeros_like(out_ref)
    out_ref[-fields:, channels:] = grad_lift


def lift_gradient(slope, prior, back, contract, moment, packed_rows):
    rows, fields, width = prior.shape
    channels = contract.shape[1]
    vmem = pl.BlockSpec(memory_space=pltpu.VMEM)
    return pl.pallas_call(
        lift_gradient_kernel,
        out_shape=jax.ShapeDtypeStruct((packed_rows, 2 * channels), jnp.float32),
        in_specs=[vmem] * 5,
        out_specs=vmem,
        scratch_shapes=[pltpu.VMEM((rows * channels, width), jnp.bfloat16)],
        compiler_params=pltpu.CompilerParams(vmem_limit_bytes=VMEM_LIMIT),
        cost_estimate=pl.CostEstimate(
            flops=2 * rows * width * 9 * channels * channels, bytes_accessed=slope.size * 2, transcendentals=0
        ),
        name="lift_gradient",
    )(slope, prior, back, contract, moment)


def unpack_kernel(channels, mine_ref, other_ref, kernel_ref, lift_ref, head_ref):
    odd = lax.rem(lax.axis_index("lon"), 2) == 1
    fields = lift_ref.shape[0]
    mine, other = mine_ref[-fields:, :], other_ref[-fields:, :]
    lift_ref[...] = (mine + other)[:, channels:]
    head_ref[...] = jnp.where(odd, other, mine)[:, :channels]
    mine, other = mine_ref[:-fields, :], other_ref[:-fields, :]
    packed = jnp.concatenate([jnp.where(odd, other, mine), jnp.where(odd, mine, other)], axis=0)
    half = channels // 2
    for i in range(3):
        block = packed[i * channels : (i + 1) * channels]
        kernel_ref[3 * i] = block[:, :channels]
        kernel_ref[3 * i + 1] = block[:, channels:]
    block = packed[3 * channels : 4 * channels]
    kernel_ref[2] = block[:, :channels]
    kernel_ref[5] = block[:, channels:]
    block = packed[4 * channels : 4 * channels + half]
    kernel_ref[8, :half] = block[:, :channels]
    kernel_ref[8, half:] = block[:, channels:]


def unpack(mine, other, channels, fields):
    return pl.pallas_call(
        functools.partial(unpack_kernel, channels),
        out_shape=(
            jax.ShapeDtypeStruct((9, channels, channels), jnp.float32),
            jax.ShapeDtypeStruct((fields, channels), jnp.float32),
            jax.ShapeDtypeStruct((fields, channels), jnp.float32),
        ),
        compiler_params=pltpu.CompilerParams(vmem_limit_bytes=VMEM_LIMIT),
        name="unpack",
    )(mine, other)


def swap(x, axis, bit):
    return lax.ppermute(x, axis, [(i, i ^ bit) for i in range(lax.axis_size(axis))])


def sum_over(x, axis, low, high):
    if high // low == 4:
        a, b, c = (swap(x, axis, k * low) for k in (1, 2, 3))
        return (x + a) + (b + c)
    bit = low
    while bit < high:
        x = x + swap(x, axis, bit)
        bit *= 2
    return x


def pair_swap(even_sends, odd_sends, axis, periodic):
    count = lax.axis_size(axis)
    even = lax.rem(lax.axis_index(axis), 2) == 0
    inner = [(i, i ^ 1) for i in range(count)]
    outer = []
    for i in range(1, count, 2):
        if i + 1 < count or periodic:
            outer += [(i, (i + 1) % count), ((i + 1) % count, i)]
    got_inner = lax.ppermute(jnp.where(even, odd_sends, even_sends), axis, inner)
    got_outer = lax.ppermute(jnp.where(even, even_sends, odd_sends), axis, outer)
    return jnp.where(even, got_outer, got_inner), jnp.where(even, got_inner, got_outer)


def per_device(
    source,
    intersection_weight,
    dest_tile,
    dest_row,
    prior_state,
    lift_weight,
    kernel,
    readout_weights,
):
    face_count = lax.axis_size("face")
    lon_count = lax.axis_size("lon")
    devices = face_count * lon_count
    src_blocks, intersections = dest_tile.shape
    fields, rows, width = prior_state.shape
    channels = kernel.shape[1]
    capacity = max(2, 2 * src_blocks * intersections // devices)
    norm = 1.0 / math.sqrt(rows * face_count * width * lon_count)

    outgoing = regrid(source, intersection_weight, dest_tile, dest_row, devices, capacity)
    outgoing, prior_state, kernel, lift_weight, readout_weights = lax.optimization_barrier(
        (outgoing, prior_state, kernel, lift_weight, readout_weights)
    )
    arrived = lax.all_to_all(outgoing, ("face", "lon"), split_axis=0, concat_axis=0, tiled=True)
    arrived = arrived.reshape(devices, (capacity + 1) * fields, source.shape[2])

    prior = prior_state.transpose(1, 0, 2)
    top, bottom = pair_swap(prior[0], prior[rows - 1], "face", False)
    columns = [
        jnp.pad(
            jnp.concatenate([top[:, at : at + 1], prior_state[:, :, at], bottom[:, at : at + 1]], axis=1),
            ((0, 0), (0, 128 - rows - 2)),
        )
        for at in (0, width - 1)
    ]
    left, right = pair_swap(columns[0], columns[1], "lon", True)

    edges = jnp.stack([top, bottom])
    sides = jnp.concatenate([left, right], axis=1)
    act, forecast, ends, lift, conv, back, contract, turned = convolve(
        prior, edges, lift_weight, kernel, readout_weights
    )
    own = jnp.concatenate(columns, axis=1)
    act, forecast, stack = finish(act, forecast, ends, own, sides, lift, conv, turned)
    remapped, packed, slope, moment = backward(
        arrived, prior, edges, stack, lift, act, forecast, readout_weights, capacity, norm
    )
    lift_part = lift_gradient(slope, prior, back, contract, moment, packed.shape[1])
    part = packed[0] + swap(packed[1], "lon", 1) + lift_part
    part = sum_over(part, "face", 1, face_count)
    part, remapped, estimate = lax.optimization_barrier(
        (part, remapped.astype(jnp.bfloat16), forecast.astype(jnp.bfloat16))
    )
    part = sum_over(part, "lon", 2, lon_count)
    grad_kernel, grad_lift, grad_head = unpack(part, swap(part, "lon", 1), channels, fields)
    return (
        remapped,
        estimate,
        grad_lift,
        grad_kernel,
        grad_head.T,
    )


def solution(mesh):
    return jax.shard_map(
        per_device,
        mesh=mesh,
        in_specs=(
            P(("face", "lon"), None, None),
            P(("face", "lon"), None, None, None),
            P(("face", "lon"), None),
            P(("face", "lon"), None),
            P(None, "face", "lon"),
            P(),
            P(),
            P(),
        ),
        out_specs=(P(None, "face", "lon"), P(None, "face", "lon"), P(), P(), P()),
        check_vma=False,
    )
```

```python
import functools
import math

import jax
import jax.numpy as jnp
from jax import lax
from jax.experimental import pallas as pl
from jax.experimental.pallas import tpu as pltpu
from jax.sharding import PartitionSpec as P

NT = (((1,), (1,)), ((), ()))
VMEM_LIMIT = 24 * 1024 * 1024
REGRID_VMEM = 60 * 1024 * 1024


def dot(a, b):
    return jnp.dot(a, b, preferred_element_type=jnp.float32)


def dot_nt(a, b):
    return lax.dot_general(a, b, NT, preferred_element_type=jnp.float32)


def regrid_kernel(
    capacity,
    tile_hbm,
    row_hbm,
    src_hbm,
    wts_hbm,
    out_ref,
    tile_ref,
    row_ref,
    src_ref,
    wts_ref,
    count_ref,
    slot_ref,
    head_ref,
    sems,
):
    blocks, fields, width = src_ref.shape
    intersections = wts_ref.shape[1]
    devices = out_ref.shape[0]
    chunks = sems.shape[0] - 3
    chunk = blocks // chunks
    copies = [
        pltpu.make_async_copy(
            wts_hbm.at[pl.ds(i * chunk, chunk)], wts_ref.at[pl.ds(i * chunk, chunk)], sems.at[i]
        )
        for i in range(chunks)
    ]
    pairs = ((tile_hbm, tile_ref), (row_hbm, row_ref), (src_hbm, src_ref))
    first = [pltpu.make_async_copy(a, b, sems.at[chunks + i]) for i, (a, b) in enumerate(pairs)]
    for copy in first + copies:
        copy.start()
    head_ref[...] = jnp.full_like(head_ref, -1.0)
    for d in range(devices):
        count_ref[d] = 0
    for copy in first:
        copy.wait()
    slot_of_lane = lax.rem(lax.broadcasted_iota(jnp.int32, (1, width), 1), capacity)
    for s in range(blocks):
        for k in range(intersections):
            tile = tile_ref[k, s]
            slot = count_ref[tile]
            count_ref[tile] = slot + 1
            slot_ref[k, s] = slot
            label = row_ref[k, s].astype(jnp.float32)
            head_ref[pl.ds(tile, 1), :] = jnp.where(slot_of_lane == slot, label, head_ref[pl.ds(tile, 1), :])
    out_ref[...] = jnp.zeros_like(out_ref)
    for d in range(devices):
        out_ref[d, capacity] = jnp.broadcast_to(head_ref[d : d + 1, :], (fields, width)).astype(jnp.bfloat16)
    for i in range(chunks):
        copies[i].wait()
        for s in range(i * chunk, (i + 1) * chunk):
            block = src_ref[s]
            for pair in range(0, intersections, 2):
                both = range(pair, min(pair + 2, intersections))
                contrib = dot(block, jnp.concatenate([wts_ref[s, k] for k in both], axis=1)).astype(jnp.bfloat16)
                for k in both:
                    out_ref[tile_ref[k, s], slot_ref[k, s]] = contrib[:, (k - pair) * width : (k - pair + 1) * width]


def regrid(source, weights, dest_tile, dest_row, devices, capacity):
    blocks, fields, width = source.shape
    intersections = weights.shape[1]
    chunks = math.gcd(blocks, 4)
    vmem = pl.BlockSpec(memory_space=pltpu.VMEM)
    return pl.pallas_call(
        functools.partial(regrid_kernel, capacity),
        out_shape=jax.ShapeDtypeStruct((devices, capacity + 1, fields, width), jnp.bfloat16),
        in_specs=[pl.BlockSpec(memory_space=pl.ANY)] * 4,
        out_specs=vmem,
        scratch_shapes=[
            pltpu.SMEM((intersections, blocks), jnp.int32),
            pltpu.SMEM((intersections, blocks), jnp.int32),
            pltpu.VMEM(source.shape, jnp.bfloat16),
            pltpu.VMEM(weights.shape, jnp.bfloat16),
            pltpu.SMEM((devices,), jnp.int32),
            pltpu.SMEM((intersections, blocks), jnp.int32),
            pltpu.VMEM((devices, width), jnp.float32),
            pltpu.SemaphoreType.DMA((chunks + 3,)),
        ],
        compiler_params=pltpu.CompilerParams(vmem_limit_bytes=REGRID_VMEM),
        cost_estimate=pl.CostEstimate(
            flops=2 * weights.size * fields, bytes_accessed=2 * weights.size, transcendentals=0
        ),
        name="regrid",
    )(dest_tile.T, dest_row.T, source, weights)


def lift_rows(prior_ref, edge_ref, lift, feat_ref):
    rows = prior_ref.shape[0]
    pitch = lift.shape[0]
    for at in range(rows + 2):
        values = edge_ref[0] if at == 0 else edge_ref[1] if at == rows + 1 else prior_ref[at - 1]
        feat_ref[at * pitch : (at + 1) * pitch, :] = dot(lift, values).astype(jnp.bfloat16)


def convolve_kernel(
    prior_ref,
    edge_ref,
    lift_weight_ref,
    kernel_ref,
    readout_ref,
    act_ref,
    forecast_ref,
    ends_ref,
    lift_ref,
    conv_ref,
    back_ref,
    contract_ref,
    turned_ref,
    feat_ref,
    hidden_ref,
    by_row_ref,
):
    rows, fields, width = prior_ref.shape
    channels = kernel_ref.shape[1]
    pitch = lift_ref.shape[0]

    taps = [kernel_ref[t].astype(jnp.float32) for t in range(9)]
    for i in range(3):
        back_ref[i * channels : (i + 1) * channels, :] = jnp.concatenate(
            [taps[6 + i], taps[3 + i], taps[i]], axis=1
        ).astype(jnp.bfloat16)
        contract_ref[i] = jnp.concatenate(taps[3 * i : 3 * i + 3], axis=1).astype(jnp.bfloat16)
    empty = jnp.zeros((pitch - channels, 3 * channels), jnp.float32)
    by_input = [piece for i in range(3) for piece in (jnp.concatenate(taps[3 * i : 3 * i + 3], axis=1), empty)]
    conv_ref[...] = jnp.concatenate(by_input, axis=0).T.astype(jnp.bfloat16)
    same = lax.broadcasted_iota(jnp.int32, (fields, pitch - channels), 0) == lax.broadcasted_iota(
        jnp.int32, (fields, pitch - channels), 1
    )
    lift = jnp.concatenate([lift_weight_ref[...].astype(jnp.float32), jnp.where(same, 1.0, 0.0)], axis=1)
    lift_ref[...] = lift.T.astype(jnp.bfloat16)
    turned_ref[...] = readout_ref[...].astype(jnp.float32).T.astype(jnp.bfloat16)

    lift_rows(prior_ref, edge_ref, lift_ref[...], feat_ref)
    col = lax.broadcasted_iota(jnp.int32, (channels, width), 1)
    lane = lax.broadcasted_iota(jnp.int32, (channels, 128), 1)
    ends_left = ends_right = jnp.zeros((channels, 128), jnp.float32)
    for y in range(rows):
        parts = dot(conv_ref[...], feat_ref[y * pitch : (y + 3) * pitch, :])
        left = jnp.where(col == 0, 0.0, pltpu.roll(parts[:channels], 1, 1))
        right = jnp.where(col == width - 1, 0.0, pltpu.roll(parts[2 * channels :], width - 1, 1))
        act = parts[channels : 2 * channels] + left + right
        act_ref[y * channels : (y + 1) * channels, :] = act
        hidden_ref[y * channels : (y + 1) * channels, :] = (act * lax.logistic(act)).astype(jnp.bfloat16)
        ends_left += pltpu.roll(jnp.where(lane == 0, act[:, :128], 0.0), y, 1)
        ends_right += pltpu.roll(jnp.where(lane == 127, act[:, -128:], 0.0), y + 1, 1)
    ends_ref[:, :128] = ends_left
    ends_ref[:, 128:] = ends_right
    for y in range(rows):
        increment = dot(turned_ref[...], hidden_ref[y * channels : (y + 1) * channels, :])
        by_row_ref[y] = prior_ref[y].astype(jnp.float32) + increment
    forecast_ref[...] = jnp.transpose(by_row_ref[...], (1, 0, 2))


def convolve(prior, edges, lift_weight, kernel, readout):
    rows, fields, width = prior.shape
    channels = kernel.shape[1]
    pitch = channels + 16
    vmem = pl.BlockSpec(memory_space=pltpu.VMEM)
    return pl.pallas_call(
        convolve_kernel,
        out_shape=(
            jax.ShapeDtypeStruct((rows * channels, width), jnp.float32),
            jax.ShapeDtypeStruct((fields, rows, width), jnp.float32),
            jax.ShapeDtypeStruct((channels, 256), jnp.float32),
            jax.ShapeDtypeStruct((pitch, fields), jnp.bfloat16),
            jax.ShapeDtypeStruct((3 * channels, 3 * pitch), jnp.bfloat16),
            jax.ShapeDtypeStruct((3 * channels, 3 * channels), jnp.bfloat16),
            jax.ShapeDtypeStruct((3, channels, 3 * channels), jnp.bfloat16),
            jax.ShapeDtypeStruct((fields, channels), jnp.bfloat16),
        ),
        in_specs=[vmem] * 5,
        out_specs=[vmem] * 8,
        scratch_shapes=[
            pltpu.VMEM(((rows + 2) * pitch, width), jnp.bfloat16),
            pltpu.VMEM((rows * channels, width), jnp.bfloat16),
            pltpu.VMEM((rows, fields, width), jnp.float32),
        ],
        compiler_params=pltpu.CompilerParams(vmem_limit_bytes=VMEM_LIMIT),
        cost_estimate=pl.CostEstimate(
            flops=2 * rows * width * 3 * channels * 3 * pitch,
            bytes_accessed=rows * width * channels * 8,
            transcendentals=rows * width * channels * 2,
        ),
        name="convolve",
    )(prior, edges, lift_weight, kernel, readout)


def finish_kernel(
    old_act_ref,
    old_forecast_ref,
    ends_ref,
    own_ref,
    side_ref,
    lift_ref,
    conv_ref,
    turned_ref,
    act_ref,
    forecast_ref,
    stack_ref,
):
    fields, rows, width = forecast_ref.shape
    channels = ends_ref.shape[0]
    side = dot(lift_ref[...], side_ref[...])
    shifted = [side] + [pltpu.roll(side, 256 - i, 1) for i in (1, 2)]
    stack = jnp.concatenate(shifted, axis=0).astype(jnp.bfloat16)
    stack_ref[...] = stack
    left = ends_ref[:, :128] + dot(conv_ref[:channels, :], stack[:, :128])
    right = ends_ref[:, 128:] + dot(conv_ref[2 * channels :, :], stack[:, 128:])
    hidden = jnp.concatenate([(act * lax.logistic(act)).astype(jnp.bfloat16) for act in (left, right)], axis=1)
    forecast = pltpu.roll(own_ref[...].astype(jnp.float32), 255, 1) + dot(turned_ref[...], hidden)

    lane = lax.broadcasted_iota(jnp.int32, (channels, 128), 1)
    for y in range(rows):
        here = slice(y * channels, (y + 1) * channels)
        from_left = pltpu.roll(left, (128 - y) % 128, 1)
        from_right = pltpu.roll(right, 127 - y, 1)
        if width == 128:
            act = jnp.where(lane == 0, from_left, jnp.where(lane == 127, from_right, old_act_ref[here, :]))
            act_ref[here, :] = act
        else:
            act_ref[here, :128] = jnp.where(lane == 0, from_left, old_act_ref[here, :128])
            act_ref[here, -128:] = jnp.where(lane == 127, from_right, old_act_ref[here, -128:])
            if width > 256:
                act_ref[here, 128:-128] = old_act_ref[here, 128:-128]
    col = lax.broadcasted_iota(jnp.int32, (rows, width), 1)
    by_row = forecast.T
    for f in range(fields):
        from_left = jnp.broadcast_to(by_row[:rows, f : f + 1], (rows, width))
        from_right = jnp.broadcast_to(by_row[128 : 128 + rows, f : f + 1], (rows, width))
        forecast_ref[f] = jnp.where(
            col == 0, from_left, jnp.where(col == width - 1, from_right, old_forecast_ref[f])
        )


def finish(act, forecast, ends, own, sides, lift, conv, turned):
    vmem = pl.BlockSpec(memory_space=pltpu.VMEM)
    return pl.pallas_call(
        finish_kernel,
        out_shape=(
            jax.ShapeDtypeStruct(act.shape, jnp.float32),
            jax.ShapeDtypeStruct(forecast.shape, jnp.float32),
            jax.ShapeDtypeStruct((conv.shape[1], 256), jnp.bfloat16),
        ),
        in_specs=[vmem] * 8,
        out_specs=[vmem] * 3,
        input_output_aliases={0: 0, 1: 1},
        compiler_params=pltpu.CompilerParams(vmem_limit_bytes=VMEM_LIMIT),
        cost_estimate=pl.CostEstimate(flops=2 * act.size, bytes_accessed=8 * act.size, transcendentals=0),
        name="finish",
    )(act, forecast, ends, own, sides, lift, conv, turned)


def backward_kernel(
    capacity,
    channels,
    norm,
    arrived_ref,
    prior_ref,
    edge_ref,
    stack_ref,
    lift_ref,
    act_ref,
    forecast_ref,
    readout_ref,
    remapped_ref,
    packed_ref,
    slope_ref,
    moment_ref,
    feat_ref,
    hidden_ref,
    block_ref,
    misfit_ref,
    state_ref,
    before_ref,
    after_ref,
):
    fields, rows, width = remapped_ref.shape
    pitch = lift_ref.shape[0]
    devices = arrived_ref.shape[0]
    per_row = width // 128
    slots = devices * capacity

    lift_rows(prior_ref, edge_ref, lift_ref[...], feat_ref)
    slope_ref[:channels, :] = jnp.zeros((channels, width), jnp.bfloat16)
    slope_ref[(rows + 1) * channels :, :] = jnp.zeros((channels, width), jnp.bfloat16)
    depth = fields * rows
    lane = lax.broadcasted_iota(jnp.int32, (fields, depth), 1)
    spread = jnp.where(lane // rows == lax.broadcasted_iota(jnp.int32, (fields, depth), 0), 1.0, 0.0)
    spread = dot(readout_ref[...], spread.astype(jnp.bfloat16))
    lane = lax.broadcasted_iota(jnp.int32, (channels, depth), 1) % rows
    for y in range(rows):
        block_ref[y * channels : (y + 1) * channels, :] = jnp.where(lane == y, spread, 0.0).astype(jnp.bfloat16)

    labels = []
    for first in range(0, devices, 128 // capacity):
        lane = lax.broadcasted_iota(jnp.int32, (fields, 128), 1) // capacity
        label = None
        for d in range(min(devices, 128 // capacity)):
            mine = arrived_ref[first + d, capacity * fields : (capacity + 1) * fields, :].astype(jnp.float32)
            label = mine if label is None else jnp.where(lane == d, mine, label)
        labels.append(label)
    labels = jnp.concatenate(labels, axis=1).astype(jnp.int32)
    tile_blocks = rows * per_row
    labels = jnp.concatenate([labels] * (tile_blocks // fields), axis=0)
    at = lax.broadcasted_iota(jnp.int32, (tile_blocks, slots), 0)
    hits = jnp.where(labels == (at % rows) * per_row + at // rows, 1.0, 0.0).astype(jnp.bfloat16)
    data = arrived_ref[:, : capacity * fields, :].astype(jnp.float32).reshape(slots, fields, 128)
    data = jnp.transpose(data, (1, 0, 2)).astype(jnp.bfloat16)
    for f in range(0, fields, 2):
        picked = dot(hits, jnp.concatenate([data[f], data[f + 1]], axis=1))
        for g in range(2):
            target = picked[:, g * 128 : (g + 1) * 128].astype(jnp.bfloat16)
            target = jnp.concatenate([target[b * rows : (b + 1) * rows] for b in range(per_row)], axis=1)
            target = target.astype(jnp.float32)
            remapped_ref[f + g] = target
            misfit_ref[f + g] = (forecast_ref[f + g] - target) * norm
    by_row = jnp.transpose(misfit_ref[...], (1, 0, 2))
    empty = jnp.zeros((fields, width), jnp.float32)
    for y in range(rows):
        state_ref[:, y * width : (y + 1) * width] = jnp.concatenate([by_row[y], empty], axis=0).astype(jnp.bfloat16)

    col = lax.broadcasted_iota(jnp.int32, (channels, width), 1)
    lane = lax.broadcasted_iota(jnp.int32, (channels, 128), 1)
    ends_left = ends_right = jnp.zeros((channels, 128), jnp.float32)
    batch = 8
    misfits = misfit_ref[...].reshape(depth, width).astype(jnp.bfloat16)
    for first in range(0, rows, batch):
        latents = dot(block_ref[first * channels : (first + batch) * channels, :], misfits)
        for y in range(first, first + batch):
            here = slice(y * channels, (y + 1) * channels)
            act = act_ref[here, :]
            sig = lax.logistic(act)
            silu = act * sig
            hidden_ref[here, :] = silu.astype(jnp.bfloat16)
            latent = latents[(y - first) * channels : (y - first + 1) * channels]
            slope = latent * (sig + silu * (1.0 - sig))
            slope_ref[(y + 1) * channels : (y + 2) * channels, :] = slope.astype(jnp.bfloat16)
            before = jnp.where(col == width - 1, 0.0, pltpu.roll(slope, width - 1, 1))
            before_ref[here, :] = before.astype(jnp.bfloat16)
            after_ref[here, :] = jnp.where(col == 0, 0.0, pltpu.roll(slope, 1, 1)).astype(jnp.bfloat16)
            ends_left += pltpu.roll(jnp.where(lane == 0, slope[:, :128], 0.0), y, 1)
            ends_right += pltpu.roll(jnp.where(lane == 127, slope[:, -128:], 0.0), y + 1, 1)

    total = None
    for first in range(0, rows, batch):
        span = range(first, first + batch)
        features = jnp.concatenate([feat_ref[y * pitch : (y + 3) * pitch, :] for y in span], axis=1)
        features = jnp.concatenate([features, state_ref[:, first * width : (first + batch) * width]], axis=0)
        others = jnp.concatenate(
            [
                jnp.concatenate([ref[(y + d) * channels : (y + d + 1) * channels, :] for y in span], axis=1)
                for ref, d in ((before_ref, 0), (slope_ref, 1), (after_ref, 0), (hidden_ref, 0))
            ],
            axis=0,
        )
        part = dot_nt(features, others)
        total = part if total is None else total + part
    grad_head = total[3 * pitch : 3 * pitch + fields, 3 * channels :]
    stack = stack_ref[...]
    from_left = dot_nt(stack[:, :128], ends_left.astype(jnp.bfloat16))
    from_right = dot_nt(stack[:, 128:], ends_right.astype(jnp.bfloat16))
    middle = jnp.zeros((3 * pitch, channels), jnp.float32)
    total = total[: 3 * pitch, : 3 * channels] + jnp.concatenate([from_left, middle, from_right], axis=1)
    for i in range(3):
        moment_ref[i] = total[i * pitch + channels : i * pitch + channels + fields, :]
    taps = [total[i * pitch : i * pitch + channels, :] for i in range(3)]
    half = channels // 2
    last = [t[:, 2 * channels :] for t in taps]
    packed = [t[:, : 2 * channels] for t in taps]
    packed.append(jnp.concatenate(last[:2], axis=1))
    packed.append(jnp.concatenate([last[2][:half], last[2][half:]], axis=1))
    packed = jnp.concatenate(packed, axis=0)
    cut = packed.shape[0] // 2
    head = jnp.concatenate([grad_head, jnp.zeros_like(grad_head)], axis=1)
    odd = lax.rem(lax.axis_index("lon"), 2)
    packed_ref[odd] = jnp.concatenate([packed[:cut], head], axis=0)
    packed_ref[1 - odd] = jnp.concatenate([packed[cut:], jnp.zeros_like(head)], axis=0)


def backward(arrived, prior, edges, stack, lift, act, forecast, readout, capacity, norm):
    fields, rows, width = forecast.shape
    channels = readout.shape[0]
    pitch = lift.shape[0]
    packed_rows = (3 * channels + channels + channels // 2) // 2 + fields
    vmem = pl.BlockSpec(memory_space=pltpu.VMEM)
    return pl.pallas_call(
        functools.partial(backward_kernel, capacity, channels, norm),
        out_shape=(
            jax.ShapeDtypeStruct((fields, rows, width), jnp.float32),
            jax.ShapeDtypeStruct((2, packed_rows, 2 * channels), jnp.float32),
            jax.ShapeDtypeStruct(((rows + 2) * channels, width), jnp.bfloat16),
            jax.ShapeDtypeStruct((3, fields, 3 * channels), jnp.float32),
        ),
        in_specs=[vmem] * 8,
        out_specs=[vmem] * 4,
        scratch_shapes=[
            pltpu.VMEM(((rows + 2) * pitch, width), jnp.bfloat16),
            pltpu.VMEM((rows * channels, width), jnp.bfloat16),
            pltpu.VMEM((rows * channels, rows * fields), jnp.bfloat16),
            pltpu.VMEM((fields, rows, width), jnp.float32),
            pltpu.VMEM((2 * fields, rows * width), jnp.bfloat16),
            pltpu.VMEM((rows * channels, width), jnp.bfloat16),
            pltpu.VMEM((rows * channels, width), jnp.bfloat16),
        ],
        compiler_params=pltpu.CompilerParams(vmem_limit_bytes=VMEM_LIMIT),
        cost_estimate=pl.CostEstimate(
            flops=2 * rows * width * 3 * channels * 3 * pitch,
            bytes_accessed=rows * width * channels * 8,
            transcendentals=0,
        ),
        name="backward",
    )(arrived, prior, edges, stack, lift, act, forecast, readout)


def lift_gradient_kernel(slope_ref, prior_ref, back_ref, contract_ref, moment_ref, out_ref, delta_ref):
    rows, fields, width = prior_ref.shape
    channels = contract_ref.shape[1]
    col = lax.broadcasted_iota(jnp.int32, (fields, width), 1)
    inside = (col > 0) & (col < width - 1)
    delta_ref[:channels, :] = jnp.zeros((channels, width), jnp.bfloat16)
    delta_ref[(rows - 1) * channels :, :] = jnp.zeros((channels, width), jnp.bfloat16)
    for y in range(1, rows - 1):
        parts = dot(back_ref[...], slope_ref[y * channels : (y + 3) * channels, :])
        grad = (
            parts[channels : 2 * channels]
            + pltpu.roll(parts[:channels], width - 1, 1)
            + pltpu.roll(parts[2 * channels :], 1, 1)
        )
        delta = grad.astype(jnp.bfloat16).astype(jnp.float32) - grad
        delta_ref[y * channels : (y + 1) * channels, :] = delta.astype(jnp.bfloat16)
    crossed = jnp.zeros((channels, fields), jnp.float32)
    batch = 4
    for first in range(0, rows, batch):
        span = range(first, first + batch)
        states = [jnp.where(inside, prior_ref[y].astype(jnp.float32), 0.0).astype(jnp.bfloat16) for y in span]
        states = jnp.concatenate(states, axis=1)
        deltas = jnp.concatenate([delta_ref[y * channels : (y + 1) * channels, :] for y in span], axis=1)
        crossed += dot_nt(deltas, states)
    grad_lift = crossed.T
    for i in range(3):
        rest, pieces = moment_ref[i], []
        for _ in range(3):
            pieces.append(rest.astype(jnp.bfloat16).astype(jnp.float32))
            rest = rest - pieces[-1]
        part = dot_nt(jnp.concatenate(pieces, axis=0).astype(jnp.bfloat16), contract_ref[i])
        grad_lift += part[:fields] + part[fields : 2 * fields] + part[2 * fields :]
    out_ref[...] = jnp.zeros_like(out_ref)
    out_ref[-fields:, channels:] = grad_lift


def lift_gradient(slope, prior, back, contract, moment, packed_rows):
    rows, fields, width = prior.shape
    channels = contract.shape[1]
    vmem = pl.BlockSpec(memory_space=pltpu.VMEM)
    return pl.pallas_call(
        lift_gradient_kernel,
        out_shape=jax.ShapeDtypeStruct((packed_rows, 2 * channels), jnp.float32),
        in_specs=[vmem] * 5,
        out_specs=vmem,
        scratch_shapes=[pltpu.VMEM((rows * channels, width), jnp.bfloat16)],
        compiler_params=pltpu.CompilerParams(vmem_limit_bytes=VMEM_LIMIT),
        cost_estimate=pl.CostEstimate(
            flops=2 * rows * width * 9 * channels * channels, bytes_accessed=slope.size * 2, transcendentals=0
        ),
        name="lift_gradient",
    )(slope, prior, back, contract, moment)


def unpack_kernel(channels, mine_ref, other_ref, kernel_ref, lift_ref, head_ref):
    odd = lax.rem(lax.axis_index("lon"), 2) == 1
    fields = lift_ref.shape[0]
    mine, other = mine_ref[-fields:, :], other_ref[-fields:, :]
    lift_ref[...] = (mine + other)[:, channels:]
    head_ref[...] = jnp.where(odd, other, mine)[:, :channels]
    mine, other = mine_ref[:-fields, :], other_ref[:-fields, :]
    packed = jnp.concatenate([jnp.where(odd, other, mine), jnp.where(odd, mine, other)], axis=0)
    half = channels // 2
    for i in range(3):
        block = packed[i * channels : (i + 1) * channels]
        kernel_ref[3 * i] = block[:, :channels]
        kernel_ref[3 * i + 1] = block[:, channels:]
    block = packed[3 * channels : 4 * channels]
    kernel_ref[2] = block[:, :channels]
    kernel_ref[5] = block[:, channels:]
    block = packed[4 * channels : 4 * channels + half]
    kernel_ref[8, :half] = block[:, :channels]
    kernel_ref[8, half:] = block[:, channels:]


def unpack(mine, other, channels, fields):
    return pl.pallas_call(
        functools.partial(unpack_kernel, channels),
        out_shape=(
            jax.ShapeDtypeStruct((9, channels, channels), jnp.float32),
            jax.ShapeDtypeStruct((fields, channels), jnp.float32),
            jax.ShapeDtypeStruct((fields, channels), jnp.float32),
        ),
        compiler_params=pltpu.CompilerParams(vmem_limit_bytes=VMEM_LIMIT),
        name="unpack",
    )(mine, other)


def swap(x, axis, bit):
    return lax.ppermute(x, axis, [(i, i ^ bit) for i in range(lax.axis_size(axis))])


def sum_over(x, axis, low, high):
    if high // low == 4:
        a, b, c = (swap(x, axis, k * low) for k in (1, 2, 3))
        return (x + a) + (b + c)
    bit = low
    while bit < high:
        x = x + swap(x, axis, bit)
        bit *= 2
    return x


def pair_swap(even_sends, odd_sends, axis, periodic):
    count = lax.axis_size(axis)
    even = lax.rem(lax.axis_index(axis), 2) == 0
    inner = [(i, i ^ 1) for i in range(count)]
    outer = []
    for i in range(1, count, 2):
        if i + 1 < count or periodic:
            outer += [(i, (i + 1) % count), ((i + 1) % count, i)]
    got_inner = lax.ppermute(jnp.where(even, odd_sends, even_sends), axis, inner)
    got_outer = lax.ppermute(jnp.where(even, even_sends, odd_sends), axis, outer)
    return jnp.where(even, got_outer, got_inner), jnp.where(even, got_inner, got_outer)


def per_device(
    source,
    intersection_weight,
    dest_tile,
    dest_row,
    prior_state,
    lift_weight,
    kernel,
    readout_weights,
):
    face_count = lax.axis_size("face")
    lon_count = lax.axis_size("lon")
    devices = face_count * lon_count
    src_blocks, intersections = dest_tile.shape
    fields, rows, width = prior_state.shape
    channels = kernel.shape[1]
    capacity = max(2, 2 * src_blocks * intersections // devices)
    norm = 1.0 / math.sqrt(rows * face_count * width * lon_count)

    outgoing = regrid(source, intersection_weight, dest_tile, dest_row, devices, capacity)
    outgoing, prior_state, kernel, lift_weight, readout_weights = lax.optimization_barrier(
        (outgoing, prior_state, kernel, lift_weight, readout_weights)
    )
    arrived = lax.all_to_all(outgoing, ("face", "lon"), split_axis=0, concat_axis=0, tiled=True)
    arrived = arrived.reshape(devices, (capacity + 1) * fields, source.shape[2])

    prior = prior_state.transpose(1, 0, 2)
    top, bottom = pair_swap(prior[0], prior[rows - 1], "face", False)
    columns = [
        jnp.pad(
            jnp.concatenate([top[:, at : at + 1], prior_state[:, :, at], bottom[:, at : at + 1]], axis=1),
            ((0, 0), (0, 128 - rows - 2)),
        )
        for at in (0, width - 1)
    ]
    left, right = pair_swap(columns[0], columns[1], "lon", True)

    edges = jnp.stack([top, bottom])
    sides = jnp.concatenate([left, right], axis=1)
    act, forecast, ends, lift, conv, back, contract, turned = convolve(
        prior, edges, lift_weight, kernel, readout_weights
    )
    own = jnp.concatenate(columns, axis=1)
    act, forecast, stack = finish(act, forecast, ends, own, sides, lift, conv, turned)
    remapped, packed, slope, moment = backward(
        arrived, prior, edges, stack, lift, act, forecast, readout_weights, capacity, norm
    )
    lift_part = lift_gradient(slope, prior, back, contract, moment, packed.shape[1])
    part = packed[0] + swap(packed[1], "lon", 1) + lift_part
    part = sum_over(part, "face", 1, face_count)
    part, remapped, estimate = lax.optimization_barrier(
        (part, remapped.astype(jnp.bfloat16), forecast.astype(jnp.bfloat16))
    )
    part = sum_over(part, "lon", 2, lon_count)
    grad_kernel, grad_lift, grad_head = unpack(part, swap(part, "lon", 1), channels, fields)
    return (
        remapped,
        estimate,
        grad_lift,
        grad_kernel,
        grad_head.T,
    )


def solution(mesh):
    return jax.shard_map(
        per_device,
        mesh=mesh,
        in_specs=(
            P(("face", "lon"), None, None),
            P(("face", "lon"), None, None, None),
            P(("face", "lon"), None),
            P(("face", "lon"), None),
            P(None, "face", "lon"),
            P(),
            P(),
            P(),
        ),
        out_specs=(P(None, "face", "lon"), P(None, "face", "lon"), P(), P(), P()),
        check_vma=False,
    )
```

```python
import functools
import math

import jax
import jax.numpy as jnp
from jax import lax
from jax.experimental import pallas as pl
from jax.experimental.pallas import tpu as pltpu
from jax.sharding import PartitionSpec as P

NT = (((1,), (1,)), ((), ()))
VMEM_LIMIT = 24 * 1024 * 1024
REGRID_VMEM = 60 * 1024 * 1024


def dot(a, b):
    return jnp.dot(a, b, preferred_element_type=jnp.float32)


def dot_nt(a, b):
    return lax.dot_general(a, b, NT, preferred_element_type=jnp.float32)


def regrid_kernel(
    capacity,
    tile_hbm,
    row_hbm,
    src_hbm,
    wts_hbm,
    out_ref,
    tile_ref,
    row_ref,
    src_ref,
    wts_ref,
    count_ref,
    slot_ref,
    head_ref,
    sems,
):
    blocks, fields, width = src_ref.shape
    intersections = wts_ref.shape[1]
    devices = out_ref.shape[0]
    chunks = sems.shape[0] - 3
    chunk = blocks // chunks
    copies = [
        pltpu.make_async_copy(
            wts_hbm.at[pl.ds(i * chunk, chunk)], wts_ref.at[pl.ds(i * chunk, chunk)], sems.at[i]
        )
        for i in range(chunks)
    ]
    pairs = ((tile_hbm, tile_ref), (row_hbm, row_ref), (src_hbm, src_ref))
    first = [pltpu.make_async_copy(a, b, sems.at[chunks + i]) for i, (a, b) in enumerate(pairs)]
    for copy in first + copies:
        copy.start()
    head_ref[...] = jnp.full_like(head_ref, -1.0)
    for d in range(devices):
        count_ref[d] = 0
    for copy in first:
        copy.wait()
    slot_of_lane = lax.rem(lax.broadcasted_iota(jnp.int32, (1, width), 1), capacity)
    for s in range(blocks):
        for k in range(intersections):
            tile = tile_ref[k, s]
            slot = count_ref[tile]
            count_ref[tile] = slot + 1
            slot_ref[k, s] = slot
            label = row_ref[k, s].astype(jnp.float32)
            head_ref[pl.ds(tile, 1), :] = jnp.where(slot_of_lane == slot, label, head_ref[pl.ds(tile, 1), :])
    out_ref[...] = jnp.zeros_like(out_ref)
    for d in range(devices):
        out_ref[d, capacity] = jnp.broadcast_to(head_ref[d : d + 1, :], (fields, width)).astype(jnp.bfloat16)
    for i in range(chunks):
        copies[i].wait()
        for s in range(i * chunk, (i + 1) * chunk):
            block = src_ref[s]
            for pair in range(0, intersections, 2):
                both = range(pair, min(pair + 2, intersections))
                contrib = dot(block, jnp.concatenate([wts_ref[s, k] for k in both], axis=1)).astype(jnp.bfloat16)
                for k in both:
                    out_ref[tile_ref[k, s], slot_ref[k, s]] = contrib[:, (k - pair) * width : (k - pair + 1) * width]


def regrid(source, weights, dest_tile, dest_row, devices, capacity):
    blocks, fields, width = source.shape
    intersections = weights.shape[1]
    chunks = math.gcd(blocks, 4)
    vmem = pl.BlockSpec(memory_space=pltpu.VMEM)
    return pl.pallas_call(
        functools.partial(regrid_kernel, capacity),
        out_shape=jax.ShapeDtypeStruct((devices, capacity + 1, fields, width), jnp.bfloat16),
        in_specs=[pl.BlockSpec(memory_space=pl.ANY)] * 4,
        out_specs=vmem,
        scratch_shapes=[
            pltpu.SMEM((intersections, blocks), jnp.int32),
            pltpu.SMEM((intersections, blocks), jnp.int32),
            pltpu.VMEM(source.shape, jnp.bfloat16),
            pltpu.VMEM(weights.shape, jnp.bfloat16),
            pltpu.SMEM((devices,), jnp.int32),
            pltpu.SMEM((intersections, blocks), jnp.int32),
            pltpu.VMEM((devices, width), jnp.float32),
            pltpu.SemaphoreType.DMA((chunks + 3,)),
        ],
        compiler_params=pltpu.CompilerParams(vmem_limit_bytes=REGRID_VMEM),
        cost_estimate=pl.CostEstimate(
            flops=2 * weights.size * fields, bytes_accessed=2 * weights.size, transcendentals=0
        ),
        name="regrid",
    )(dest_tile.T, dest_row.T, source, weights)


def lift_rows(prior_ref, edge_ref, lift, feat_ref):
    rows = prior_ref.shape[0]
    pitch = lift.shape[0]
    for at in range(rows + 2):
        values = edge_ref[0] if at == 0 else edge_ref[1] if at == rows + 1 else prior_ref[at - 1]
        feat_ref[at * pitch : (at + 1) * pitch, :] = dot(lift, values).astype(jnp.bfloat16)


def convolve_kernel(
    prior_ref,
    edge_ref,
    lift_weight_ref,
    kernel_ref,
    readout_ref,
    act_ref,
    forecast_ref,
    ends_ref,
    lift_ref,
    conv_ref,
    back_ref,
    contract_ref,
    turned_ref,
    feat_ref,
    hidden_ref,
    by_row_ref,
):
    rows, fields, width = prior_ref.shape
    channels = kernel_ref.shape[1]
    pitch = lift_ref.shape[0]

    taps = [kernel_ref[t].astype(jnp.float32) for t in range(9)]
    for i in range(3):
        back_ref[i * channels : (i + 1) * channels, :] = jnp.concatenate(
            [taps[6 + i], taps[3 + i], taps[i]], axis=1
        ).astype(jnp.bfloat16)
        contract_ref[i] = jnp.concatenate(taps[3 * i : 3 * i + 3], axis=1).astype(jnp.bfloat16)
    empty = jnp.zeros((pitch - channels, 3 * channels), jnp.float32)
    by_input = [piece for i in range(3) for piece in (jnp.concatenate(taps[3 * i : 3 * i + 3], axis=1), empty)]
    conv_ref[...] = jnp.concatenate(by_input, axis=0).T.astype(jnp.bfloat16)
    same = lax.broadcasted_iota(jnp.int32, (fields, pitch - channels), 0) == lax.broadcasted_iota(
        jnp.int32, (fields, pitch - channels), 1
    )
    lift = jnp.concatenate([lift_weight_ref[...].astype(jnp.float32), jnp.where(same, 1.0, 0.0)], axis=1)
    lift_ref[...] = lift.T.astype(jnp.bfloat16)
    turned_ref[...] = readout_ref[...].astype(jnp.float32).T.astype(jnp.bfloat16)

    lift_rows(prior_ref, edge_ref, lift_ref[...], feat_ref)
    col = lax.broadcasted_iota(jnp.int32, (channels, width), 1)
    lane = lax.broadcasted_iota(jnp.int32, (channels, 128), 1)
    ends_left = ends_right = jnp.zeros((channels, 128), jnp.float32)
    for y in range(rows):
        parts = dot(conv_ref[...], feat_ref[y * pitch : (y + 3) * pitch, :])
        left = jnp.where(col == 0, 0.0, pltpu.roll(parts[:channels], 1, 1))
        right = jnp.where(col == width - 1, 0.0, pltpu.roll(parts[2 * channels :], width - 1, 1))
        act = parts[channels : 2 * channels] + left + right
        act_ref[y * channels : (y + 1) * channels, :] = act
        hidden_ref[y * channels : (y + 1) * channels, :] = (act * lax.logistic(act)).astype(jnp.bfloat16)
        ends_left += pltpu.roll(jnp.where(lane == 0, act[:, :128], 0.0), y, 1)
        ends_right += pltpu.roll(jnp.where(lane == 127, act[:, -128:], 0.0), y + 1, 1)
    ends_ref[:, :128] = ends_left
    ends_ref[:, 128:] = ends_right
    for y in range(rows):
        increment = dot(turned_ref[...], hidden_ref[y * channels : (y + 1) * channels, :])
        by_row_ref[y] = prior_ref[y].astype(jnp.float32) + increment
    forecast_ref[...] = jnp.transpose(by_row_ref[...], (1, 0, 2))


def convolve(prior, edges, lift_weight, kernel, readout):
    rows, fields, width = prior.shape
    channels = kernel.shape[1]
    pitch = channels + 16
    vmem = pl.BlockSpec(memory_space=pltpu.VMEM)
    return pl.pallas_call(
        convolve_kernel,
        out_shape=(
            jax.ShapeDtypeStruct((rows * channels, width), jnp.float32),
            jax.ShapeDtypeStruct((fields, rows, width), jnp.float32),
            jax.ShapeDtypeStruct((channels, 256), jnp.float32),
            jax.ShapeDtypeStruct((pitch, fields), jnp.bfloat16),
            jax.ShapeDtypeStruct((3 * channels, 3 * pitch), jnp.bfloat16),
            jax.ShapeDtypeStruct((3 * channels, 3 * channels), jnp.bfloat16),
            jax.ShapeDtypeStruct((3, channels, 3 * channels), jnp.bfloat16),
            jax.ShapeDtypeStruct((fields, channels), jnp.bfloat16),
        ),
        in_specs=[vmem] * 5,
        out_specs=[vmem] * 8,
        scratch_shapes=[
            pltpu.VMEM(((rows + 2) * pitch, width), jnp.bfloat16),
            pltpu.VMEM((rows * channels, width), jnp.bfloat16),
            pltpu.VMEM((rows, fields, width), jnp.float32),
        ],
        compiler_params=pltpu.CompilerParams(vmem_limit_bytes=VMEM_LIMIT),
        cost_estimate=pl.CostEstimate(
            flops=2 * rows * width * 3 * channels * 3 * pitch,
            bytes_accessed=rows * width * channels * 8,
            transcendentals=rows * width * channels * 2,
        ),
        name="convolve",
    )(prior, edges, lift_weight, kernel, readout)


def finish_kernel(
    old_act_ref,
    old_forecast_ref,
    ends_ref,
    own_ref,
    side_ref,
    lift_ref,
    conv_ref,
    turned_ref,
    act_ref,
    forecast_ref,
    stack_ref,
):
    fields, rows, width = forecast_ref.shape
    channels = ends_ref.shape[0]
    side = dot(lift_ref[...], side_ref[...])
    shifted = [side] + [pltpu.roll(side, 256 - i, 1) for i in (1, 2)]
    stack = jnp.concatenate(shifted, axis=0).astype(jnp.bfloat16)
    stack_ref[...] = stack
    left = ends_ref[:, :128] + dot(conv_ref[:channels, :], stack[:, :128])
    right = ends_ref[:, 128:] + dot(conv_ref[2 * channels :, :], stack[:, 128:])
    hidden = jnp.concatenate([(act * lax.logistic(act)).astype(jnp.bfloat16) for act in (left, right)], axis=1)
    forecast = pltpu.roll(own_ref[...].astype(jnp.float32), 255, 1) + dot(turned_ref[...], hidden)

    lane = lax.broadcasted_iota(jnp.int32, (channels, 128), 1)
    for y in range(rows):
        here = slice(y * channels, (y + 1) * channels)
        from_left = pltpu.roll(left, (128 - y) % 128, 1)
        from_right = pltpu.roll(right, 127 - y, 1)
        if width == 128:
            act = jnp.where(lane == 0, from_left, jnp.where(lane == 127, from_right, old_act_ref[here, :]))
            act_ref[here, :] = act
        else:
            act_ref[here, :128] = jnp.where(lane == 0, from_left, old_act_ref[here, :128])
            act_ref[here, -128:] = jnp.where(lane == 127, from_right, old_act_ref[here, -128:])
            if width > 256:
                act_ref[here, 128:-128] = old_act_ref[here, 128:-128]
    col = lax.broadcasted_iota(jnp.int32, (rows, width), 1)
    by_row = forecast.T
    for f in range(fields):
        from_left = jnp.broadcast_to(by_row[:rows, f : f + 1], (rows, width))
        from_right = jnp.broadcast_to(by_row[128 : 128 + rows, f : f + 1], (rows, width))
        forecast_ref[f] = jnp.where(
            col == 0, from_left, jnp.where(col == width - 1, from_right, old_forecast_ref[f])
        )


def finish(act, forecast, ends, own, sides, lift, conv, turned):
    vmem = pl.BlockSpec(memory_space=pltpu.VMEM)
    return pl.pallas_call(
        finish_kernel,
        out_shape=(
            jax.ShapeDtypeStruct(act.shape, jnp.float32),
            jax.ShapeDtypeStruct(forecast.shape, jnp.float32),
            jax.ShapeDtypeStruct((conv.shape[1], 256), jnp.bfloat16),
        ),
        in_specs=[vmem] * 8,
        out_specs=[vmem] * 3,
        input_output_aliases={0: 0, 1: 1},
        compiler_params=pltpu.CompilerParams(vmem_limit_bytes=VMEM_LIMIT),
        cost_estimate=pl.CostEstimate(flops=2 * act.size, bytes_accessed=8 * act.size, transcendentals=0),
        name="finish",
    )(act, forecast, ends, own, sides, lift, conv, turned)


def backward_kernel(
    capacity,
    channels,
    norm,
    arrived_ref,
    prior_ref,
    edge_ref,
    stack_ref,
    lift_ref,
    act_ref,
    forecast_ref,
    readout_ref,
    remapped_ref,
    packed_ref,
    slope_ref,
    moment_ref,
    feat_ref,
    hidden_ref,
    block_ref,
    misfit_ref,
    state_ref,
    before_ref,
    after_ref,
):
    fields, rows, width = remapped_ref.shape
    pitch = lift_ref.shape[0]
    devices = arrived_ref.shape[0]
    per_row = width // 128
    slots = devices * capacity

    lift_rows(prior_ref, edge_ref, lift_ref[...], feat_ref)
    slope_ref[:channels, :] = jnp.zeros((channels, width), jnp.bfloat16)
    slope_ref[(rows + 1) * channels :, :] = jnp.zeros((channels, width), jnp.bfloat16)
    depth = fields * rows
    lane = lax.broadcasted_iota(jnp.int32, (fields, depth), 1)
    spread = jnp.where(lane // rows == lax.broadcasted_iota(jnp.int32, (fields, depth), 0), 1.0, 0.0)
    spread = dot(readout_ref[...], spread.astype(jnp.bfloat16))
    lane = lax.broadcasted_iota(jnp.int32, (channels, depth), 1) % rows
    for y in range(rows):
        block_ref[y * channels : (y + 1) * channels, :] = jnp.where(lane == y, spread, 0.0).astype(jnp.bfloat16)

    labels = []
    for first in range(0, devices, 128 // capacity):
        lane = lax.broadcasted_iota(jnp.int32, (fields, 128), 1) // capacity
        label = None
        for d in range(min(devices, 128 // capacity)):
            mine = arrived_ref[first + d, capacity * fields : (capacity + 1) * fields, :].astype(jnp.float32)
            label = mine if label is None else jnp.where(lane == d, mine, label)
        labels.append(label)
    labels = jnp.concatenate(labels, axis=1).astype(jnp.int32)
    tile_blocks = rows * per_row
    labels = jnp.concatenate([labels] * (tile_blocks // fields), axis=0)
    at = lax.broadcasted_iota(jnp.int32, (tile_blocks, slots), 0)
    hits = jnp.where(labels == (at % rows) * per_row + at // rows, 1.0, 0.0).astype(jnp.bfloat16)
    data = arrived_ref[:, : capacity * fields, :].astype(jnp.float32).reshape(slots, fields, 128)
    data = jnp.transpose(data, (1, 0, 2)).astype(jnp.bfloat16)
    for f in range(0, fields, 2):
        picked = dot(hits, jnp.concatenate([data[f], data[f + 1]], axis=1))
        for g in range(2):
            target = picked[:, g * 128 : (g + 1) * 128].astype(jnp.bfloat16)
            target = jnp.concatenate([target[b * rows : (b + 1) * rows] for b in range(per_row)], axis=1)
            target = target.astype(jnp.float32)
            remapped_ref[f + g] = target
            misfit_ref[f + g] = (forecast_ref[f + g] - target) * norm
    by_row = jnp.transpose(misfit_ref[...], (1, 0, 2))
    empty = jnp.zeros((fields, width), jnp.float32)
    for y in range(rows):
        state_ref[:, y * width : (y + 1) * width] = jnp.concatenate([by_row[y], empty], axis=0).astype(jnp.bfloat16)

    col = lax.broadcasted_iota(jnp.int32, (channels, width), 1)
    lane = lax.broadcasted_iota(jnp.int32, (channels, 128), 1)
    ends_left = ends_right = jnp.zeros((channels, 128), jnp.float32)
    batch = 8
    misfits = misfit_ref[...].reshape(depth, width).astype(jnp.bfloat16)
    for first in range(0, rows, batch):
        latents = dot(block_ref[first * channels : (first + batch) * channels, :], misfits)
        for y in range(first, first + batch):
            here = slice(y * channels, (y + 1) * channels)
            act = act_ref[here, :]
            sig = lax.logistic(act)
            silu = act * sig
            hidden_ref[here, :] = silu.astype(jnp.bfloat16)
            latent = latents[(y - first) * channels : (y - first + 1) * channels]
            slope = latent * (sig + silu * (1.0 - sig))
            slope_ref[(y + 1) * channels : (y + 2) * channels, :] = slope.astype(jnp.bfloat16)
            before = jnp.where(col == width - 1, 0.0, pltpu.roll(slope, width - 1, 1))
            before_ref[here, :] = before.astype(jnp.bfloat16)
            after_ref[here, :] = jnp.where(col == 0, 0.0, pltpu.roll(slope, 1, 1)).astype(jnp.bfloat16)
            ends_left += pltpu.roll(jnp.where(lane == 0, slope[:, :128], 0.0), y, 1)
            ends_right += pltpu.roll(jnp.where(lane == 127, slope[:, -128:], 0.0), y + 1, 1)

    total = None
    for first in range(0, rows, batch):
        span = range(first, first + batch)
        features = jnp.concatenate([feat_ref[y * pitch : (y + 3) * pitch, :] for y in span], axis=1)
        features = jnp.concatenate([features, state_ref[:, first * width : (first + batch) * width]], axis=0)
        others = jnp.concatenate(
            [
                jnp.concatenate([ref[(y + d) * channels : (y + d + 1) * channels, :] for y in span], axis=1)
                for ref, d in ((before_ref, 0), (slope_ref, 1), (after_ref, 0), (hidden_ref, 0))
            ],
            axis=0,
        )
        part = dot_nt(features, others)
        total = part if total is None else total + part
    grad_head = total[3 * pitch : 3 * pitch + fields, 3 * channels :]
    stack = stack_ref[...]
    from_left = dot_nt(stack[:, :128], ends_left.astype(jnp.bfloat16))
    from_right = dot_nt(stack[:, 128:], ends_right.astype(jnp.bfloat16))
    middle = jnp.zeros((3 * pitch, channels), jnp.float32)
    total = total[: 3 * pitch, : 3 * channels] + jnp.concatenate([from_left, middle, from_right], axis=1)
    for i in range(3):
        moment_ref[i] = total[i * pitch + channels : i * pitch + channels + fields, :]
    taps = [total[i * pitch : i * pitch + channels, :] for i in range(3)]
    half = channels // 2
    last = [t[:, 2 * channels :] for t in taps]
    packed = [t[:, : 2 * channels] for t in taps]
    packed.append(jnp.concatenate(last[:2], axis=1))
    packed.append(jnp.concatenate([last[2][:half], last[2][half:]], axis=1))
    packed = jnp.concatenate(packed, axis=0)
    cut = packed.shape[0] // 2
    head = jnp.concatenate([grad_head, jnp.zeros_like(grad_head)], axis=1)
    odd = lax.rem(lax.axis_index("lon"), 2)
    packed_ref[odd] = jnp.concatenate([packed[:cut], head], axis=0)
    packed_ref[1 - odd] = jnp.concatenate([packed[cut:], jnp.zeros_like(head)], axis=0)


def backward(arrived, prior, edges, stack, lift, act, forecast, readout, capacity, norm):
    fields, rows, width = forecast.shape
    channels = readout.shape[0]
    pitch = lift.shape[0]
    packed_rows = (3 * channels + channels + channels // 2) // 2 + fields
    vmem = pl.BlockSpec(memory_space=pltpu.VMEM)
    return pl.pallas_call(
        functools.partial(backward_kernel, capacity, channels, norm),
        out_shape=(
            jax.ShapeDtypeStruct((fields, rows, width), jnp.float32),
            jax.ShapeDtypeStruct((2, packed_rows, 2 * channels), jnp.float32),
            jax.ShapeDtypeStruct(((rows + 2) * channels, width), jnp.bfloat16),
            jax.ShapeDtypeStruct((3, fields, 3 * channels), jnp.float32),
        ),
        in_specs=[vmem] * 8,
        out_specs=[vmem] * 4,
        scratch_shapes=[
            pltpu.VMEM(((rows + 2) * pitch, width), jnp.bfloat16),
            pltpu.VMEM((rows * channels, width), jnp.bfloat16),
            pltpu.VMEM((rows * channels, rows * fields), jnp.bfloat16),
            pltpu.VMEM((fields, rows, width), jnp.float32),
            pltpu.VMEM((2 * fields, rows * width), jnp.bfloat16),
            pltpu.VMEM((rows * channels, width), jnp.bfloat16),
            pltpu.VMEM((rows * channels, width), jnp.bfloat16),
        ],
        compiler_params=pltpu.CompilerParams(vmem_limit_bytes=VMEM_LIMIT),
        cost_estimate=pl.CostEstimate(
            flops=2 * rows * width * 3 * channels * 3 * pitch,
            bytes_accessed=rows * width * channels * 8,
            transcendentals=0,
        ),
        name="backward",
    )(arrived, prior, edges, stack, lift, act, forecast, readout)


def lift_gradient_kernel(slope_ref, prior_ref, back_ref, contract_ref, moment_ref, out_ref, delta_ref):
    rows, fields, width = prior_ref.shape
    channels = contract_ref.shape[1]
    col = lax.broadcasted_iota(jnp.int32, (fields, width), 1)
    inside = (col > 0) & (col < width - 1)
    grad_lift = jnp.zeros((fields, channels), jnp.float32)
    for i in range(3):
        rest, pieces = moment_ref[i], []
        for _ in range(3):
            pieces.append(rest.astype(jnp.bfloat16).astype(jnp.float32))
            rest = rest - pieces[-1]
        part = dot_nt(jnp.concatenate(pieces, axis=0).astype(jnp.bfloat16), contract_ref[i])
        grad_lift += part[:fields] + part[fields : 2 * fields] + part[2 * fields :]
    delta_ref[:channels, :] = jnp.zeros((channels, width), jnp.bfloat16)
    delta_ref[(rows - 1) * channels :, :] = jnp.zeros((channels, width), jnp.bfloat16)
    for y in range(1, rows - 1):
        parts = dot(back_ref[...], slope_ref[y * channels : (y + 3) * channels, :])
        grad = (
            parts[channels : 2 * channels]
            + pltpu.roll(parts[:channels], width - 1, 1)
            + pltpu.roll(parts[2 * channels :], 1, 1)
        )
        delta = grad.astype(jnp.bfloat16).astype(jnp.float32) - grad
        delta_ref[y * channels : (y + 1) * channels, :] = delta.astype(jnp.bfloat16)
    crossed = jnp.zeros((channels, fields), jnp.float32)
    batch = 4
    for first in range(0, rows, batch):
        span = range(first, first + batch)
        states = [jnp.where(inside, prior_ref[y].astype(jnp.float32), 0.0).astype(jnp.bfloat16) for y in span]
        states = jnp.concatenate(states, axis=1)
        deltas = jnp.concatenate([delta_ref[y * channels : (y + 1) * channels, :] for y in span], axis=1)
        crossed += dot_nt(deltas, states)
    grad_lift += crossed.T
    out_ref[...] = jnp.zeros_like(out_ref)
    out_ref[-fields:, channels:] = grad_lift


def lift_gradient(slope, prior, back, contract, moment, packed_rows):
    rows, fields, width = prior.shape
    channels = contract.shape[1]
    vmem = pl.BlockSpec(memory_space=pltpu.VMEM)
    return pl.pallas_call(
        lift_gradient_kernel,
        out_shape=jax.ShapeDtypeStruct((packed_rows, 2 * channels), jnp.float32),
        in_specs=[vmem] * 5,
        out_specs=vmem,
        scratch_shapes=[pltpu.VMEM((rows * channels, width), jnp.bfloat16)],
        compiler_params=pltpu.CompilerParams(vmem_limit_bytes=VMEM_LIMIT),
        cost_estimate=pl.CostEstimate(
            flops=2 * rows * width * 9 * channels * channels, bytes_accessed=slope.size * 2, transcendentals=0
        ),
        name="lift_gradient",
    )(slope, prior, back, contract, moment)


def unpack_kernel(channels, mine_ref, other_ref, kernel_ref, lift_ref, head_ref):
    odd = lax.rem(lax.axis_index("lon"), 2) == 1
    fields = lift_ref.shape[0]
    mine, other = mine_ref[-fields:, :], other_ref[-fields:, :]
    lift_ref[...] = (mine + other)[:, channels:]
    head_ref[...] = jnp.where(odd, other, mine)[:, :channels]
    mine, other = mine_ref[:-fields, :], other_ref[:-fields, :]
    packed = jnp.concatenate([jnp.where(odd, other, mine), jnp.where(odd, mine, other)], axis=0)
    half = channels // 2
    for i in range(3):
        block = packed[i * channels : (i + 1) * channels]
        kernel_ref[3 * i] = block[:, :channels]
        kernel_ref[3 * i + 1] = block[:, channels:]
    block = packed[3 * channels : 4 * channels]
    kernel_ref[2] = block[:, :channels]
    kernel_ref[5] = block[:, channels:]
    block = packed[4 * channels : 4 * channels + half]
    kernel_ref[8, :half] = block[:, :channels]
    kernel_ref[8, half:] = block[:, channels:]


def unpack(mine, other, channels, fields):
    return pl.pallas_call(
        functools.partial(unpack_kernel, channels),
        out_shape=(
            jax.ShapeDtypeStruct((9, channels, channels), jnp.float32),
            jax.ShapeDtypeStruct((fields, channels), jnp.float32),
            jax.ShapeDtypeStruct((fields, channels), jnp.float32),
        ),
        compiler_params=pltpu.CompilerParams(vmem_limit_bytes=VMEM_LIMIT),
        name="unpack",
    )(mine, other)


def swap(x, axis, bit):
    return lax.ppermute(x, axis, [(i, i ^ bit) for i in range(lax.axis_size(axis))])


def sum_over(x, axis, low, high):
    if high // low == 4:
        b, a, c = (swap(x, axis, k * low) for k in (2, 1, 3))
        return (x + a) + (b + c)
    bit = low
    while bit < high:
        x = x + swap(x, axis, bit)
        bit *= 2
    return x


def pair_swap(even_sends, odd_sends, axis, periodic):
    count = lax.axis_size(axis)
    even = lax.rem(lax.axis_index(axis), 2) == 0
    inner = [(i, i ^ 1) for i in range(count)]
    outer = []
    for i in range(1, count, 2):
        if i + 1 < count or periodic:
            outer += [(i, (i + 1) % count), ((i + 1) % count, i)]
    got_inner = lax.ppermute(jnp.where(even, odd_sends, even_sends), axis, inner)
    got_outer = lax.ppermute(jnp.where(even, even_sends, odd_sends), axis, outer)
    return jnp.where(even, got_outer, got_inner), jnp.where(even, got_inner, got_outer)


def per_device(
    source,
    intersection_weight,
    dest_tile,
    dest_row,
    prior_state,
    lift_weight,
    kernel,
    readout_weights,
):
    face_count = lax.axis_size("face")
    lon_count = lax.axis_size("lon")
    devices = face_count * lon_count
    src_blocks, intersections = dest_tile.shape
    fields, rows, width = prior_state.shape
    channels = kernel.shape[1]
    capacity = max(2, 2 * src_blocks * intersections // devices)
    norm = 1.0 / math.sqrt(rows * face_count * width * lon_count)

    outgoing = regrid(source, intersection_weight, dest_tile, dest_row, devices, capacity)
    outgoing, prior_state, kernel, lift_weight, readout_weights = lax.optimization_barrier(
        (outgoing, prior_state, kernel, lift_weight, readout_weights)
    )
    arrived = lax.all_to_all(outgoing, ("face", "lon"), split_axis=0, concat_axis=0, tiled=True)
    arrived = arrived.reshape(devices, (capacity + 1) * fields, source.shape[2])

    prior = prior_state.transpose(1, 0, 2)
    top, bottom = pair_swap(prior[0], prior[rows - 1], "face", False)
    columns = [
        jnp.pad(
            jnp.concatenate([top[:, at : at + 1], prior_state[:, :, at], bottom[:, at : at + 1]], axis=1),
            ((0, 0), (0, 128 - rows - 2)),
        )
        for at in (0, width - 1)
    ]
    left, right = pair_swap(columns[0], columns[1], "lon", True)

    edges = jnp.stack([top, bottom])
    sides = jnp.concatenate([left, right], axis=1)
    act, forecast, ends, lift, conv, back, contract, turned = convolve(
        prior, edges, lift_weight, kernel, readout_weights
    )
    own = jnp.concatenate(columns, axis=1)
    act, forecast, stack = finish(act, forecast, ends, own, sides, lift, conv, turned)
    remapped, packed, slope, moment = backward(
        arrived, prior, edges, stack, lift, act, forecast, readout_weights, capacity, norm
    )
    lift_part = lift_gradient(slope, prior, back, contract, moment, packed.shape[1])
    part = packed[0] + swap(packed[1], "lon", 1) + lift_part
    part = sum_over(part, "face", 1, face_count)
    part, remapped, estimate = lax.optimization_barrier(
        (part, remapped.astype(jnp.bfloat16), forecast.astype(jnp.bfloat16))
    )
    part = sum_over(part, "lon", 2, lon_count)
    grad_kernel, grad_lift, grad_head = unpack(part, swap(part, "lon", 1), channels, fields)
    return (
        remapped,
        estimate,
        grad_lift,
        grad_kernel,
        grad_head.T,
    )


def solution(mesh):
    return jax.shard_map(
        per_device,
        mesh=mesh,
        in_specs=(
            P(("face", "lon"), None, None),
            P(("face", "lon"), None, None, None),
            P(("face", "lon"), None),
            P(("face", "lon"), None),
            P(None, "face", "lon"),
            P(),
            P(),
            P(),
        ),
        out_specs=(P(None, "face", "lon"), P(None, "face", "lon"), P(), P(), P()),
        check_vma=False,
    )
```
